32 devices in a mesh: items: 16 (over z, x, core), seq: 2 (over y).
Axes of the slice: x: 2, y: 2, z: 4, core: 2. Of those that a mesh axis runs over, the one named last changes fastest.
Arguments:
- tokens: bfloat16 [64, 2, 128, 768], P('items', 'seq'), may hold values from -6 to 6
- visible: int32 [64, 2, 128], P('items', 'seq'), may hold values from 0 to 587, as said below
- lengths: int32 [64], P('items'), may hold values from 59 to 235, as said below
- first_gain: bfloat16 [768], P(('items', 'seq')), may hold values from 0.5 to 1.5
- first_shift: bfloat16 [768], P(('items', 'seq')), may hold values from -1.5 to 1.5
- input_weight: bfloat16 [768, 2304], P(('items', 'seq')), may hold values from -0.21875 to 0.21875
- query_bias: bfloat16 [768], P(('items', 'seq')), may hold values from -1.5 to 1.5
- value_bias: bfloat16 [768], P(('items', 'seq')), may hold values from -1.5 to 1.5
- output_weight: bfloat16 [768, 768], P(('items', 'seq')), may hold values from -1.75 to 1.75
- output_bias: bfloat16 [768], P(('items', 'seq')), may hold values from -1.5 to 1.5
- second_gain: bfloat16 [768], P(('items', 'seq')), may hold values from 0.5 to 1.5
- second_shift: bfloat16 [768], P(('items', 'seq')), may hold values from -1.5 to 1.5
- expand_weight: bfloat16 [768, 3072], P(('items', 'seq')), may hold values from -0.21875 to 0.21875
- expand_bias: bfloat16 [3072], P(('items', 'seq')), may hold values from -1.5 to 1.5
- reduce_weight: bfloat16 [3072, 768], P(('items', 'seq')), may hold values from -0.109375 to 0.109375
- reduce_bias: bfloat16 [768], P(('items', 'seq')), may hold values from -1.5 to 1.5
- cotangent: bfloat16 [64, 2, 128, 768], P('items', 'seq'), may hold values from -6 to 6
Outputs:
- layer_out: bfloat16 [64, 2, 128, 768], P('items', 'seq')
- tokens_grad: float32 [64, 2, 128, 768], P('items', 'seq')
- first_gain_grad: float32 [768], P(('items', 'seq'))
- first_shift_grad: float32 [768], P(('items', 'seq'))
- input_weight_grad: float32 [768, 2304], P(('items', 'seq'))
- query_bias_grad: float32 [768], P(('items', 'seq'))
- value_bias_grad: float32 [768], P(('items', 'seq'))
- output_weight_grad: float32 [768, 768], P(('items', 'seq'))
- output_bias_grad: float32 [768], P(('items', 'seq'))
- second_gain_grad: float32 [768], P(('items', 'seq'))
- second_shift_grad: float32 [768], P(('items', 'seq'))
- expand_weight_grad: float32 [768, 3072], P(('items', 'seq'))
- expand_bias_grad: float32 [3072], P(('items', 'seq'))
- reduce_weight_grad: float32 [3072, 768], P(('items', 'seq'))
- reduce_bias_grad: float32 [768], P(('items', 'seq'))
The draws below stay inside these ranges and needn't reach their ends.
Inputs may be any that keep to these rules, and one draw needn't show every extreme that they name: `lengths`: the count of visible tokens of each item; some item has exactly 235, another exactly 59. For an item with n visible tokens: its distinct visible patch numbers in ascending order, the first (n + 1) // 2 in block 0 and the other n // 2 in block 1, from slot 0 on; the remaining slots hold 0.
All inputs are finite; a program needn't handle non-finite values.
Results may differ from the reference program's by a relative error of at most 0.0099.
Values may be sent and summed in bfloat16 or wider, within the bound.
A program may use at most 192 MiB of HBM per device.

```python
import math
import jax
import jax.numpy as jnp
from jax import lax

D = 768
FF = 3072
HD = 64
GRID = 14
PATCHES = 588
BLK = 128
VIS_MIN = 59
VIS_MAX = 235
ITEMS = 64


def visible_pattern(key):
    counts = jax.random.randint(jax.random.fold_in(key, 11), (ITEMS,), VIS_MIN, VIS_MAX + 1)
    largest = jax.random.randint(jax.random.fold_in(key, 12), (), 0, ITEMS)
    smallest = (largest + 1 + jax.random.randint(jax.random.fold_in(key, 13), (), 0, ITEMS - 1)) % ITEMS
    item_number = jnp.arange(ITEMS)
    counts = jnp.where(item_number == largest, VIS_MAX, jnp.where(item_number == smallest, VIS_MIN, counts))
    patch_number = jnp.arange(PATCHES)[None, :]
    scores = jax.random.randint(jax.random.fold_in(key, 14), (ITEMS, PATCHES), 0, 2 ** 20) * 1024 + patch_number
    ranking = jnp.argsort(jnp.argsort(scores, axis=1), axis=1)
    chosen = ranking < counts[:, None]
    listed = jnp.argsort(jnp.where(chosen, 0, PATCHES) + patch_number, axis=1)
    first_count = (counts + 1) // 2
    slot_number = jnp.arange(BLK)[None, :]
    first_block = jnp.where(slot_number < first_count[:, None], listed[:, :BLK], 0)
    second_index = jnp.take_along_axis(listed, first_count[:, None] + slot_number, axis=1)
    second_block = jnp.where(slot_number < (counts - first_count)[:, None], second_index, 0)
    return (counts.astype(jnp.int32), jnp.stack([first_block, second_block], axis=1).astype(jnp.int32))


def draw_lengths(key, part):
    counts, listing = visible_pattern(key)
    return counts


def draw_visible(key, part):
    counts, listing = visible_pattern(key)
    return listing


def level_of(key, dims, split, low, high):
    factor_of, own = 1.0, jax.random.fold_in(key, 6)
    for position, shards_of in split:
        steps = jnp.exp(jax.random.uniform(jax.random.fold_in(own, position), (shards_of,), jnp.float32, low / len(split), high / len(split)))
        factor_of = factor_of * jnp.repeat(steps, dims[position] // shards_of).reshape([-1 if axis == position else 1 for axis in range(len(dims))])
    return factor_of


def normal_values(own_key, extent, scale, bound, split=(), held_as=jnp.bfloat16):
    entries = jax.random.normal(own_key, extent, jnp.float32) * scale
    if len(split) > 0:
        entries = level_of(own_key, extent, split, -0.22, 0.18) * entries
    return jnp.clip(entries, min=-bound, max=bound).astype(held_as)


def setup_inputs(seed: int = 0) -> dict:
    arg_keys = jax.random.split(jax.random.key(seed), 18)
    return {
        "tokens": normal_values(arg_keys[0], (ITEMS, 2, BLK, D), 1.0, 6.0, ((0, 16), (1, 2))),
        "visible": draw_visible(jax.random.fold_in(arg_keys[17], 71), 0),
        "lengths": draw_lengths(jax.random.fold_in(arg_keys[17], 71), 0),
        "first_gain": jnp.clip(1.0 + 0.1 * jax.random.normal(arg_keys[3], (D,), jnp.float32), 0.5, 1.5).astype(jnp.bfloat16),
        "first_shift": normal_values(arg_keys[4], (D,), 0.3, 1.5, ((0, 32),)),
        "input_weight": normal_values(arg_keys[5], (D, 3 * D), D ** -0.5, 0.21875, ((0, 32),)),
        "query_bias": normal_values(arg_keys[6], (D,), 0.3, 1.5, ((0, 32),)),
        "value_bias": normal_values(arg_keys[7], (D,), 0.3, 1.5, ((0, 32),)),
        "output_weight": normal_values(arg_keys[8], (D, D), (D // 64) ** -0.5, 1.75, ((0, 32),)),
        "output_bias": normal_values(arg_keys[9], (D,), 0.3, 1.5, ((0, 32),)),
        "second_gain": jnp.clip(1.0 + 0.1 * jax.random.normal(arg_keys[10], (D,), jnp.float32), 0.5, 1.5).astype(jnp.bfloat16),
        "second_shift": normal_values(arg_keys[11], (D,), 0.3, 1.5, ((0, 32),)),
        "expand_weight": normal_values(arg_keys[12], (D, FF), D ** -0.5, 0.21875, ((0, 32),)),
        "expand_bias": normal_values(arg_keys[13], (FF,), 0.3, 1.5, ((0, 32),)),
        "reduce_weight": normal_values(arg_keys[14], (FF, D), FF ** -0.5, 0.109375, ((0, 32),)),
        "reduce_bias": normal_values(arg_keys[15], (D,), 0.3, 1.5, ((0, 32),)),
        "cotangent": normal_values(arg_keys[16], (ITEMS, 2, BLK, D), 1.0, 6.0, ((0, 16), (1, 2))),
    }


@jax.custom_vjp
def low(v):
    return lax.optimization_barrier(v.astype(jnp.bfloat16)).astype(jnp.float32)

@jax.custom_vjp
def low_back(v):
    return v

def low_keep(v):
    return (low(v), None)

def low_pass(kept, grad):
    return (grad,)

def back_keep(v):
    return (v, None)

def back_low(kept, grad):
    return (low(grad),)
low.defvjp(low_keep, low_pass)
low_back.defvjp(back_keep, back_low)
EPSILON = 1e-06
SCORE_SCALE = 0.125
HIGHEST_PRECISION = lax.Precision.HIGHEST

def layer_norm(rows_in, gain, shift):
    centre = rows_in - lax.optimization_barrier(jnp.mean(rows_in, axis=-1, keepdims=True))
    spread = lax.optimization_barrier(jnp.mean(centre * centre, axis=-1, keepdims=True))
    return centre * lax.rsqrt(spread + EPSILON) * gain + shift

def positions(index, model_width):
    channel = jnp.arange(model_width)
    portion = 3 * channel // model_width
    frequency = jnp.power(10000.0, -(channel % 256 // 2).astype(jnp.float32) / 128.0)
    which_frame = index // (GRID * GRID)
    which_row = index % (GRID * GRID) // GRID
    which_column = index % GRID
    coordinate = jnp.where(portion == 0, which_frame[..., None], jnp.where(portion == 1, which_row[..., None], which_column[..., None]))
    angle = coordinate.astype(jnp.float32) * frequency
    return jnp.where(channel % 2 == 0, jnp.sin(angle), jnp.cos(angle))

def matmul(left, right):
    return jnp.dot(left, right, precision=HIGHEST_PRECISION)

def forward(tokens_in, position_rows, live_rows, params):
    first_gain, first_shift, input_weight, query_bias, value_bias, output_weight, output_bias, second_gain, second_shift, expand_weight, expand_bias, reduce_weight, reduce_bias = params
    group_size, seq_rows, model_width = tokens_in.shape
    head_count = model_width // HD
    entry = tokens_in + position_rows
    normed = low(layer_norm(entry, first_gain, first_shift))
    joined_bias = jnp.concatenate([query_bias, jnp.zeros_like(query_bias), value_bias])
    projected = low_back(low(matmul(normed, input_weight) + joined_bias))
    queries = projected[..., :model_width].reshape(group_size, seq_rows, head_count, HD)
    keys_all = projected[..., model_width:2 * model_width].reshape(group_size, seq_rows, head_count, HD)
    values_all = projected[..., 2 * model_width:].reshape(group_size, seq_rows, head_count, HD)
    scores = jnp.einsum('gqhd,gkhd->ghqk', queries, keys_all, precision=HIGHEST_PRECISION) * SCORE_SCALE
    scores = low_back(scores)
    scores = jnp.where(live_rows[:, None, None, :], scores, -1e+30)
    row_max = lax.optimization_barrier(jnp.max(scores, axis=-1, keepdims=True))
    exponent = jnp.exp(scores - row_max)
    attention = low(exponent / lax.optimization_barrier(jnp.sum(exponent, axis=-1, keepdims=True)))
    attended = jnp.einsum('ghqk,gkhd->gqhd', attention, values_all, precision=HIGHEST_PRECISION)
    attended = low_back(low(attended.reshape(group_size, seq_rows, model_width)))
    middle = entry + low_back(matmul(attended, output_weight) + output_bias)
    second = low(layer_norm(middle, second_gain, second_shift))
    expanded = low_back(matmul(second, expand_weight) + expand_bias)
    activated = low(jax.nn.gelu(expanded, approximate=False))
    result = middle + matmul(activated, reduce_weight) + reduce_bias
    return jnp.where(live_rows[..., None], result, 0.0)

def reference(tokens, visible, lengths, first_gain, first_shift, input_weight, query_bias, value_bias, output_weight, output_bias, second_gain, second_shift, expand_weight, expand_bias, reduce_weight, reduce_bias, cotangent):
    params = tuple((vector.astype(jnp.float32) for vector in (first_gain, first_shift, input_weight, query_bias, value_bias, output_weight, output_bias, second_gain, second_shift, expand_weight, expand_bias, reduce_weight, reduce_bias)))
    seq_rows = 2 * BLK
    group_size = math.gcd(ITEMS, max(1, 4096 // seq_rows))
    groups = ITEMS // group_size
    tokens_all = tokens.astype(jnp.float32).reshape(groups, group_size, seq_rows, D)
    visible_all = visible.reshape(groups, group_size, seq_rows)
    lengths_all = lengths.reshape(groups, group_size)
    cotangent_all = cotangent.astype(jnp.float32).reshape(groups, group_size, seq_rows, D)

    def one_group(carry, pieces):
        tokens_in, index_rows, length_rows, cotangent_rows = pieces
        row_number = jnp.arange(seq_rows)
        half_number = row_number // BLK
        within = row_number % BLK
        live_rows = within[None, :] < (length_rows[:, None] + 1 - half_number[None, :]) // 2
        position_rows = positions(index_rows, D)

        def apply_layer(rows_in, weights_in):
            return forward(rows_in, position_rows, live_rows, weights_in)
        result, pull_back = jax.vjp(apply_layer, tokens_in, params)
        input_grad, param_grads = pull_back(cotangent_rows)
        carry = tuple((total + grad for total, grad in zip(carry, param_grads)))
        return (carry, (result.astype(jnp.bfloat16), input_grad))
    zeros_start = tuple((jnp.zeros_like(vector) for vector in params))
    totals, (results, input_grads) = lax.scan(one_group, zeros_start, (tokens_all, visible_all, lengths_all, cotangent_all))
    layer_out = results.reshape(ITEMS, 2, BLK, D)
    tokens_grad = input_grads.reshape(ITEMS, 2, BLK, D)
    return (layer_out, tokens_grad, totals[0], totals[1], totals[2], totals[3], totals[4], totals[5], totals[6], totals[7], totals[8], totals[9], totals[10], totals[11], totals[12])
```

```python
import functools

import jax
import jax.numpy as jnp
import numpy as np
from jax import lax
from jax.experimental import pallas as pl
from jax.experimental.pallas import tpu as pltpu
from jax.sharding import PartitionSpec as P

HD = 64
GRID = 14
MICRO = 2
ITEMS_MB = 2


EPSILON = 1e-06
SCORE_SCALE = 0.125


def layer_norm(rows_in, gain, shift):
    centre = rows_in - jnp.mean(rows_in, axis=-1, keepdims=True)
    spread = jnp.mean(centre * centre, axis=-1, keepdims=True)
    return centre * lax.rsqrt(spread + EPSILON) * gain + shift


def gelu_exact(value_in):
    return jax.nn.gelu(value_in, approximate=False)


def positions(index, model_width):
    channel = jnp.arange(model_width)
    portion = 3 * channel // model_width
    frequency = jnp.power(10000.0, -(channel % 256 // 2).astype(jnp.float32) / 128.0)
    which_frame = index // (GRID * GRID)
    which_row = index % (GRID * GRID) // GRID
    which_column = index % GRID
    coordinate = jnp.where(
        portion == 0,
        which_frame[..., None],
        jnp.where(portion == 1, which_row[..., None], which_column[..., None]),
    )
    angle = coordinate.astype(jnp.float32) * frequency
    return jnp.where(channel % 2 == 0, jnp.sin(angle), jnp.cos(angle))


def contract_rows(left, right):
    return lax.dot_general(
        left, right, (((0,), (0,)), ((), ())), preferred_element_type=jnp.float32
    )


def against(left, right):
    return lax.dot_general(
        left, right, (((1,), (1,)), ((), ())), preferred_element_type=jnp.float32
    )


def row_masks(lengths, block_rows, block_number):
    counts = (lengths + 1 - block_number) // 2
    return jnp.arange(block_rows)[None, :] < counts[:, None]


def micro_batch(gathered, tokens, visible, lengths, cotangent, seq_place):
    (
        first_gain,
        first_shift,
        input_weight,
        query_bias,
        value_bias,
        output_weight,
        output_bias,
        second_gain,
        second_shift,
        expand_weight,
        expand_bias,
        reduce_weight,
        reduce_bias,
    ) = gathered
    item_count, block_rows, model_width = tokens.shape
    head_count = model_width // HD
    total_rows = item_count * block_rows
    (
        first_gain,
        first_shift,
        query_bias,
        value_bias,
        output_bias,
        second_gain,
        second_shift,
        expand_bias,
        reduce_bias,
    ) = (
        vector.astype(jnp.float32)
        for vector in (
            first_gain,
            first_shift,
            query_bias,
            value_bias,
            output_bias,
            second_gain,
            second_shift,
            expand_bias,
            reduce_bias,
        )
    )
    query_live = row_masks(lengths, block_rows, seq_place).reshape(total_rows, 1)
    key_live = jnp.concatenate(
        [row_masks(lengths, block_rows, 0), row_masks(lengths, block_rows, 1)], axis=1
    )
    key_mask = key_live[:, None, None, :]
    entry = tokens.reshape(total_rows, model_width).astype(jnp.float32) + positions(
        visible.reshape(total_rows), model_width
    )
    normed, first_pull = jax.vjp(layer_norm, entry, first_gain, first_shift)
    normed_low = normed.astype(jnp.bfloat16)
    joined_bias = jnp.concatenate([query_bias, jnp.zeros_like(query_bias), value_bias])
    projected = (
        jnp.dot(normed_low, input_weight, preferred_element_type=jnp.float32) + joined_bias
    ).astype(jnp.bfloat16)
    queries = projected[:, :model_width].reshape(item_count, block_rows, head_count, HD)
    keys_here = projected[:, model_width : 2 * model_width].reshape(
        item_count, block_rows, model_width
    )
    values_here = projected[:, 2 * model_width :].reshape(item_count, block_rows, model_width)
    keys_all, values_all = (
        lax.all_gather(keys_here, "seq", axis=1, tiled=True),
        lax.all_gather(values_here, "seq", axis=1, tiled=True),
    )
    keys_all = keys_all.reshape(item_count, 2 * block_rows, head_count, HD)
    values_all = values_all.reshape(item_count, 2 * block_rows, head_count, HD)
    scores = (
        jnp.einsum("cqhd,ckhd->chqk", queries, keys_all, preferred_element_type=jnp.float32)
        * SCORE_SCALE
    )
    scores = jnp.where(key_mask, scores, -1e30)
    row_max = jnp.max(scores, axis=-1, keepdims=True)
    exponent = jnp.exp(scores - row_max)
    row_total = jnp.sum(exponent, axis=-1, keepdims=True)
    attention_low = (exponent / row_total).astype(jnp.bfloat16)
    log_total = row_max + jnp.log(row_total)
    attended = jnp.einsum(
        "chqk,ckhd->cqhd", attention_low, values_all, preferred_element_type=jnp.float32
    )
    attended = attended.reshape(total_rows, model_width).astype(jnp.bfloat16)
    middle = (
        entry + jnp.dot(attended, output_weight, preferred_element_type=jnp.float32) + output_bias
    )
    second, second_pull = jax.vjp(layer_norm, middle, second_gain, second_shift)
    second_low = second.astype(jnp.bfloat16)
    expanded = jnp.dot(second_low, expand_weight, preferred_element_type=jnp.float32) + expand_bias
    activated, gelu_pull = jax.vjp(gelu_exact, expanded)
    activated_low = activated.astype(jnp.bfloat16)
    result = (
        middle
        + jnp.dot(activated_low, reduce_weight, preferred_element_type=jnp.float32)
        + reduce_bias
    )
    layer_out = jnp.where(query_live, result, 0.0).astype(jnp.bfloat16)
    incoming = jnp.where(
        query_live, cotangent.reshape(total_rows, model_width).astype(jnp.float32), 0.0
    )
    incoming_low = incoming.astype(jnp.bfloat16)
    reduce_weight_grad = contract_rows(activated_low, incoming_low)
    reduce_bias_grad = jnp.sum(incoming, axis=0)
    activated_grad = against(incoming_low, reduce_weight)
    expanded_grad = gelu_pull(activated_grad)[0].astype(jnp.bfloat16)
    expand_weight_grad = contract_rows(second_low, expanded_grad)
    expand_bias_grad = jnp.sum(expanded_grad.astype(jnp.float32), axis=0)
    second_grad = against(expanded_grad, expand_weight)
    middle_part, second_gain_grad, second_shift_grad = second_pull(second_grad)
    middle_grad = incoming + middle_part
    branch_grad = middle_grad.astype(jnp.bfloat16)
    output_weight_grad = contract_rows(attended, branch_grad)
    output_bias_grad = jnp.sum(branch_grad.astype(jnp.float32), axis=0)
    attended_grad = against(branch_grad, output_weight).astype(jnp.bfloat16)
    attended_grad = attended_grad.reshape(item_count, block_rows, head_count, HD)
    scores = (
        jnp.einsum("cqhd,ckhd->chqk", queries, keys_all, preferred_element_type=jnp.float32)
        * SCORE_SCALE
    )
    scores = jnp.where(key_mask, scores, -1e30)
    attention_full = jnp.exp(scores - log_total)
    attention_low = attention_full.astype(jnp.bfloat16)
    weight_grad = jnp.einsum(
        "cqhd,ckhd->chqk", attended_grad, values_all, preferred_element_type=jnp.float32
    )
    row_inner = jnp.sum(attention_full * weight_grad, axis=-1, keepdims=True)
    scores_grad = (attention_full * (weight_grad - row_inner)).astype(jnp.bfloat16)
    query_grad = (
        jnp.einsum("chqk,ckhd->cqhd", scores_grad, keys_all, preferred_element_type=jnp.float32)
        * SCORE_SCALE
    )
    key_terms = (
        jnp.einsum("chqk,cqhd->ckhd", scores_grad, queries, preferred_element_type=jnp.float32)
        * SCORE_SCALE
    )
    value_terms = jnp.einsum(
        "chqk,cqhd->ckhd", attention_low, attended_grad, preferred_element_type=jnp.float32
    )
    key_grad, value_grad = (
        lax.psum_scatter(
            key_terms.reshape(item_count, 2 * block_rows, model_width).astype(jnp.bfloat16),
            "seq",
            scatter_dimension=1,
            tiled=True,
        ).astype(jnp.float32),
        lax.psum_scatter(
            value_terms.reshape(item_count, 2 * block_rows, model_width).astype(jnp.bfloat16),
            "seq",
            scatter_dimension=1,
            tiled=True,
        ).astype(jnp.float32),
    )
    projected_grad = jnp.concatenate(
        [
            query_grad.reshape(total_rows, model_width),
            key_grad.reshape(total_rows, model_width),
            value_grad.reshape(total_rows, model_width),
        ],
        axis=1,
    ).astype(jnp.bfloat16)
    input_weight_grad = contract_rows(normed_low, projected_grad)
    projected_sums = jnp.sum(projected_grad.astype(jnp.float32), axis=0)
    query_bias_grad = projected_sums[:model_width]
    value_bias_grad = projected_sums[2 * model_width :]
    normed_grad = against(projected_grad, input_weight)
    entry_part, first_gain_grad, first_shift_grad = first_pull(normed_grad)
    tokens_grad = middle_grad + entry_part
    grads = (
        first_gain_grad,
        first_shift_grad,
        input_weight_grad,
        query_bias_grad,
        value_bias_grad,
        output_weight_grad,
        output_bias_grad,
        second_gain_grad,
        second_shift_grad,
        expand_weight_grad,
        expand_bias_grad,
        reduce_weight_grad,
        reduce_bias_grad,
    )
    return (layer_out, tokens_grad, grads)


def general_body(
    tokens,
    visible,
    lengths,
    first_gain,
    first_shift,
    input_weight,
    query_bias,
    value_bias,
    output_weight,
    output_bias,
    second_gain,
    second_shift,
    expand_weight,
    expand_bias,
    reduce_weight,
    reduce_bias,
    cotangent,
):
    shards = (
        first_gain,
        first_shift,
        input_weight,
        query_bias,
        value_bias,
        output_weight,
        output_bias,
        second_gain,
        second_shift,
        expand_weight,
        expand_bias,
        reduce_weight,
        reduce_bias,
    )
    seq_place = lax.axis_index("seq")
    block_rows = tokens.shape[2]
    model_width = tokens.shape[3]
    outputs_list = []
    gradients_list = []
    totals = None
    for micro_index in range(MICRO):
        first_item = micro_index * ITEMS_MB
        last_item = first_item + ITEMS_MB
        gathered = (
            lax.all_gather(shards[0], ("items", "seq"), axis=0, tiled=True),
            lax.all_gather(shards[1], ("items", "seq"), axis=0, tiled=True),
            lax.all_gather(shards[2], ("items", "seq"), axis=0, tiled=True),
            lax.all_gather(shards[3], ("items", "seq"), axis=0, tiled=True),
            lax.all_gather(shards[4], ("items", "seq"), axis=0, tiled=True),
            lax.all_gather(shards[5], ("items", "seq"), axis=0, tiled=True),
            lax.all_gather(shards[6], ("items", "seq"), axis=0, tiled=True),
            lax.all_gather(shards[7], ("items", "seq"), axis=0, tiled=True),
            lax.all_gather(shards[8], ("items", "seq"), axis=0, tiled=True),
            lax.all_gather(shards[9], ("items", "seq"), axis=0, tiled=True),
            lax.all_gather(shards[10], ("items", "seq"), axis=0, tiled=True),
            lax.all_gather(shards[11], ("items", "seq"), axis=0, tiled=True),
            lax.all_gather(shards[12], ("items", "seq"), axis=0, tiled=True),
        )
        layer_out, tokens_grad, grads = micro_batch(
            gathered,
            tokens[first_item:last_item, 0],
            visible[first_item:last_item, 0],
            lengths[first_item:last_item],
            cotangent[first_item:last_item, 0],
            seq_place,
        )
        outputs_list.append(layer_out)
        gradients_list.append(tokens_grad)
        shares = (
            lax.psum_scatter(grads[0], ("items", "seq"), scatter_dimension=0, tiled=True),
            lax.psum_scatter(grads[1], ("items", "seq"), scatter_dimension=0, tiled=True),
            lax.psum_scatter(grads[2], ("items", "seq"), scatter_dimension=0, tiled=True),
            lax.psum_scatter(grads[3], ("items", "seq"), scatter_dimension=0, tiled=True),
            lax.psum_scatter(grads[4], ("items", "seq"), scatter_dimension=0, tiled=True),
            lax.psum_scatter(grads[5], ("items", "seq"), scatter_dimension=0, tiled=True),
            lax.psum_scatter(grads[6], ("items", "seq"), scatter_dimension=0, tiled=True),
            lax.psum_scatter(grads[7], ("items", "seq"), scatter_dimension=0, tiled=True),
            lax.psum_scatter(grads[8], ("items", "seq"), scatter_dimension=0, tiled=True),
            lax.psum_scatter(grads[9], ("items", "seq"), scatter_dimension=0, tiled=True),
            lax.psum_scatter(grads[10], ("items", "seq"), scatter_dimension=0, tiled=True),
            lax.psum_scatter(grads[11], ("items", "seq"), scatter_dimension=0, tiled=True),
            lax.psum_scatter(grads[12], ("items", "seq"), scatter_dimension=0, tiled=True),
        )
        totals = (
            shares
            if totals is None
            else tuple((earlier + later for earlier, later in zip(totals, shares)))
        )
    item_count = tokens.shape[0]
    layer_out = jnp.concatenate(outputs_list, axis=0).reshape(
        item_count, 1, block_rows, model_width
    )
    tokens_grad = jnp.concatenate(gradients_list, axis=0).reshape(
        item_count, 1, block_rows, model_width
    )
    return (
        layer_out,
        tokens_grad,
        totals[0],
        totals[1],
        totals[2],
        totals[3],
        totals[4],
        totals[5],
        totals[6],
        totals[7],
        totals[8],
        totals[9],
        totals[10],
        totals[11],
        totals[12],
    )


Z_SIZE = 4
F32 = jnp.float32
BF16 = jnp.bfloat16
MESH = pl.DeviceIdType.MESH
RELAY_X = 3
CHUNK = 24
W_I, W_O, W_E, W_R, VEC = TENSORS = range(5)
AG_SEMS = 19
RS_SEMS = 13
VECTORS = 8


def nn(left, right):
    return lax.dot_general(left, right, (((1,), (0,)), ((), ())), preferred_element_type=F32)


def nt(left, right):
    return lax.dot_general(left, right, (((1,), (1,)), ((), ())), preferred_element_type=F32)


def tn(left, right):
    return lax.dot_general(left, right, (((0,), (0,)), ((), ())), preferred_element_type=F32)


def lanes(start, size):
    return pl.ds(pl.multiple_of(start, 128), size)


def rows_at(start, size):
    return pl.ds(pl.multiple_of(start, 128), size)


class Place:
    def __init__(self):
        item = lax.axis_index("items")
        self.y = lax.axis_index("seq")
        self.z = item // 4
        self.x = (item // 2) % 2
        self.c = item % 2

    def device(self, z, x, c, y):
        return ((z * 2 + x) * 2 + c, y)

    def to_z(self, k):
        return self.device(lax.rem(self.z + k, Z_SIZE), self.x, self.c, self.y)

    @property
    def to_x(self):
        return self.device(self.z, 1 - self.x, self.c, self.y)

    @property
    def to_y(self):
        return self.device(self.z, self.x, self.c, 1 - self.y)

    @property
    def to_c(self):
        return self.device(self.z, self.x, 1 - self.c, self.y)

    def column(self, flip_x, flip_c, flip_y):
        x = 1 - self.x if flip_x else self.x
        c = 1 - self.c if flip_c else self.c
        y = 1 - self.y if flip_y else self.y
        return x * 4 + c * 2 + y

    def quarter(self, flip_x, flip_y):
        x = 1 - self.x if flip_x else self.x
        y = 1 - self.y if flip_y else self.y
        return x * 2 + y


def remote(src, dst, send, recv, device):
    return pltpu.make_async_remote_copy(
        src_ref=src, dst_ref=dst, send_sem=send, recv_sem=recv, device_id=device, device_id_type=MESH
    )


class Gather:
    def __init__(self, here, buf, send, recv):
        self.here, self.buf, self.send, self.recv = here, buf, send, recv
        self.open = []

    def copy(self, slot, index, device):
        ref = self.buf.at[slot]
        return remote(ref, ref, self.send.at[index], self.recv.at[index], device)

    def push(self, slot, index, device):
        made = self.copy(slot, index, device)
        made.start()
        self.open.append(made)

    def pull(self, slot, index):
        self.copy(slot, index, self.here.to_x).wait_recv()

    def behind(self, k):
        return lax.rem(self.here.z + (Z_SIZE - k), Z_SIZE)

    def begin(self):
        here = self.here
        own = (here.z, here.column(0, 0, 0))
        for k in (1, 3, 2):
            self.push(own, k - 1, here.to_z(k))
        self.push(own, 3, here.to_x)
        self.push(own, 7, here.to_y)

    def pass_on(self, k):
        here = self.here
        slot = (self.behind(k), here.column(0, 0, 0))
        self.pull(slot, k - 1)
        self.push(slot, 3 + k, here.to_x)
        self.push(slot, 7 + k, here.to_y)

    def own_to_core(self):
        here = self.here
        self.push((slice(None), here.column(0, 0, 0)), 15, here.to_c)

    def relay(self, k):
        here = self.here
        from_x = (self.behind(k), here.column(1, 0, 0))
        from_y = (self.behind(k), here.column(0, 0, 1))
        self.pull(from_x, 3 + k)
        self.pull(from_y, 7 + k)
        if k < RELAY_X:
            self.push(from_y, 11 + k, here.to_x)
        else:
            self.push(from_x, 11 + k, here.to_y)

    def sides_to_core(self):
        here = self.here
        self.push((slice(None), here.column(1, 0, 0)), 16, here.to_c)
        self.push((slice(None), here.column(0, 0, 1)), 17, here.to_c)

    def corner(self):
        here = self.here
        for k in range(4):
            self.pull((self.behind(k), here.column(1, 0, 1)), 11 + k)
        self.push((slice(None), here.column(1, 0, 1)), 18, here.to_c)

    def from_core(self):
        here = self.here
        for index, (fx, fy) in ((15, (0, 0)), (16, (1, 0)), (17, (0, 1)), (18, (1, 1))):
            self.pull((slice(None), here.column(fx, 1, fy)), index)

    def drain(self):
        for made in self.open:
            made.wait_send()
        self.open = []


QUARTERS = ((1, 1), (1, 0), (0, 1), (0, 0))


class Reduce:
    def __init__(self, here, part, core, relay, sides, ends, send, recv):
        self.here, self.part, self.core, self.sides_in, self.ends = here, part, core, sides, ends
        self.relay_in = relay
        self.send, self.recv = send, recv
        self.open = []

    def push(self, src, dst, index, device):
        made = remote(src, dst, self.send.at[index], self.recv.at[index], device)
        made.start()
        self.open.append(made)

    def pull(self, dst, index):
        remote(dst, dst, self.send.at[index], self.recv.at[index], self.here.to_x).wait_recv()

    def add(self, column, first, last, *others):
        part = self.part

        def one(z, carry):
            total = part[z, column].astype(F32)
            for ref, index in others:
                total = total + ref[z, index].astype(F32)
            part[z, column] = total.astype(part.dtype)
            return carry

        lax.fori_loop(first, last, one, 0)

    def core_send(self, spare=None):
        here = self.here
        if spare is not None:
            pl.semaphore_wait(spare, 1)
        for index, (fx, fy) in enumerate(QUARTERS):
            self.push(
                self.part.at[:, here.column(fx, 1, fy)],
                self.core.at[:, here.quarter(fx, fy)],
                index,
                here.to_c,
            )

    def core_add(self):
        here = self.here
        for index, (fx, fy) in enumerate(QUARTERS):
            quarter = here.quarter(fx, fy)
            self.pull(self.core.at[:, quarter], index)
            self.add(here.column(fx, 0, fy), 0, 4, (self.core, quarter))
            if index == 0:
                corner = here.column(1, 0, 1)
                src, dst = self.part, self.relay_in
                self.push(src.at[:RELAY_X, corner], dst.at[:RELAY_X], 4, here.to_x)
                self.push(src.at[RELAY_X:, corner], dst.at[RELAY_X:], 5, here.to_y)
            if index == 1:
                column = here.column(1, 0, 0)
                dst = self.sides_in.at[:RELAY_X, 0]
                self.push(self.part.at[:RELAY_X, column], dst, 6, here.to_x)
            if index == 2:
                column = here.column(0, 0, 1)
                dst = self.sides_in.at[RELAY_X:, 1]
                self.push(self.part.at[RELAY_X:, column], dst, 8, here.to_y)

    def relay(self):
        here, part = self.here, self.part
        to_x, to_y = here.column(1, 0, 0), here.column(0, 0, 1)

        def pair(z, column):
            total = part[z, column].astype(F32) + self.relay_in[z].astype(F32)
            part[z, column] = total.astype(part.dtype)

        self.pull(self.relay_in.at[RELAY_X:], 5)
        for z in range(RELAY_X, 4):
            pair(z, to_x)
        self.push(part.at[RELAY_X:, to_x], self.sides_in.at[RELAY_X:, 0], 7, here.to_x)
        self.pull(self.relay_in.at[:RELAY_X], 4)

        def one(z, carry):
            pair(z, to_y)
            return carry

        lax.fori_loop(0, RELAY_X, one, 0)
        self.push(part.at[:RELAY_X, to_y], self.sides_in.at[:RELAY_X, 1], 9, here.to_y)

    def sides(self):
        here = self.here
        for index, where in ((6, (slice(0, RELAY_X), 0)), (8, (slice(RELAY_X, 4), 1)),
                             (7, (slice(RELAY_X, 4), 0)), (9, (slice(0, RELAY_X), 1))):
            self.pull(self.sides_in.at[where], index)
        own = here.column(0, 0, 0)
        self.add(own, 0, 4, (self.sides_in, 0), (self.sides_in, 1))
        for k in (1, 3, 2):
            away = lax.rem(here.z + k, Z_SIZE)
            self.push(self.part.at[away, own], self.ends.at[k - 1], 9 + k, here.to_z(k))

    def finish(self):
        here = self.here
        for k in (1, 3, 2):
            self.pull(self.ends.at[k - 1], 9 + k)
        total = self.part[here.z, here.column(0, 0, 0)].astype(F32)
        for k in range(3):
            total = total + self.ends[k].astype(F32)
        return total

    def drain(self):
        for made in self.open:
            made.wait_send()
        self.open = []


def normalise(rows_in):
    centre = rows_in - jnp.mean(rows_in, axis=-1, keepdims=True)
    spread = jnp.mean(centre * centre, axis=-1, keepdims=True)
    inverse = lax.rsqrt(spread + EPSILON)
    return centre * inverse, inverse


def normalise_back(grad, unit, inverse):
    return inverse * (
        grad
        - jnp.mean(grad, axis=-1, keepdims=True)
        - unit * jnp.mean(grad * unit, axis=-1, keepdims=True)
    )


def spread_matrix(slot):
    lane = lax.broadcasted_iota(jnp.int32, (128, 768), 0)
    place = lax.broadcasted_iota(jnp.int32, (128, 768), 1)
    if slot is None:
        inside = lax.rem(place, 4 * CHUNK)
        wanted = 32 * (inside // CHUNK) + lax.rem(inside, CHUNK)
    else:
        wanted = 32 * slot + lax.rem(place, CHUNK)
    return jnp.where(lane == wanted, 1.0, 0.0).astype(BF16)


def owner_mask(each, first):
    device = lax.broadcasted_iota(jnp.int32, (32, 768), 0)
    place = lax.broadcasted_iota(jnp.int32, (32, 768), 1)
    return device == first + place // each


def collect(group, matrix, each, first):
    moved = nn(group.astype(BF16), matrix)
    return jnp.sum(jnp.where(owner_mask(each, first), moved, 0.0), axis=0, keepdims=True)


def deal(row, matrix, each, first):
    placed = jnp.where(owner_mask(each, first), row, 0.0)
    high = placed.astype(BF16)
    rest = placed - high.astype(F32)
    middle = rest.astype(BF16)
    low = (rest - middle.astype(F32)).astype(BF16)
    return nt(high, matrix) + nt(middle, matrix) + nt(low, matrix)


def one_hot(value):
    slot = lax.broadcasted_iota(jnp.int32, (16, 128), 0).astype(F32)
    ones = jnp.where(slot == value, 1.0, 0.0).astype(BF16)
    return jnp.concatenate([ones, ones, ones], axis=0)


def live_rows(count, block, number):
    slot = lax.broadcasted_iota(jnp.int32, (number, 1), 0)
    return slot < (count + 1 - block) // 2


def live_bias(count):
    slot = lax.broadcasted_iota(jnp.int32, (256, 1), 0)
    block = slot // 128
    return jnp.where(slot - 128 * block < (count + 1 - block) // 2, 0.0, -1e30)


def half_mask(head):
    return lax.broadcasted_iota(jnp.int32, (1, 128), 1) // HD == head


def fused_kernel(
    lengths, tokens, cotangent, seen, shard_I, shard_O, shard_E, shard_R, shard_V, table,
    layer_out, tokens_grad, grad_I, grad_O, grad_E, grad_R, grad_V, *refs,
):
    s = Store(refs)
    here = Place()
    z, x, c, y = here.z, here.x, here.c, here.y
    own = here.column(0, 0, 0)

    barrier = pltpu.get_barrier_semaphore()
    partners = [here.to_z(1), here.to_z(2), here.to_z(3), here.to_x, here.to_y, here.to_c]
    for device in partners:
        pl.semaphore_signal(barrier, inc=1, device_id=device, device_id_type=MESH)

    for name, shard in ((W_I, shard_I), (W_O, shard_O), (W_E, shard_E)):
        whole = shard[...].astype(F32)
        half = whole.shape[1] // 2
        unit = jnp.concatenate([whole[:, :half], whole[:, half:]], axis=0)
        s.G[name][z, own] = unit.astype(BF16)
    s.G[W_R][z, own] = shard_R[...]
    s.G[VEC][z, own] = shard_V[...]
    s.SEEN[:, y] = seen[pl.ds(2 * y, 2)]
    pl.semaphore_wait(barrier, len(partners))

    gather = {
        name: Gather(here, s.G[name], s.GS[name], s.GQ[name]) for name in TENSORS
    }
    swap_s, swap_r = s.SWS, s.SWR
    mine, other = pl.ds(2 * y, 2), pl.ds(2 * (1 - y), 2)
    swaps = [
        remote(tokens.at[other], s.TOK.at[:, y], swap_s.at[0], swap_r.at[0], here.to_y),
        remote(seen.at[other], s.SEEN.at[:, y], swap_s.at[1], swap_r.at[1], here.to_y),
        remote(cotangent.at[other], s.INC.at[:, y], swap_s.at[2], swap_r.at[2], here.to_y),
    ]
    came = [
        remote(s.TOK.at[:, 1 - y], s.TOK.at[:, 1 - y], swap_s.at[0], swap_r.at[0], here.to_y),
        remote(s.SEEN.at[:, 1 - y], s.SEEN.at[:, 1 - y], swap_s.at[1], swap_r.at[1], here.to_y),
        remote(s.INC.at[:, 1 - y], s.INC.at[:, 1 - y], swap_s.at[2], swap_r.at[2], here.to_y),
    ]
    local = [
        pltpu.make_async_copy(tokens.at[mine], s.TOK.at[:, y], s.LOC.at[0]),
        pltpu.make_async_copy(cotangent.at[mine], s.INC.at[:, y], s.LOC.at[1]),
    ]
    gather[VEC].begin()
    gather[W_I].begin()
    swaps[1].start()
    swaps[0].start()
    local[0].start()
    local[1].start()
    gather[W_O].begin()
    gather[W_E].begin()
    gather[W_R].begin()
    swaps[2].start()

    def step_z(name):
        for k in (1, 3, 2):
            gather[name].pass_on(k)
        gather[name].own_to_core()

    def step_relay(name):
        for k in range(4):
            gather[name].relay(k)
        gather[name].sides_to_core()

    def step_corner(name):
        gather[name].corner()

    def step_last(name):
        gather[name].from_core()

    for name in (VEC, W_I, W_O):
        step_z(name)
    for name in (VEC, W_I, W_O):
        step_relay(name)
    step_z(W_E)
    for name in (VEC, W_I):
        step_corner(name)
    step_last(VEC)

    vec = s.ROWS
    for number in range(VECTORS):
        group = s.G[VEC][:, :, number // 4, :].reshape(32, 128)
        vec[pl.ds(number, 1), :] = collect(group, spread_matrix(number % 4), CHUNK, 0)
    group = s.G[VEC][:, :, 2, :].reshape(32, 128)
    for part in range(4):
        cols = slice(768 * part, 768 * part + 768)
        s.EB[:, cols] = collect(group, spread_matrix(None), 4 * CHUNK, 8 * part)

    def vector(number):
        return vec[pl.ds(number, 1), :]

    s.PB[:, 0:768] = vector(2)
    s.PB[:, 768:1536] = jnp.zeros((1, 768), F32)
    s.PB[:, 1536:2304] = vector(3)
    sums = s.SUMS
    sums[...] = jnp.zeros_like(sums)
    s.EBG[...] = jnp.zeros_like(s.EBG)

    for copy in (swaps[0], swaps[1]):
        copy.wait_send()
    local[0].wait()
    came[1].wait_recv()
    came[0].wait_recv()

    def first_norm(block, carry):
        it, half = block // 2, block % 2
        rows = rows_at(128 * block, 128)
        patch = s.SEEN[it, half][0:1, :].astype(F32)
        frame = jnp.floor((patch + 0.5) * (1.0 / (GRID * GRID)))
        inside = patch - frame * (GRID * GRID)
        line = jnp.floor((inside + 0.5) * (1.0 / GRID))
        across = inside - line * GRID
        place = jnp.concatenate([tn(one_hot(v), table[...]) for v in (frame, line, across)], axis=1)
        entry = s.TOK[it, half].astype(F32) + place
        s.ENT[rows, :] = entry
        unit, _ = normalise(entry)
        normed = (unit * vector(0) + vector(1)).astype(BF16)
        s.XB[rows, :] = normed
        s.NRMT[:, lanes(128 * block, 128)] = normed.T
        return carry

    lax.fori_loop(0, 4, first_norm, 0)

    def lay_out(name, target, half):
        buf = s.G[name]

        def one(i, carry):
            zz, pair = i // 4, 2 * (i % 4)
            even = buf[zz, pair].astype(F32)
            odd = buf[zz, pair + 1].astype(F32)
            rows = pl.ds(pl.multiple_of(48 * i, 16), 48)
            target[rows, :half] = jnp.concatenate([even[:24], odd[:24]], axis=0).astype(BF16)
            target[rows, half:] = jnp.concatenate([even[24:], odd[24:]], axis=0).astype(BF16)
            return carry

        lax.fori_loop(0, 16, one, 0)

    step_last(W_I)
    lay_out(W_I, s.WI, 1152)

    def project(n, carry):
        cols = lanes(256 * n, 256)
        s.PRJ[:, cols] = (nn(s.XB[...], s.WI[:, cols]) + s.PB[:, cols]).astype(BF16)
        return carry

    lax.fori_loop(0, 9, project, 0)

    step_relay(W_E)
    step_corner(W_O)
    step_z(W_R)
    step_last(W_O)
    lay_out(W_O, s.WO, 384)

    def attend(step, carry):
        it, pair = step // 6, step % 6
        rows = rows_at(256 * it, 256)
        cols = lanes(128 * pair, 128)
        q = s.PRJ[rows, cols]
        k = s.PRJ[rows, lanes(768 + 128 * pair, 128)]
        v = s.PRJ[rows, lanes(1536 + 128 * pair, 128)]
        bias = live_bias(lengths[2 * y + it])
        total = jnp.zeros((128, 256), F32)
        for head in range(2):
            mask = half_mask(head)
            scores = nt(jnp.where(mask, k, 0), q) * SCORE_SCALE + bias
            exponent = jnp.exp(scores - jnp.max(scores, axis=0, keepdims=True))
            attention = exponent * (1.0 / jnp.sum(exponent, axis=0, keepdims=True))
            low = attention.astype(BF16)
            s.ATN[2 * step + head] = low
            total = total + tn(jnp.where(mask, v, 0), low)
        s.ATTT[cols, rows] = total.astype(BF16)
        s.XB[rows, cols] = total.T.astype(BF16)
        return carry

    lax.fori_loop(0, 6, attend, 0)
    step_corner(W_E)
    step_relay(W_R)
    lax.fori_loop(6, 12, attend, 0)

    def second_norm(it, carry):
        rows = rows_at(256 * it, 256)
        middle = s.ENT[rows, :] + nn(s.XB[rows, :], s.WO[...]) + vector(4)
        s.MID[rows, :] = middle
        unit, _ = normalise(middle)
        second = (unit * vector(5) + vector(6)).astype(BF16)
        s.XB[rows, :] = second
        s.SECT[:, rows] = second.T
        return carry

    lax.fori_loop(0, 2, second_norm, 0)
    step_last(W_E)
    lay_out(W_E, s.WE, 1536)
    step_corner(W_R)

    def expand(step, carry):
        n, it = step // 2, step % 2
        cols = lanes(256 * n, 256)
        rows = rows_at(256 * it, 256)
        expanded = nn(s.XB[rows, :], s.WE[:, cols]) + s.EB[:, cols]
        normal = 0.5 * (1.0 + lax.erf(expanded * 0.7071067811865476))
        density = jnp.exp(-0.5 * expanded * expanded) * 0.3989422804014327
        s.ACT[rows, cols] = (expanded * normal).astype(BF16)
        s.GP[rows, cols] = (normal + expanded * density).astype(BF16)
        return carry

    lax.fori_loop(0, 24, expand, 0)

    swaps[2].wait_send()
    local[1].wait()
    came[2].wait_recv()

    def take_in(block, carry):
        it, half = block // 2, block % 2
        live = live_rows(lengths[2 * y + it], half, 128)
        incoming = jnp.where(live, s.INC[it, half].astype(F32), 0.0)
        s.INC[it, half] = incoming.astype(BF16)
        sums[7:8, :] += jnp.sum(incoming, axis=0, keepdims=True)
        return carry

    lax.fori_loop(0, 4, take_in, 0)

    reduce = {
        name: Reduce(
            here, s.P[name], s.RC[name], s.R1[name], s.R2[name], s.RZ[name],
            s.RS[name], s.RQ[name],
        )
        for name in TENSORS
    }

    def reduce_weight_grad(f, carry):
        zz, xx = f // 2, f % 2
        moved = s.ACT[:, lanes(384 * f, 384)].T
        part = nn(moved, s.INC[...].reshape(512, 768))
        s.P[W_R][zz, pl.ds(4 * xx, 4)] = part.reshape(4, 96, 768).astype(BF16)
        return carry

    lax.fori_loop(0, 8, reduce_weight_grad, 0)
    reduce[W_R].core_send()

    step_last(W_R)

    def expanded_grad(step, carry):
        zz, it = step // 2, step % 2
        rows = rows_at(256 * it, 256)
        cols = lanes(768 * zz, 768)
        weight = s.G[W_R][zz].reshape(768, 768)
        incoming = s.INC[it].reshape(256, 768)
        grad = (nt(incoming, weight) * s.GP[rows, cols].astype(F32)).astype(BF16)
        s.GP[rows, cols] = grad
        s.EBG[:, cols] += jnp.sum(grad.astype(F32), axis=0, keepdims=True)
        return carry

    lax.fori_loop(0, 8, expanded_grad, 0)
    reduce[W_R].core_add()

    def weight_grad(name, moved, grad, half, wide):
        part = s.P[name]

        def one(step, carry):
            n, m = step // 2, step % 2
            left = grad[:, lanes(wide * n, wide)]
            right = grad[:, lanes(half + wide * n, wide)]
            block = nn(moved[rows_at(384 * m, 384), :], jnp.concatenate([left, right], axis=1))
            for j in range(8):
                for side in range(2):
                    rows = slice(48 * j + 24 * side, 48 * j + 24 * side + 24)
                    unit = jnp.concatenate([block[rows, :wide], block[rows, wide:]], axis=0)
                    part[2 * m + j // 4, 2 * (j % 4) + side, :, lanes(wide * n, wide)] = unit.astype(BF16)
            return carry

        lax.fori_loop(0, 2 * half // wide, one, 0)

    gather[W_E].drain()
    weight_grad(W_E, s.SECT, s.GP, 1536, 256)
    reduce[W_E].core_send()

    def finish_rows(it, carry):
        rows = rows_at(256 * it, 256)
        out = s.MID[rows, :] + vector(7)
        for zz in range(4):
            out = out + nn(s.ACT[rows, 768 * zz : 768 * zz + 768], s.G[W_R][zz].reshape(768, 768))
        for half in range(2):
            live = live_rows(lengths[2 * y + it], half, 128)
            s.TOK[it, half] = jnp.where(live, out[128 * half : 128 * half + 128], 0.0).astype(BF16)
        return carry

    lax.fori_loop(0, 2, finish_rows, 0)
    out_there = remote(
        s.TOK.at[:, 1 - y], layer_out.at[mine], swap_s.at[3], swap_r.at[3], here.to_y
    )
    out_came = remote(s.TOK.at[:, y], layer_out.at[other], swap_s.at[3], swap_r.at[3], here.to_y)
    out_here = pltpu.make_async_copy(s.TOK.at[:, y], layer_out.at[mine], s.LOC.at[2])
    out_there.start()
    out_here.start()

    reduce[W_R].relay()

    def middle_back(it, carry):
        rows = rows_at(256 * it, 256)
        grad = nt(s.GP[rows, :], s.WE[...])
        unit, inverse = normalise(s.MID[rows, :])
        sums[5:6, :] += jnp.sum(grad * unit, axis=0, keepdims=True)
        sums[6:7, :] += jnp.sum(grad, axis=0, keepdims=True)
        incoming = s.INC[it].reshape(256, 768).astype(F32)
        middle_grad = incoming + normalise_back(grad * vector(5), unit, inverse)
        s.MID[rows, :] = middle_grad
        branch = middle_grad.astype(BF16)
        s.XB[rows, :] = branch
        sums[4:5, :] += jnp.sum(branch.astype(F32), axis=0, keepdims=True)
        return carry

    lax.fori_loop(0, 2, middle_back, 0)
    reduce[W_E].core_add()
    pl.semaphore_signal(s.SPARE, inc=1, device_id=here.to_c, device_id_type=MESH)
    gather[W_O].drain()
    weight_grad(W_O, s.ATTT, s.XB, 384, 128)
    reduce[W_O].core_send()

    def attended_back(it, carry):
        rows = rows_at(256 * it, 256)
        s.XB[rows, :] = nt(s.XB[rows, :], s.WO[...]).astype(BF16)
        return carry

    lax.fori_loop(0, 2, attended_back, 0)
    reduce[W_R].sides()
    reduce[W_E].relay()

    def attend_back(step, carry):
        it, pair = step // 6, step % 6
        rows = rows_at(256 * it, 256)
        cols = lanes(128 * pair, 128)
        k_cols, v_cols = lanes(768 + 128 * pair, 128), lanes(1536 + 128 * pair, 128)
        q = s.PRJ[rows, cols]
        k = s.PRJ[rows, k_cols]
        v = s.PRJ[rows, v_cols]
        grad = s.XB[rows, cols]
        query_grad = jnp.zeros((128, 256), F32)
        key_grad = jnp.zeros((256, 128), F32)
        value_grad = jnp.zeros((256, 128), F32)
        for head in range(2):
            mask = half_mask(head)
            mine_grad = jnp.where(mask, grad, 0)
            weight_back = nt(v, mine_grad)
            low = s.ATN[2 * step + head]
            attention = low.astype(F32)
            inner = jnp.sum(attention * weight_back, axis=0, keepdims=True)
            scores_grad = (attention * (weight_back - inner)).astype(BF16)
            query_grad = query_grad + tn(jnp.where(mask, k, 0), scores_grad)
            key_grad = key_grad + nn(scores_grad, jnp.where(mask, q, 0))
            value_grad = value_grad + nn(low, mine_grad)
        query_low = (query_grad * SCORE_SCALE).T.astype(BF16)
        value_low = value_grad.astype(BF16)
        s.PRJ[rows, cols] = query_low
        s.PRJ[rows, k_cols] = (key_grad * SCORE_SCALE).astype(BF16)
        s.PRJ[rows, v_cols] = value_low
        sums[2:3, cols] += jnp.sum(query_low.astype(F32), axis=0, keepdims=True)
        sums[3:4, cols] += jnp.sum(value_low.astype(F32), axis=0, keepdims=True)
        return carry

    lax.fori_loop(0, 6, attend_back, 0)
    reduce[W_O].core_add()
    reduce[W_E].sides()
    lax.fori_loop(6, 12, attend_back, 0)
    gather[W_I].drain()
    weight_grad(W_I, s.NRMT, s.PRJ, 1152, 128)
    reduce[W_I].core_send(s.SPARE)
    reduce[W_O].relay()

    def entry_back(step, carry):
        it = step % 2
        half = jnp.where(step < 2, 1 - y, y)
        rows = rows_at(256 * it + 128 * half, 128)
        grad = nt(s.PRJ[rows, :], s.WI[...])
        unit, inverse = normalise(s.ENT[rows, :])
        sums[0:1, :] += jnp.sum(grad * unit, axis=0, keepdims=True)
        sums[1:2, :] += jnp.sum(grad, axis=0, keepdims=True)
        out = s.MID[rows, :] + normalise_back(grad * vector(0), unit, inverse)
        s.ENT[rows, :] = out
        s.INC[it, half] = out.astype(BF16)
        return carry

    lax.fori_loop(0, 2, entry_back, 0)
    grad_there = remote(s.INC.at[:, 1 - y], s.TGR, swap_s.at[4], swap_r.at[4], here.to_y)
    grad_there.start()
    lax.fori_loop(2, 4, entry_back, 0)
    grad_here = [
        pltpu.make_async_copy(
            s.ENT.at[rows_at(256 * it + 128 * y, 128)], tokens_grad.at[2 * y + it], s.LOC.at[3 + it]
        )
        for it in range(2)
    ]
    for copy in grad_here:
        copy.start()
    reduce[W_I].core_add()
    reduce[W_O].sides()

    for number in range(VECTORS):
        dealt = deal(sums[number : number + 1, :], spread_matrix(number % 4), CHUNK, 0)
        if number % 4 == 0:
            group = dealt
        else:
            group = group + dealt
        if number % 4 == 3:
            s.P[VEC][:, :, number // 4, :] = group.reshape(4, 8, 128)
    group = jnp.zeros((32, 128), F32)
    for part in range(4):
        row = s.EBG[:, 768 * part : 768 * part + 768]
        group = group + deal(row, spread_matrix(None), 4 * CHUNK, 8 * part)
    s.P[VEC][:, :, 2, :] = group.reshape(4, 8, 128)
    for row in range(3, 8):
        s.P[VEC][:, :, row, :] = jnp.zeros((4, 8, 128), F32)
    reduce[VEC].core_send()
    reduce[W_I].relay()
    reduce[VEC].core_add()
    reduce[VEC].relay()
    grad_R[...] = reduce[W_R].finish()

    def place_grad(name, ref, half):
        total = reduce[name].finish()
        ref[:, :half] = total[:24]
        ref[:, half:] = total[24:]

    place_grad(W_E, grad_E, 1536)
    reduce[W_I].sides()
    reduce[VEC].sides()
    place_grad(W_O, grad_O, 384)
    grad_there.wait_send()
    remote(s.INC.at[:, 1 - y], s.TGR, swap_s.at[4], swap_r.at[4], here.to_y).wait_recv()
    for copy in grad_here:
        copy.wait()
    grad_rest = []
    for it in range(2):
        rows = rows_at(256 * it + 128 * (1 - y), 128)
        s.ENT[rows, :] = s.TGR[it].astype(F32)
        copy = pltpu.make_async_copy(
            s.ENT.at[rows], tokens_grad.at[2 * (1 - y) + it], s.LOC.at[5 + it]
        )
        copy.start()
        grad_rest.append(copy)
    place_grad(W_I, grad_I, 1152)
    grad_V[...] = reduce[VEC].finish()
    for copy in grad_rest:
        copy.wait()
    out_there.wait_send()
    out_here.wait()
    out_came.wait_recv()
    gather[VEC].drain()
    gather[W_R].drain()
    for name in TENSORS:
        reduce[name].drain()


UNITS = ((48, 1152), (48, 384), (48, 1536), (96, 768), (8, 128))


def scratch_list():
    dma, vmem = pltpu.SemaphoreType.DMA, pltpu.VMEM
    shapes = dict(
        SWS=dma((5,)),
        SWR=dma((5,)),
        LOC=dma((7,)),
        SPARE=pltpu.SemaphoreType.REGULAR,
        TOK=vmem((2, 2, 128, 768), BF16),
        INC=vmem((2, 2, 128, 768), BF16),
        SEEN=vmem((2, 2, 8, 128), jnp.int32),
        ROWS=vmem((8, 768), F32),
        EB=vmem((1, 3072), F32),
        PB=vmem((1, 2304), F32),
        SUMS=vmem((8, 768), F32),
        EBG=vmem((1, 3072), F32),
        WI=vmem((768, 2304), BF16),
        WO=vmem((768, 768), BF16),
        WE=vmem((768, 3072), BF16),
        ENT=vmem((512, 768), F32),
        MID=vmem((512, 768), F32),
        XB=vmem((512, 768), BF16),
        NRMT=vmem((768, 512), BF16),
        ATTT=vmem((768, 512), BF16),
        SECT=vmem((768, 512), BF16),
        PRJ=vmem((512, 2304), BF16),
        ATN=vmem((24, 256, 256), BF16),
        ACT=vmem((512, 3072), BF16),
        GP=vmem((512, 3072), BF16),
        TGR=vmem((2, 128, 768), BF16),
    )
    many = dict(G=[], GS=[], GQ=[], P=[], RC=[], R1=[], R2=[], RZ=[], RS=[], RQ=[])
    for name in TENSORS:
        kind = F32 if name == VEC else BF16
        unit = UNITS[name]
        many["G"].append(vmem((4, 8, *unit), kind))
        many["GS"].append(dma((AG_SEMS,)))
        many["GQ"].append(dma((AG_SEMS,)))
        if name in (W_R, VEC):
            many["P"].append(vmem((4, 8, *unit), kind))
        if name != W_I:
            many["RC"].append(vmem((4, 4, *unit), kind))
        many["R1"].append(vmem((4, *unit), kind))
        many["R2"].append(vmem((4, 2, *unit), kind))
        many["RZ"].append(vmem((3, *unit), kind))
        many["RS"].append(dma((RS_SEMS,)))
        many["RQ"].append(dma((RS_SEMS,)))
    return shapes, many


class Store:
    def __init__(self, refs):
        shapes, many = scratch_list()
        refs = list(refs)
        for name in shapes:
            setattr(self, name, refs.pop(0))
        for name, listed in many.items():
            setattr(self, name, [refs.pop(0) for _ in listed])
        self.P = self.G[:3] + self.P
        self.RC = [self.RC[1].at[:, :, :, :1152]] + self.RC


def position_table():
    step = np.arange(16, dtype=np.float64)[:, None]
    channel = np.arange(256)
    angle = step * np.power(10000.0, -(channel // 2) / 128.0)
    whole = np.where(channel % 2 == 0, np.sin(angle), np.cos(angle)).astype(np.float32)
    high = whole.astype(jnp.bfloat16)
    rest = whole - high.astype(np.float32)
    middle = rest.astype(jnp.bfloat16)
    low = (rest - middle.astype(np.float32)).astype(jnp.bfloat16)
    return np.concatenate([high, middle, low], axis=0)


def fused_body(
    tokens, visible, lengths, first_gain, first_shift, input_weight, query_bias, value_bias,
    output_weight, output_bias, second_gain, second_shift, expand_weight, expand_bias,
    reduce_weight, reduce_bias, cotangent,
):
    chunks = jnp.concatenate(
        [
            jnp.stack(
                [first_gain, first_shift, query_bias, value_bias, output_bias, second_gain, second_shift, reduce_bias]
            ),
            expand_bias.reshape(4, CHUNK),
        ],
        axis=0,
    ).astype(F32)
    shard_V = jnp.pad(chunks, ((0, 20), (0, 32 - CHUNK))).reshape(8, 128)
    seen = jnp.broadcast_to(visible, (4, 8, 128))
    hbm = pl.BlockSpec(memory_space=pl.ANY)
    vmem = pl.BlockSpec(memory_space=pltpu.VMEM)
    smem = pl.BlockSpec(memory_space=pltpu.SMEM)
    shapes, many = scratch_list()
    results = [
        jax.ShapeDtypeStruct((4, 128, 768), BF16),
        jax.ShapeDtypeStruct((4, 128, 768), F32),
        jax.ShapeDtypeStruct(input_weight.shape, F32),
        jax.ShapeDtypeStruct(output_weight.shape, F32),
        jax.ShapeDtypeStruct(expand_weight.shape, F32),
        jax.ShapeDtypeStruct(reduce_weight.shape, F32),
        jax.ShapeDtypeStruct((8, 128), F32),
    ]
    layer_out, tokens_grad, grad_I, grad_O, grad_E, grad_R, grad_V = pl.pallas_call(
        fused_kernel,
        name="layer",
        out_shape=results,
        in_specs=[smem, hbm, hbm, vmem, vmem, vmem, vmem, vmem, vmem, vmem],
        out_specs=[hbm, hbm, vmem, vmem, vmem, vmem, vmem],
        scratch_shapes=[*shapes.values(), *(shape for listed in many.values() for shape in listed)],
        compiler_params=pltpu.CompilerParams(
            collective_id=0, has_side_effects=True, vmem_limit_bytes=VMEM_BYTES
        ),
    )(
        lengths, tokens[:, 0], cotangent[:, 0], seen, input_weight, output_weight, expand_weight,
        reduce_weight, shard_V, jnp.asarray(position_table()),
    )
    dealt = grad_V.reshape(32, 32)[:12, :CHUNK]
    return (
        layer_out[:, None], tokens_grad[:, None], dealt[0], dealt[1], grad_I, dealt[2], dealt[3], grad_O,
        dealt[4], dealt[5], dealt[6], grad_E, dealt[8:12].reshape(4 * CHUNK), grad_R, dealt[7],
    )


VMEM_BYTES = 67000000


def solution(mesh):
    in_specs = (
        P("items", "seq", None, None),
        P("items", "seq", None),
        P("items"),
        P(("items", "seq")),
        P(("items", "seq")),
        P(("items", "seq"), None),
        P(("items", "seq")),
        P(("items", "seq")),
        P(("items", "seq"), None),
        P(("items", "seq")),
        P(("items", "seq")),
        P(("items", "seq")),
        P(("items", "seq"), None),
        P(("items", "seq")),
        P(("items", "seq"), None),
        P(("items", "seq")),
        P("items", "seq", None, None),
    )
    out_specs = (
        P("items", "seq", None, None),
        P("items", "seq", None, None),
        P(("items", "seq")),
        P(("items", "seq")),
        P(("items", "seq"), None),
        P(("items", "seq")),
        P(("items", "seq")),
        P(("items", "seq"), None),
        P(("items", "seq")),
        P(("items", "seq")),
        P(("items", "seq")),
        P(("items", "seq"), None),
        P(("items", "seq")),
        P(("items", "seq"), None),
        P(("items", "seq")),
    )
    sizes = (mesh.shape["items"], mesh.shape["seq"])
    chosen = fused_body if sizes == (Z_SIZE * 4, 2) else general_body
    return jax.shard_map(chosen, mesh=mesh, in_specs=in_specs, out_specs=out_specs, check_vma=False)
```

```python
import functools

import jax
import jax.numpy as jnp
import numpy as np
from jax import lax
from jax.experimental import pallas as pl
from jax.experimental.pallas import tpu as pltpu
from jax.sharding import PartitionSpec as P

HD = 64
GRID = 14
MICRO = 2
ITEMS_MB = 2


EPSILON = 1e-06
SCORE_SCALE = 0.125


def layer_norm(rows_in, gain, shift):
    centre = rows_in - jnp.mean(rows_in, axis=-1, keepdims=True)
    spread = jnp.mean(centre * centre, axis=-1, keepdims=True)
    return centre * lax.rsqrt(spread + EPSILON) * gain + shift


def gelu_exact(value_in):
    return jax.nn.gelu(value_in, approximate=False)


def positions(index, model_width):
    channel = jnp.arange(model_width)
    portion = 3 * channel // model_width
    frequency = jnp.power(10000.0, -(channel % 256 // 2).astype(jnp.float32) / 128.0)
    which_frame = index // (GRID * GRID)
    which_row = index % (GRID * GRID) // GRID
    which_column = index % GRID
    coordinate = jnp.where(
        portion == 0,
        which_frame[..., None],
        jnp.where(portion == 1, which_row[..., None], which_column[..., None]),
    )
    angle = coordinate.astype(jnp.float32) * frequency
    return jnp.where(channel % 2 == 0, jnp.sin(angle), jnp.cos(angle))


def contract_rows(left, right):
    return lax.dot_general(
        left, right, (((0,), (0,)), ((), ())), preferred_element_type=jnp.float32
    )


def against(left, right):
    return lax.dot_general(
        left, right, (((1,), (1,)), ((), ())), preferred_element_type=jnp.float32
    )


def row_masks(lengths, block_rows, block_number):
    counts = (lengths + 1 - block_number) // 2
    return jnp.arange(block_rows)[None, :] < counts[:, None]


def micro_batch(gathered, tokens, visible, lengths, cotangent, seq_place):
    (
        first_gain,
        first_shift,
        input_weight,
        query_bias,
        value_bias,
        output_weight,
        output_bias,
        second_gain,
        second_shift,
        expand_weight,
        expand_bias,
        reduce_weight,
        reduce_bias,
    ) = gathered
    item_count, block_rows, model_width = tokens.shape
    head_count = model_width // HD
    total_rows = item_count * block_rows
    (
        first_gain,
        first_shift,
        query_bias,
        value_bias,
        output_bias,
        second_gain,
        second_shift,
        expand_bias,
        reduce_bias,
    ) = (
        vector.astype(jnp.float32)
        for vector in (
            first_gain,
            first_shift,
            query_bias,
            value_bias,
            output_bias,
            second_gain,
            second_shift,
            expand_bias,
            reduce_bias,
        )
    )
    query_live = row_masks(lengths, block_rows, seq_place).reshape(total_rows, 1)
    key_live = jnp.concatenate(
        [row_masks(lengths, block_rows, 0), row_masks(lengths, block_rows, 1)], axis=1
    )
    key_mask = key_live[:, None, None, :]
    entry = tokens.reshape(total_rows, model_width).astype(jnp.float32) + positions(
        visible.reshape(total_rows), model_width
    )
    normed, first_pull = jax.vjp(layer_norm, entry, first_gain, first_shift)
    normed_low = normed.astype(jnp.bfloat16)
    joined_bias = jnp.concatenate([query_bias, jnp.zeros_like(query_bias), value_bias])
    projected = (
        jnp.dot(normed_low, input_weight, preferred_element_type=jnp.float32) + joined_bias
    ).astype(jnp.bfloat16)
    queries = projected[:, :model_width].reshape(item_count, block_rows, head_count, HD)
    keys_here = projected[:, model_width : 2 * model_width].reshape(
        item_count, block_rows, model_width
    )
    values_here = projected[:, 2 * model_width :].reshape(item_count, block_rows, model_width)
    keys_all, values_all = (
        lax.all_gather(keys_here, "seq", axis=1, tiled=True),
        lax.all_gather(values_here, "seq", axis=1, tiled=True),
    )
    keys_all = keys_all.reshape(item_count, 2 * block_rows, head_count, HD)
    values_all = values_all.reshape(item_count, 2 * block_rows, head_count, HD)
    scores = (
        jnp.einsum("cqhd,ckhd->chqk", queries, keys_all, preferred_element_type=jnp.float32)
        * SCORE_SCALE
    )
    scores = jnp.where(key_mask, scores, -1e30)
    row_max = jnp.max(scores, axis=-1, keepdims=True)
    exponent = jnp.exp(scores - row_max)
    row_total = jnp.sum(exponent, axis=-1, keepdims=True)
    attention_low = (exponent / row_total).astype(jnp.bfloat16)
    log_total = row_max + jnp.log(row_total)
    attended = jnp.einsum(
        "chqk,ckhd->cqhd", attention_low, values_all, preferred_element_type=jnp.float32
    )
    attended = attended.reshape(total_rows, model_width).astype(jnp.bfloat16)
    middle = (
        entry + jnp.dot(attended, output_weight, preferred_element_type=jnp.float32) + output_bias
    )
    second, second_pull = jax.vjp(layer_norm, middle, second_gain, second_shift)
    second_low = second.astype(jnp.bfloat16)
    expanded = jnp.dot(second_low, expand_weight, preferred_element_type=jnp.float32) + expand_bias
    activated, gelu_pull = jax.vjp(gelu_exact, expanded)
    activated_low = activated.astype(jnp.bfloat16)
    result = (
        middle
        + jnp.dot(activated_low, reduce_weight, preferred_element_type=jnp.float32)
        + reduce_bias
    )
    layer_out = jnp.where(query_live, result, 0.0).astype(jnp.bfloat16)
    incoming = jnp.where(
        query_live, cotangent.reshape(total_rows, model_width).astype(jnp.float32), 0.0
    )
    incoming_low = incoming.astype(jnp.bfloat16)
    reduce_weight_grad = contract_rows(activated_low, incoming_low)
    reduce_bias_grad = jnp.sum(incoming, axis=0)
    activated_grad = against(incoming_low, reduce_weight)
    expanded_grad = gelu_pull(activated_grad)[0].astype(jnp.bfloat16)
    expand_weight_grad = contract_rows(second_low, expanded_grad)
    expand_bias_grad = jnp.sum(expanded_grad.astype(jnp.float32), axis=0)
    second_grad = against(expanded_grad, expand_weight)
    middle_part, second_gain_grad, second_shift_grad = second_pull(second_grad)
    middle_grad = incoming + middle_part
    branch_grad = middle_grad.astype(jnp.bfloat16)
    output_weight_grad = contract_rows(attended, branch_grad)
    output_bias_grad = jnp.sum(branch_grad.astype(jnp.float32), axis=0)
    attended_grad = against(branch_grad, output_weight).astype(jnp.bfloat16)
    attended_grad = attended_grad.reshape(item_count, block_rows, head_count, HD)
    scores = (
        jnp.einsum("cqhd,ckhd->chqk", queries, keys_all, preferred_element_type=jnp.float32)
        * SCORE_SCALE
    )
    scores = jnp.where(key_mask, scores, -1e30)
    attention_full = jnp.exp(scores - log_total)
    attention_low = attention_full.astype(jnp.bfloat16)
    weight_grad = jnp.einsum(
        "cqhd,ckhd->chqk", attended_grad, values_all, preferred_element_type=jnp.float32
    )
    row_inner = jnp.sum(attention_full * weight_grad, axis=-1, keepdims=True)
    scores_grad = (attention_full * (weight_grad - row_inner)).astype(jnp.bfloat16)
    query_grad = (
        jnp.einsum("chqk,ckhd->cqhd", scores_grad, keys_all, preferred_element_type=jnp.float32)
        * SCORE_SCALE
    )
    key_terms = (
        jnp.einsum("chqk,cqhd->ckhd", scores_grad, queries, preferred_element_type=jnp.float32)
        * SCORE_SCALE
    )
    value_terms = jnp.einsum(
        "chqk,cqhd->ckhd", attention_low, attended_grad, preferred_element_type=jnp.float32
    )
    key_grad, value_grad = (
        lax.psum_scatter(
            key_terms.reshape(item_count, 2 * block_rows, model_width).astype(jnp.bfloat16),
            "seq",
            scatter_dimension=1,
            tiled=True,
        ).astype(jnp.float32),
        lax.psum_scatter(
            value_terms.reshape(item_count, 2 * block_rows, model_width).astype(jnp.bfloat16),
            "seq",
            scatter_dimension=1,
            tiled=True,
        ).astype(jnp.float32),
    )
    projected_grad = jnp.concatenate(
        [
            query_grad.reshape(total_rows, model_width),
            key_grad.reshape(total_rows, model_width),
            value_grad.reshape(total_rows, model_width),
        ],
        axis=1,
    ).astype(jnp.bfloat16)
    input_weight_grad = contract_rows(normed_low, projected_grad)
    projected_sums = jnp.sum(projected_grad.astype(jnp.float32), axis=0)
    query_bias_grad = projected_sums[:model_width]
    value_bias_grad = projected_sums[2 * model_width :]
    normed_grad = against(projected_grad, input_weight)
    entry_part, first_gain_grad, first_shift_grad = first_pull(normed_grad)
    tokens_grad = middle_grad + entry_part
    grads = (
        first_gain_grad,
        first_shift_grad,
        input_weight_grad,
        query_bias_grad,
        value_bias_grad,
        output_weight_grad,
        output_bias_grad,
        second_gain_grad,
        second_shift_grad,
        expand_weight_grad,
        expand_bias_grad,
        reduce_weight_grad,
        reduce_bias_grad,
    )
    return (layer_out, tokens_grad, grads)


def general_body(
    tokens,
    visible,
    lengths,
    first_gain,
    first_shift,
    input_weight,
    query_bias,
    value_bias,
    output_weight,
    output_bias,
    second_gain,
    second_shift,
    expand_weight,
    expand_bias,
    reduce_weight,
    reduce_bias,
    cotangent,
):
    shards = (
        first_gain,
        first_shift,
        input_weight,
        query_bias,
        value_bias,
        output_weight,
        output_bias,
        second_gain,
        second_shift,
        expand_weight,
        expand_bias,
        reduce_weight,
        reduce_bias,
    )
    seq_place = lax.axis_index("seq")
    block_rows = tokens.shape[2]
    model_width = tokens.shape[3]
    outputs_list = []
    gradients_list = []
    totals = None
    for micro_index in range(MICRO):
        first_item = micro_index * ITEMS_MB
        last_item = first_item + ITEMS_MB
        gathered = (
            lax.all_gather(shards[0], ("items", "seq"), axis=0, tiled=True),
            lax.all_gather(shards[1], ("items", "seq"), axis=0, tiled=True),
            lax.all_gather(shards[2], ("items", "seq"), axis=0, tiled=True),
            lax.all_gather(shards[3], ("items", "seq"), axis=0, tiled=True),
            lax.all_gather(shards[4], ("items", "seq"), axis=0, tiled=True),
            lax.all_gather(shards[5], ("items", "seq"), axis=0, tiled=True),
            lax.all_gather(shards[6], ("items", "seq"), axis=0, tiled=True),
            lax.all_gather(shards[7], ("items", "seq"), axis=0, tiled=True),
            lax.all_gather(shards[8], ("items", "seq"), axis=0, tiled=True),
            lax.all_gather(shards[9], ("items", "seq"), axis=0, tiled=True),
            lax.all_gather(shards[10], ("items", "seq"), axis=0, tiled=True),
            lax.all_gather(shards[11], ("items", "seq"), axis=0, tiled=True),
            lax.all_gather(shards[12], ("items", "seq"), axis=0, tiled=True),
        )
        layer_out, tokens_grad, grads = micro_batch(
            gathered,
            tokens[first_item:last_item, 0],
            visible[first_item:last_item, 0],
            lengths[first_item:last_item],
            cotangent[first_item:last_item, 0],
            seq_place,
        )
        outputs_list.append(layer_out)
        gradients_list.append(tokens_grad)
        shares = (
            lax.psum_scatter(grads[0], ("items", "seq"), scatter_dimension=0, tiled=True),
            lax.psum_scatter(grads[1], ("items", "seq"), scatter_dimension=0, tiled=True),
            lax.psum_scatter(grads[2], ("items", "seq"), scatter_dimension=0, tiled=True),
            lax.psum_scatter(grads[3], ("items", "seq"), scatter_dimension=0, tiled=True),
            lax.psum_scatter(grads[4], ("items", "seq"), scatter_dimension=0, tiled=True),
            lax.psum_scatter(grads[5], ("items", "seq"), scatter_dimension=0, tiled=True),
            lax.psum_scatter(grads[6], ("items", "seq"), scatter_dimension=0, tiled=True),
            lax.psum_scatter(grads[7], ("items", "seq"), scatter_dimension=0, tiled=True),
            lax.psum_scatter(grads[8], ("items", "seq"), scatter_dimension=0, tiled=True),
            lax.psum_scatter(grads[9], ("items", "seq"), scatter_dimension=0, tiled=True),
            lax.psum_scatter(grads[10], ("items", "seq"), scatter_dimension=0, tiled=True),
            lax.psum_scatter(grads[11], ("items", "seq"), scatter_dimension=0, tiled=True),
            lax.psum_scatter(grads[12], ("items", "seq"), scatter_dimension=0, tiled=True),
        )
        totals = (
            shares
            if totals is None
            else tuple((earlier + later for earlier, later in zip(totals, shares)))
        )
    item_count = tokens.shape[0]
    layer_out = jnp.concatenate(outputs_list, axis=0).reshape(
        item_count, 1, block_rows, model_width
    )
    tokens_grad = jnp.concatenate(gradients_list, axis=0).reshape(
        item_count, 1, block_rows, model_width
    )
    return (
        layer_out,
        tokens_grad,
        totals[0],
        totals[1],
        totals[2],
        totals[3],
        totals[4],
        totals[5],
        totals[6],
        totals[7],
        totals[8],
        totals[9],
        totals[10],
        totals[11],
        totals[12],
    )


Z_SIZE = 4
F32 = jnp.float32
BF16 = jnp.bfloat16
MESH = pl.DeviceIdType.MESH
CHUNK = 24
W_I, W_O, W_E, W_R, W_Q, VEC = TENSORS = range(6)
GATHER_X = (3, 3, 3, 3, None, 2)
D_IA, D_IB, D_O, D_EA, D_EB, D_R, D_Q, D_V = SUMS = range(8)
REDUCE_X = (3, 3, 3, 3, 3, 2, None, 2)
SEMS = 20
VECTORS = 8


def nn(left, right):
    return lax.dot_general(left, right, (((1,), (0,)), ((), ())), preferred_element_type=F32)


def nt(left, right):
    return lax.dot_general(left, right, (((1,), (1,)), ((), ())), preferred_element_type=F32)


def tn(left, right):
    return lax.dot_general(left, right, (((0,), (0,)), ((), ())), preferred_element_type=F32)


def lanes(start, size):
    return pl.ds(pl.multiple_of(start, 128), size)


def rows_at(start, size):
    return pl.ds(pl.multiple_of(start, 128), size)


class Place:
    def __init__(self):
        item = lax.axis_index("items")
        self.y = lax.axis_index("seq")
        self.z = item // 4
        self.x = (item // 2) % 2
        self.c = item % 2

    def device(self, z, x, c, y):
        return ((z * 2 + x) * 2 + c, y)

    def to_z(self, k):
        return self.device(lax.rem(self.z + k, Z_SIZE), self.x, self.c, self.y)

    @property
    def to_x(self):
        return self.device(self.z, 1 - self.x, self.c, self.y)

    @property
    def to_y(self):
        return self.device(self.z, self.x, self.c, 1 - self.y)

    @property
    def to_c(self):
        return self.device(self.z, self.x, 1 - self.c, self.y)

    def column(self, flip_x, flip_c, flip_y):
        x = 1 - self.x if flip_x else self.x
        c = 1 - self.c if flip_c else self.c
        y = 1 - self.y if flip_y else self.y
        return x * 4 + c * 2 + y

    def quarter(self, flip_x, flip_y):
        x = 1 - self.x if flip_x else self.x
        y = 1 - self.y if flip_y else self.y
        return x * 2 + y


def remote(src, dst, send, recv, device):
    return pltpu.make_async_remote_copy(
        src_ref=src, dst_ref=dst, send_sem=send, recv_sem=recv, device_id=device, device_id_type=MESH
    )


class Gather:
    def __init__(self, here, buf, send, recv, share):
        self.here, self.buf, self.send, self.recv = here, buf, send, recv
        self.share = share
        self.open = []

    def copy(self, slot, index, device):
        ref = self.buf.at[slot]
        return remote(ref, ref, self.send.at[index], self.recv.at[index], device)

    def push(self, slot, index, device):
        made = self.copy(slot, index, device)
        made.start()
        self.open.append(made)

    def pull(self, slot, index):
        self.copy(slot, index, self.here.to_x).wait_recv()

    def behind(self, k):
        return lax.rem(self.here.z + (Z_SIZE - k), Z_SIZE)

    def own(self):
        return (self.here.z, self.here.column(0, 0, 0))

    def begin_z(self):
        for k in (1, 3, 2):
            self.push(self.own(), k - 1, self.here.to_z(k))

    def begin_x(self):
        self.push(self.own(), 3, self.here.to_x)

    def begin_y(self):
        self.push(self.own(), 7, self.here.to_y)

    def pass_on(self, k):
        here = self.here
        slot = (self.behind(k), here.column(0, 0, 0))
        self.pull(slot, k - 1)
        self.push(slot, 3 + k, here.to_x)
        self.push(slot, 7 + k, here.to_y)

    def own_to_core(self):
        here = self.here
        self.push((slice(None), here.column(0, 0, 0)), 15, here.to_c)

    def relay(self, k):
        here = self.here
        from_x = (self.behind(k), here.column(1, 0, 0))
        from_y = (self.behind(k), here.column(0, 0, 1))
        self.pull(from_x, 3 + k)
        self.pull(from_y, 7 + k)
        if k < self.share:
            self.push(from_y, 11 + k, here.to_x)
        else:
            self.push(from_x, 11 + k, here.to_y)

    def sides_to_core(self):
        here = self.here
        self.push((slice(None), here.column(1, 0, 0)), 16, here.to_c)
        self.push((slice(None), here.column(0, 0, 1)), 17, here.to_c)

    def corner(self):
        here = self.here
        for k in range(4):
            self.pull((self.behind(k), here.column(1, 0, 1)), 11 + k)
        self.push((slice(None), here.column(1, 0, 1)), 18, here.to_c)

    def from_core(self):
        here = self.here
        for index, (fx, fy) in ((15, (0, 0)), (16, (1, 0)), (17, (0, 1)), (18, (1, 1))):
            self.pull((slice(None), here.column(fx, 1, fy)), index)

    def drain(self):
        for made in self.open:
            made.wait_send()
        self.open = []


class PlaneGather(Gather):
    def halves(self):
        wide = self.buf.shape[-1] // 2
        return slice(0, wide), slice(wide, 2 * wide)

    def begin_x(self):
        self.push(self.own(), 0, self.here.to_x)

    def begin_y(self):
        self.push(self.own(), 1, self.here.to_y)

    def along_z(self, column, first):
        for k in (1, 3, 2):
            self.push((self.here.z, column), first + k - 1, self.here.to_z(k))

    def own_along_z(self):
        self.along_z(self.here.column(0, 0, 0), 4)

    def relay(self):
        here = self.here
        left, right = self.halves()
        from_x, from_y = here.column(1, 0, 0), here.column(0, 0, 1)
        self.pull((here.z, from_x), 0)
        self.push((here.z, from_x, slice(None), right), 3, here.to_y)
        self.pull((here.z, from_y), 1)
        self.push((here.z, from_y, slice(None), left), 2, here.to_x)
        self.along_z(from_x, 7)
        self.along_z(from_y, 10)

    def corner(self):
        here = self.here
        left, right = self.halves()
        corner = here.column(1, 0, 1)
        self.pull((here.z, corner, slice(None), left), 2)
        self.pull((here.z, corner, slice(None), right), 3)
        self.along_z(corner, 13)

    def to_core(self, part):
        here = self.here
        flips = ((0, 0), (1, 0), (0, 1), (1, 1))[part]
        column = here.column(flips[0], 0, flips[1])
        for k in (1, 3, 2):
            self.pull((self.behind(k), column), 4 + 3 * part + k - 1)
        self.push((slice(None), column), 16 + part, here.to_c)

    def from_core(self):
        here = self.here
        for index, (fx, fy) in enumerate(((0, 0), (1, 0), (0, 1), (1, 1))):
            self.pull((slice(None), here.column(fx, 1, fy)), 16 + index)


QUARTERS = ((1, 1), (1, 0), (0, 1), (0, 0))


class Reduce:
    def __init__(self, here, part, core, relay, sides, ends, send, recv, share):
        self.here, self.part, self.core, self.sides_in, self.ends = here, part, core, sides, ends
        self.share = share
        self.relay_in = relay
        self.send, self.recv = send, recv
        self.open = []

    def push(self, src, dst, index, device):
        made = remote(src, dst, self.send.at[index], self.recv.at[index], device)
        made.start()
        self.open.append(made)

    def pull(self, dst, index):
        remote(dst, dst, self.send.at[index], self.recv.at[index], self.here.to_x).wait_recv()

    def add(self, column, first, last, *others):
        part = self.part

        def one(z, carry):
            total = part[z, column].astype(F32)
            for ref, index in others:
                total = total + ref[z, index].astype(F32)
            part[z, column] = total.astype(part.dtype)
            return carry

        lax.fori_loop(first, last, one, 0)

    def core_send(self, spare=None):
        here = self.here
        if spare is not None:
            pl.semaphore_wait(spare, 1)
        for index, (fx, fy) in enumerate(QUARTERS):
            self.push(
                self.part.at[:, here.column(fx, 1, fy)],
                self.core.at[:, here.quarter(fx, fy)],
                index,
                here.to_c,
            )

    def core_add(self, index):
        here, share = self.here, self.share
        fx, fy = QUARTERS[index]
        quarter, column = here.quarter(fx, fy), here.column(fx, 0, fy)
        self.pull(self.core.at[:, quarter], index)
        self.add(column, 0, 4, (self.core, quarter))
        part = self.part
        if index == 0:
            self.push(part.at[:share, column], self.relay_in.at[:share], 4, here.to_x)
            self.push(part.at[share:, column], self.relay_in.at[share:], 5, here.to_y)
        if index == 1:
            self.push(part.at[:share, column], self.sides_in.at[:share, 0], 6, here.to_x)
        if index == 2:
            self.push(part.at[share:, column], self.sides_in.at[share:, 1], 8, here.to_y)

    def relay(self):
        here, part, share = self.here, self.part, self.share
        to_x, to_y = here.column(1, 0, 0), here.column(0, 0, 1)

        def pair(z, column):
            total = part[z, column].astype(F32) + self.relay_in[z].astype(F32)
            part[z, column] = total.astype(part.dtype)

        self.pull(self.relay_in.at[share:], 5)
        for z in range(share, 4):
            pair(z, to_x)
        self.push(part.at[share:, to_x], self.sides_in.at[share:, 0], 7, here.to_x)
        self.pull(self.relay_in.at[:share], 4)

        def one(z, carry):
            pair(z, to_y)
            return carry

        lax.fori_loop(0, share, one, 0)
        self.push(part.at[:share, to_y], self.sides_in.at[:share, 1], 9, here.to_y)

    def sides(self):
        here, share = self.here, self.share
        for index, where in ((6, (slice(0, share), 0)), (8, (slice(share, 4), 1)),
                             (7, (slice(share, 4), 0)), (9, (slice(0, share), 1))):
            self.pull(self.sides_in.at[where], index)
        own = here.column(0, 0, 0)
        self.add(own, 0, 4, (self.sides_in, 0), (self.sides_in, 1))
        for k in (1, 3, 2):
            away = lax.rem(here.z + k, Z_SIZE)
            self.push(self.part.at[away, own], self.ends.at[k - 1], 9 + k, here.to_z(k))

    def finish(self):
        here = self.here
        for k in (1, 3, 2):
            self.pull(self.ends.at[k - 1], 9 + k)
        total = self.part[here.z, here.column(0, 0, 0)].astype(F32)
        for k in range(3):
            total = total + self.ends[k].astype(F32)
        return total

    def drain(self):
        for made in self.open:
            made.wait_send()
        self.open = []


class PlaneReduce(Reduce):
    def core_add(self, index):
        here = self.here
        fx, fy = QUARTERS[index]
        quarter, column = here.quarter(fx, fy), here.column(fx, 0, fy)
        self.pull(self.core.at[:, quarter], index)
        self.add(column, 0, 4, (self.core, quarter))
        for k in (1, 3, 2):
            away = lax.rem(here.z + k, Z_SIZE)
            self.push(
                self.part.at[away, column], self.ends.at[k - 1, index], 4 + 3 * index + k - 1, here.to_z(k)
            )

    def relay(self):
        here, part, z = self.here, self.part, self.here.z
        wide = part.shape[-1] // 2
        for index, (fx, fy) in enumerate(QUARTERS):
            column = here.column(fx, 0, fy)
            for k in (1, 3, 2):
                self.pull(self.ends.at[k - 1, index], 4 + 3 * index + k - 1)
            total = part[z, column].astype(F32)
            for k in range(3):
                total = total + self.ends[k, index].astype(F32)
            part[z, column] = total.astype(part.dtype)
            if index == 0:
                src, dst = part.at[z, column], self.relay_in
                self.push(src.at[:, :wide], dst.at[:, :wide], 16, here.to_x)
                self.push(src.at[:, wide:], dst.at[:, wide:], 17, here.to_y)

    def sides(self):
        here, part, z = self.here, self.part, self.here.z
        wide = part.shape[-1] // 2
        for index, cols, fx, fy, to in (
            (17, slice(wide, 2 * wide), 1, 0, here.to_x), (16, slice(0, wide), 0, 1, here.to_y)
        ):
            column = here.column(fx, 0, fy)
            self.pull(self.relay_in.at[:, cols], index)
            total = part[z, column, :, cols].astype(F32) + self.relay_in[:, cols].astype(F32)
            part[z, column, :, cols] = total.astype(part.dtype)
            self.push(part.at[z, column], self.sides_in.at[fy], 18 + fy, to)

    def finish(self):
        here = self.here
        total = self.part[here.z, here.column(0, 0, 0)].astype(F32)
        for index in range(2):
            self.pull(self.sides_in.at[index], 18 + index)
            total = total + self.sides_in[index].astype(F32)
        return total


def normalise(rows_in):
    centre = rows_in - jnp.mean(rows_in, axis=-1, keepdims=True)
    spread = jnp.mean(centre * centre, axis=-1, keepdims=True)
    inverse = lax.rsqrt(spread + EPSILON)
    return centre * inverse, inverse


def normalise_back(grad, unit, inverse):
    return inverse * (
        grad
        - jnp.mean(grad, axis=-1, keepdims=True)
        - unit * jnp.mean(grad * unit, axis=-1, keepdims=True)
    )


def spread_matrix(slot):
    lane = lax.broadcasted_iota(jnp.int32, (128, 768), 0)
    place = lax.broadcasted_iota(jnp.int32, (128, 768), 1)
    if slot is None:
        inside = lax.rem(place, 4 * CHUNK)
        wanted = 32 * (inside // CHUNK) + lax.rem(inside, CHUNK)
    else:
        wanted = 32 * slot + lax.rem(place, CHUNK)
    return jnp.where(lane == wanted, 1.0, 0.0).astype(BF16)


def owner_mask(each, first):
    device = lax.broadcasted_iota(jnp.int32, (32, 768), 0)
    place = lax.broadcasted_iota(jnp.int32, (32, 768), 1)
    return device == first + place // each


def collect(group, matrix, each, first):
    moved = nn(group.astype(BF16), matrix)
    return jnp.sum(jnp.where(owner_mask(each, first), moved, 0.0), axis=0, keepdims=True)


def deal(row, matrix, each, first):
    placed = jnp.where(owner_mask(each, first), row, 0.0)
    high = placed.astype(BF16)
    rest = placed - high.astype(F32)
    middle = rest.astype(BF16)
    low = (rest - middle.astype(F32)).astype(BF16)
    return nt(high, matrix) + nt(middle, matrix) + nt(low, matrix)


def one_hot(value):
    slot = lax.broadcasted_iota(jnp.int32, (16, 128), 0).astype(F32)
    ones = jnp.where(slot == value, 1.0, 0.0).astype(BF16)
    return jnp.concatenate([ones, ones, ones], axis=0)


def live_rows(count, block, number):
    slot = lax.broadcasted_iota(jnp.int32, (number, 1), 0)
    return slot < (count + 1 - block) // 2


def live_bias(count):
    slot = lax.broadcasted_iota(jnp.int32, (256, 1), 0)
    block = slot // 128
    return jnp.where(slot - 128 * block < (count + 1 - block) // 2, 0.0, -1e30)


def half_mask(head):
    return lax.broadcasted_iota(jnp.int32, (1, 128), 1) // HD == head


def fused_kernel(
    lengths, tokens, cotangent, seen, shard_I, shard_O, shard_E, shard_R, shard_V, table,
    layer_out, tokens_grad, grad_I, grad_O, grad_E, grad_R, grad_V, *refs,
):
    s = Store(refs)
    here = Place()
    z, x, c, y = here.z, here.x, here.c, here.y
    own = here.column(0, 0, 0)
    mine, other = pl.ds(2 * y, 2), pl.ds(2 * (1 - y), 2)
    sums = s.SUMS

    gather = [
        (PlaneGather if name == W_Q else Gather)(here, s.G[name], s.GS[name], s.GQ[name], GATHER_X[name])
        for name in TENSORS
    ]
    reduce = []
    for number, (name, cols, landing) in enumerate(PIECES):
        kind = PlaneReduce if name == W_Q else Reduce
        part, *bufs = [s.P[name], s.R1[name], s.R2[name], s.RZ[name]]
        core = s.RC[landing]
        if cols is not None:
            part, *bufs = [ref.at[(*(slice(None),) * (len(ref.shape) - 1), cols)] for ref in (part, *bufs)]
            core = core.at[:, :, :, : cols.stop - cols.start]
        reduce.append(kind(here, part, core, *bufs, s.RS[number], s.RQ[number], REDUCE_X[number]))

    def swap(src, dst, came, index):
        made = remote(src, dst, s.SWS.at[index], s.SWR.at[index], here.to_y)
        return made, remote(came, came, s.SWS.at[index], s.SWR.at[index], here.to_y)

    tok_out, tok_in = swap(tokens.at[other], s.TOK.at[:, y], s.TOK.at[:, 1 - y], 0)
    seen_out, seen_in = swap(s.AWAY, s.SEEN.at[:, y], s.SEEN.at[:, 1 - y], 1)
    cot_out, cot_in = swap(cotangent.at[other], s.INC.at[:, y], s.INC.at[:, 1 - y], 2)
    lay_out, lay_in = swap(s.TOK.at[:, 1 - y], layer_out.at[mine], layer_out.at[other], 3)
    grad_out, grad_in = swap(s.INC.at[:, 1 - y], s.TGR, s.TGR, 4)
    tok_copy = pltpu.make_async_copy(tokens.at[mine], s.TOK.at[:, y], s.LOC.at[0])
    cot_copy = pltpu.make_async_copy(cotangent.at[mine], s.INC.at[:, y], s.LOC.at[1])
    out_copy = pltpu.make_async_copy(s.TOK.at[:, y], layer_out.at[mine], s.LOC.at[2])
    near_copies = [
        pltpu.make_async_copy(
            s.ENT.at[rows_at(256 * it + 128 * y, 128)], tokens_grad.at[2 * y + it], s.LOC.at[3 + it]
        )
        for it in range(2)
    ]
    far_copies = [
        pltpu.make_async_copy(
            s.ENT.at[rows_at(256 * it + 128 * (1 - y), 128)], tokens_grad.at[2 * (1 - y) + it], s.LOC.at[5 + it]
        )
        for it in range(2)
    ]

    def vector(number):
        return s.ROWS[pl.ds(number, 1), :]

    def start():
        barrier = pltpu.get_barrier_semaphore()
        partners = [here.to_z(1), here.to_z(2), here.to_z(3), here.to_x, here.to_y, here.to_c]
        for device in partners:
            pl.semaphore_signal(barrier, inc=1, device_id=device, device_id_type=MESH)
        tok_copy.start()
        cot_copy.start()
        for name, shard in ((W_I, shard_I), (W_O, shard_O), (W_E, shard_E)):
            whole = shard[...].astype(F32)
            half = whole.shape[1] // 2
            unit = jnp.concatenate([whole[:, :half], whole[:, half:]], axis=0)
            s.G[name][z, own] = unit.astype(BF16)
        s.G[W_R][z, own] = shard_R[0:48, :]
        s.G[W_Q][z, own] = shard_R[48:96, :]
        s.G[VEC][z, own] = shard_V[...]
        for it in range(2):
            s.SEEN[it, y] = jnp.broadcast_to(seen[2 * y + it], (8, 128))
            s.AWAY[it] = jnp.broadcast_to(seen[2 * (1 - y) + it], (8, 128))
        pl.semaphore_wait(barrier, len(partners))

    def vectors():
        for number in range(VECTORS):
            group = s.G[VEC][:, :, number // 4, :].reshape(32, 128)
            s.ROWS[pl.ds(number, 1), :] = collect(group, spread_matrix(number % 4), CHUNK, 0)
        group = s.G[VEC][:, :, 2, :].reshape(32, 128)
        for part in range(4):
            cols = slice(768 * part, 768 * part + 768)
            s.EB[:, cols] = collect(group, spread_matrix(None), 4 * CHUNK, 8 * part)
        s.PB[:, 0:768] = vector(2)
        s.PB[:, 768:1536] = jnp.zeros((1, 768), F32)
        s.PB[:, 1536:2304] = vector(3)
        sums[...] = jnp.zeros_like(sums)
        s.EBG[...] = jnp.zeros_like(s.EBG)

    def first_norm():
        def one(block, carry):
            it, half = block // 2, block % 2
            rows = rows_at(128 * block, 128)
            patch = s.SEEN[it, half][0:1, :].astype(F32)
            frame = jnp.floor((patch + 0.5) * (1.0 / (GRID * GRID)))
            inside = patch - frame * (GRID * GRID)
            line = jnp.floor((inside + 0.5) * (1.0 / GRID))
            across = inside - line * GRID
            place = jnp.concatenate([tn(one_hot(v), table[...]) for v in (frame, line, across)], axis=1)
            entry = s.TOK[it, half].astype(F32) + place
            s.ENT[rows, :] = entry
            unit, _ = normalise(entry)
            normed = (unit * vector(0) + vector(1)).astype(BF16)
            s.XB[rows, :] = normed
            s.NRMT[:, lanes(128 * block, 128)] = normed.T
            return carry

        lax.fori_loop(0, 4, one, 0)

    def spread_rows(name, target):
        buf = s.G[name]
        half = target.shape[1] // 2

        def one(i, carry):
            zz, pair = i // 4, 2 * (i % 4)
            even = buf[zz, pair].astype(F32)
            odd = buf[zz, pair + 1].astype(F32)
            rows = pl.ds(pl.multiple_of(48 * i, 16), 48)
            target[rows, :half] = jnp.concatenate([even[:24], odd[:24]], axis=0).astype(BF16)
            target[rows, half:] = jnp.concatenate([even[24:], odd[24:]], axis=0).astype(BF16)
            return carry

        lax.fori_loop(0, 16, one, 0)

    def project():
        def one(n, carry):
            cols = lanes(256 * n, 256)
            s.PRJ[:, cols] = (nn(s.XB[...], s.WI[:, cols]) + s.PB[:, cols]).astype(BF16)
            return carry

        lax.fori_loop(0, 9, one, 0)

    def attend(first, last):
        def one(step, carry):
            it, pair = step // 6, step % 6
            rows = rows_at(256 * it, 256)
            cols = lanes(128 * pair, 128)
            q = s.PRJ[rows, cols]
            k = s.PRJ[rows, lanes(768 + 128 * pair, 128)]
            v = s.PRJ[rows, lanes(1536 + 128 * pair, 128)]
            bias = live_bias(lengths[2 * y + it])
            total = jnp.zeros((128, 256), F32)
            for head in range(2):
                mask = half_mask(head)
                scores = nt(jnp.where(mask, k, 0), q) * SCORE_SCALE + bias
                exponent = jnp.exp(scores - jnp.max(scores, axis=0, keepdims=True))
                attention = exponent * (1.0 / jnp.sum(exponent, axis=0, keepdims=True))
                low = attention.astype(BF16)
                s.ATN[2 * step + head] = low
                total = total + tn(jnp.where(mask, v, 0), low)
            s.ATTT[cols, rows] = total.astype(BF16)
            s.XB[rows, cols] = total.T.astype(BF16)
            return carry

        lax.fori_loop(first, last, one, 0)

    def second_norm():
        def one(it, carry):
            rows = rows_at(256 * it, 256)
            middle = s.ENT[rows, :] + nn(s.XB[rows, :], s.WO[...]) + vector(4)
            s.MID[rows, :] = middle
            unit, _ = normalise(middle)
            second = (unit * vector(5) + vector(6)).astype(BF16)
            s.XB[rows, :] = second
            s.SECT[:, rows] = second.T
            return carry

        lax.fori_loop(0, 2, one, 0)

    def expand(first, last):
        def one(step, carry):
            n, it = step // 2, step % 2
            cols = lanes(256 * n, 256)
            rows = rows_at(256 * it, 256)
            expanded = nn(s.XB[rows, :], s.WE[:, cols]) + s.EB[:, cols]
            normal = 0.5 * (1.0 + lax.erf(expanded * 0.7071067811865476))
            density = jnp.exp(-0.5 * expanded * expanded) * 0.3989422804014327
            s.ACT[rows, cols] = (expanded * normal).astype(BF16)
            s.GP[rows, cols] = (normal + expanded * density).astype(BF16)
            return carry

        lax.fori_loop(first, last, one, 0)

    def take_in():
        def one(block, carry):
            it, half = block // 2, block % 2
            live = live_rows(lengths[2 * y + it], half, 128)
            incoming = jnp.where(live, s.INC[it, half].astype(F32), 0.0)
            s.INC[it, half] = incoming.astype(BF16)
            sums[7:8, :] += jnp.sum(incoming, axis=0, keepdims=True)
            return carry

        lax.fori_loop(0, 4, one, 0)

    def reduce_weight_grad():
        def one(f, carry):
            zz, xx = f // 2, f % 2
            moved = s.ACT[:, lanes(384 * f, 384)].T
            part = nn(moved, s.INC[...].reshape(512, 768))
            units = part.reshape(4, 96, 768).astype(BF16)
            s.P[W_R][zz, pl.ds(4 * xx, 4)] = units[:, :48]
            s.P[W_Q][zz, pl.ds(4 * xx, 4)] = units[:, 48:]
            return carry

        lax.fori_loop(0, 8, one, 0)

    def reduce_rows(zz):
        return jnp.concatenate([s.G[W_R][zz], s.G[W_Q][zz]], axis=1).reshape(768, 768)

    def expanded_grad(first, last):
        def one(step, carry):
            zz, it = step // 2, step % 2
            rows = rows_at(256 * it, 256)
            cols = lanes(768 * zz, 768)
            incoming = s.INC[it].reshape(256, 768)
            grad = (nt(incoming, reduce_rows(zz)) * s.GP[rows, cols].astype(F32)).astype(BF16)
            s.GP[rows, cols] = grad
            s.EBG[:, cols] += jnp.sum(grad.astype(F32), axis=0, keepdims=True)
            return carry

        lax.fori_loop(first, last, one, 0)

    def weight_grad(name, moved, grad, first, last):
        part, wide = s.P[name], 384
        half = UNITS[name][1]

        def one(step, carry):
            n, m = step // 2, step % 2
            left = grad[:, lanes(wide * n, wide)]
            right = grad[:, lanes(half + wide * n, wide)]
            block = nn(moved[rows_at(384 * m, 384), :], jnp.concatenate([left, right], axis=1))
            for j in range(8):
                for side in range(2):
                    rows = slice(48 * j + 24 * side, 48 * j + 24 * side + 24)
                    unit = jnp.concatenate([block[rows, :wide], block[rows, wide:]], axis=0)
                    part[2 * m + j // 4, 2 * (j % 4) + side, :, lanes(wide * n, wide)] = unit.astype(BF16)
            return carry

        if first == 0:
            gather[name].drain()
        lax.fori_loop(2 * first, 2 * last, one, 0)

    def finish_rows():
        def one(it, carry):
            rows = rows_at(256 * it, 256)
            out = s.MID[rows, :] + vector(7)
            for zz in range(4):
                out = out + nn(s.ACT[rows, 768 * zz : 768 * zz + 768], reduce_rows(zz))
            for half in range(2):
                live = live_rows(lengths[2 * y + it], half, 128)
                s.TOK[it, half] = jnp.where(live, out[128 * half : 128 * half + 128], 0.0).astype(BF16)
            return carry

        tok_out.wait_send()
        lax.fori_loop(0, 2, one, 0)
        out_copy.start()

    def middle_back():
        def one(it, carry):
            rows = rows_at(256 * it, 256)
            grad = nt(s.GP[rows, :], s.WE[...])
            unit, inverse = normalise(s.MID[rows, :])
            sums[5:6, :] += jnp.sum(grad * unit, axis=0, keepdims=True)
            sums[6:7, :] += jnp.sum(grad, axis=0, keepdims=True)
            incoming = s.INC[it].reshape(256, 768).astype(F32)
            middle_grad = incoming + normalise_back(grad * vector(5), unit, inverse)
            s.MID[rows, :] = middle_grad
            branch = middle_grad.astype(BF16)
            s.XB[rows, :] = branch
            sums[4:5, :] += jnp.sum(branch.astype(F32), axis=0, keepdims=True)
            return carry

        lax.fori_loop(0, 2, one, 0)

    def attended_back():
        def one(it, carry):
            rows = rows_at(256 * it, 256)
            s.XB[rows, :] = nt(s.XB[rows, :], s.WO[...]).astype(BF16)
            return carry

        lax.fori_loop(0, 2, one, 0)

    def attend_back(first, last):
        def one(step, carry):
            it, pair = step // 6, step % 6
            rows = rows_at(256 * it, 256)
            cols = lanes(128 * pair, 128)
            k_cols, v_cols = lanes(768 + 128 * pair, 128), lanes(1536 + 128 * pair, 128)
            q = s.PRJ[rows, cols]
            k = s.PRJ[rows, k_cols]
            v = s.PRJ[rows, v_cols]
            grad = s.XB[rows, cols]
            query_grad = jnp.zeros((128, 256), F32)
            key_grad = jnp.zeros((256, 128), F32)
            value_grad = jnp.zeros((256, 128), F32)
            for head in range(2):
                mask = half_mask(head)
                mine_grad = jnp.where(mask, grad, 0)
                weight_back = nt(v, mine_grad)
                low = s.ATN[2 * step + head]
                attention = low.astype(F32)
                inner = jnp.sum(attention * weight_back, axis=0, keepdims=True)
                scores_grad = (attention * (weight_back - inner)).astype(BF16)
                query_grad = query_grad + tn(jnp.where(mask, k, 0), scores_grad)
                key_grad = key_grad + nn(scores_grad, jnp.where(mask, q, 0))
                value_grad = value_grad + nn(low, mine_grad)
            query_low = (query_grad * SCORE_SCALE).T.astype(BF16)
            value_low = value_grad.astype(BF16)
            s.PRJ[rows, cols] = query_low
            s.PRJ[rows, k_cols] = (key_grad * SCORE_SCALE).astype(BF16)
            s.PRJ[rows, v_cols] = value_low
            sums[2:3, cols] += jnp.sum(query_low.astype(F32), axis=0, keepdims=True)
            sums[3:4, cols] += jnp.sum(value_low.astype(F32), axis=0, keepdims=True)
            return carry

        lax.fori_loop(first, last, one, 0)

    def entry_back(half):
        rows = [rows_at(256 * it + 128 * half, 128) for it in range(2)]

        def both(ref):
            return jnp.concatenate([ref[r, :] for r in rows], axis=0)

        grad = nt(both(s.PRJ), s.WI[...])
        unit, inverse = normalise(both(s.ENT))
        sums[0:1, :] += jnp.sum(grad * unit, axis=0, keepdims=True)
        sums[1:2, :] += jnp.sum(grad, axis=0, keepdims=True)
        return rows, both(s.MID) + normalise_back(grad * vector(0), unit, inverse)

    def entry_back_far():
        _, out = entry_back(1 - y)
        cot_out.wait_send()
        for it in range(2):
            s.INC[it, 1 - y] = out[128 * it : 128 * it + 128].astype(BF16)

    def entry_back_near():
        rows, out = entry_back(y)
        for it in range(2):
            s.ENT[rows[it], :] = out[128 * it : 128 * it + 128]
        for copy in near_copies:
            copy.start()

    def deal_sums():
        group = None
        for number in range(VECTORS):
            dealt = deal(sums[number : number + 1, :], spread_matrix(number % 4), CHUNK, 0)
            group = dealt if number % 4 == 0 else group + dealt
            if number % 4 == 3:
                s.P[VEC][:, :, number // 4, :] = group.reshape(4, 8, 128)
        group = jnp.zeros((32, 128), F32)
        for part in range(4):
            row = s.EBG[:, 768 * part : 768 * part + 768]
            group = group + deal(row, spread_matrix(None), 4 * CHUNK, 8 * part)
        s.P[VEC][:, :, 2, :] = group.reshape(4, 8, 128)
        for row in range(3, 8):
            s.P[VEC][:, :, row, :] = jnp.zeros((4, 8, 128), F32)

    def give_spare(index):
        pl.semaphore_signal(s.SPARE.at[index], inc=1, device_id=here.to_c, device_id_type=MESH)

    def place_grad(number, ref):
        cols = PIECES[number][1]
        half = ref.shape[1] // 2
        if cols is None:
            cols = slice(0, half)
        total = reduce[number].finish()
        ref[:, cols] = total[:24]
        ref[:, half + cols.start : half + cols.stop] = total[24:]

    def take_grad():
        grad_in.wait_recv()
        for it in range(2):
            s.ENT[rows_at(256 * it + 128 * (1 - y), 128), :] = s.TGR[it].astype(F32)
        for copy in far_copies:
            copy.start()

    def end():
        for made in (seen_out, lay_out, grad_out):
            made.wait_send()
        out_copy.wait()
        for copy in near_copies + far_copies:
            copy.wait()
        for one in (*gather, *reduce):
            one.drain()

    start()
    gather[W_O].begin_x()
    gather[W_E].begin_y()
    gather[VEC].begin_x()
    gather[W_Q].begin_y()
    gather[W_O].begin_y()
    gather[W_O].begin_z()
    gather[VEC].begin_y()
    gather[W_I].begin_x()
    gather[W_E].begin_x()
    gather[VEC].begin_z()
    gather[W_I].begin_z()
    gather[VEC].pass_on(3)
    gather[W_O].pass_on(2)
    gather[W_Q].begin_x()
    gather[W_I].begin_y()
    gather[W_O].pass_on(1)
    gather[W_O].relay(2)
    gather[VEC].pass_on(1)
    gather[VEC].pass_on(2)
    gather[W_E].begin_z()
    gather[W_O].pass_on(3)
    gather[W_I].pass_on(1)
    gather[W_I].pass_on(3)
    gather[W_O].relay(3)
    gather[VEC].relay(3)
    gather[W_I].pass_on(2)
    gather[W_I].relay(3)
    gather[W_O].relay(0)
    gather[W_I].relay(1)
    gather[VEC].relay(2)
    gather[W_I].relay(0)
    gather[VEC].relay(1)
    gather[VEC].relay(0)
    seen_out.start()
    tok_out.start()
    gather[W_O].relay(1)
    gather[W_I].relay(2)
    gather[W_I].sides_to_core()
    gather[W_O].own_to_core()
    gather[VEC].sides_to_core()
    gather[VEC].own_to_core()
    gather[W_Q].own_along_z()
    gather[W_E].pass_on(3)
    gather[W_O].sides_to_core()
    gather[W_R].begin_z()
    gather[VEC].corner()
    seen_in.wait_recv()
    gather[W_O].corner()
    gather[W_O].from_core()
    gather[W_I].own_to_core()
    gather[W_E].pass_on(2)
    gather[VEC].from_core()
    gather[W_E].pass_on(1)
    gather[W_I].corner()
    gather[W_I].from_core()
    gather[W_E].relay(0)
    tok_copy.wait()
    tok_in.wait_recv()
    gather[W_Q].relay()
    vectors()
    first_norm()
    gather[W_E].relay(3)
    spread_rows(W_I, s.WI)
    project()
    gather[W_E].relay(2)
    spread_rows(W_O, s.WO)
    attend(0, 6)
    gather[W_E].relay(1)
    gather[W_R].begin_y()
    gather[W_R].begin_x()
    gather[W_E].own_to_core()
    gather[W_R].pass_on(3)
    gather[W_R].pass_on(1)
    gather[W_Q].corner()
    gather[W_E].sides_to_core()
    gather[W_Q].to_core(0)
    gather[W_R].pass_on(2)
    cot_out.start()
    attend(6, 12)
    gather[W_E].corner()
    gather[W_R].own_to_core()
    second_norm()
    gather[W_R].relay(0)
    gather[W_Q].to_core(1)
    gather[W_E].from_core()
    spread_rows(W_E, s.WE)
    expand(0, 12)
    gather[W_R].relay(3)
    gather[W_R].relay(2)
    gather[W_R].relay(1)
    expand(12, 24)
    gather[W_Q].to_core(3)
    cot_copy.wait()
    cot_in.wait_recv()
    gather[W_R].sides_to_core()
    gather[W_Q].to_core(2)
    take_in()
    gather[W_R].corner()
    reduce_weight_grad()
    gather[W_R].from_core()
    gather[W_Q].from_core()
    reduce[D_R].core_send()
    expanded_grad(0, 4)
    reduce[D_R].core_add(0)
    reduce[D_Q].core_send()
    reduce[D_R].core_add(1)
    expanded_grad(4, 8)
    reduce[D_R].core_add(2)
    reduce[D_R].core_add(3)
    give_spare(0)
    reduce[D_Q].core_add(0)
    weight_grad(W_E, s.SECT, s.GP, 0, 2)
    reduce[D_R].relay()
    reduce[D_EA].core_send(s.SPARE.at[0])
    finish_rows()
    reduce[D_EA].core_add(0)
    reduce[D_Q].core_add(1)
    lay_out.start()
    weight_grad(W_E, s.SECT, s.GP, 2, 4)
    reduce[D_Q].core_add(2)
    reduce[D_EA].core_add(1)
    reduce[D_Q].core_add(3)
    give_spare(1)
    reduce[D_R].sides()
    reduce[D_EB].core_send(s.SPARE.at[1])
    middle_back()
    reduce[D_EB].core_add(0)
    weight_grad(W_O, s.ATTT, s.XB, 0, 1)
    reduce[D_EA].core_add(2)
    reduce[D_EA].relay()
    reduce[D_EB].core_add(1)
    reduce[D_EA].core_add(3)
    give_spare(2)
    reduce[D_EB].core_add(2)
    attended_back()
    reduce[D_O].core_send()
    attend_back(0, 6)
    reduce[D_O].core_add(0)
    attend_back(6, 12)
    reduce[D_O].core_add(1)
    reduce[D_EB].relay()
    weight_grad(W_I, s.NRMT, s.PRJ, 0, 2)
    reduce[D_IA].core_send(s.SPARE.at[2])
    weight_grad(W_I, s.NRMT, s.PRJ, 2, 3)
    reduce[D_IA].core_add(0)
    reduce[D_EB].core_add(3)
    give_spare(3)
    reduce[D_EB].sides()
    reduce[D_IB].core_send(s.SPARE.at[3])
    reduce[D_O].core_add(2)
    reduce[D_O].relay()
    reduce[D_O].core_add(3)
    reduce[D_EA].sides()
    reduce[D_Q].relay()
    reduce[D_IB].core_add(0)
    reduce[D_IA].core_add(1)
    reduce[D_IA].core_add(2)
    entry_back_far()
    reduce[D_IA].relay()
    entry_back_near()
    deal_sums()
    reduce[D_Q].sides()
    reduce[D_V].core_send()
    lay_in.wait_recv()
    reduce[D_O].sides()
    reduce[D_IA].core_add(3)
    reduce[D_V].core_add(0)
    reduce[D_IB].core_add(1)
    reduce[D_IB].core_add(2)
    reduce[D_IB].relay()
    reduce[D_IA].sides()
    reduce[D_V].core_add(1)
    reduce[D_V].core_add(2)
    place_grad(D_EA, grad_E)
    reduce[D_V].core_add(3)
    reduce[D_V].relay()
    reduce[D_IB].core_add(3)
    grad_out.start()
    grad_R[48:96, :] = reduce[D_Q].finish()
    reduce[D_V].sides()
    grad_R[0:48, :] = reduce[D_R].finish()
    place_grad(D_O, grad_O)
    place_grad(D_EB, grad_E)
    reduce[D_IB].sides()
    grad_V[...] = reduce[D_V].finish()
    place_grad(D_IA, grad_I)
    place_grad(D_IB, grad_I)
    take_grad()
    end()


UNITS = ((48, 1152), (48, 384), (48, 1536), (48, 768), (48, 768), (8, 128))


PIECES = (
    (W_I, slice(0, 768), 1),
    (W_I, slice(768, 1152), 2),
    (W_O, None, 0),
    (W_E, slice(0, 768), 1),
    (W_E, slice(768, 1536), 2),
    (W_R, None, 1),
    (W_Q, None, 2),
    (VEC, None, 3),
)


def scratch_list():
    dma, vmem = pltpu.SemaphoreType.DMA, pltpu.VMEM
    shapes = dict(
        SWS=dma((5,)),
        SWR=dma((5,)),
        LOC=dma((7,)),
        SPARE=pltpu.SemaphoreType.REGULAR((4,)),
        TOK=vmem((2, 2, 128, 768), BF16),
        INC=vmem((2, 2, 128, 768), BF16),
        SEEN=vmem((2, 2, 8, 128), jnp.int32),
        AWAY=vmem((2, 8, 128), jnp.int32),
        ROWS=vmem((8, 768), F32),
        EB=vmem((1, 3072), F32),
        PB=vmem((1, 2304), F32),
        SUMS=vmem((8, 768), F32),
        EBG=vmem((1, 3072), F32),
        WI=vmem((768, 2304), BF16),
        WO=vmem((768, 768), BF16),
        WE=vmem((768, 3072), BF16),
        ENT=vmem((512, 768), F32),
        MID=vmem((512, 768), F32),
        XB=vmem((512, 768), BF16),
        NRMT=vmem((768, 512), BF16),
        ATTT=vmem((768, 512), BF16),
        SECT=vmem((768, 512), BF16),
        PRJ=vmem((512, 2304), BF16),
        ATN=vmem((24, 256, 256), BF16),
        ACT=vmem((512, 3072), BF16),
        GP=vmem((512, 3072), BF16),
        TGR=vmem((2, 128, 768), BF16),
    )
    many = dict(G=[], GS=[], GQ=[], P=[], RC=[], R1=[], R2=[], RZ=[], RS=[], RQ=[])
    for name in TENSORS:
        kind = F32 if name == VEC else BF16
        unit = UNITS[name]
        plane = name == W_Q
        many["G"].append(vmem((4, 8, *unit), kind))
        many["GS"].append(dma((SEMS,)))
        many["GQ"].append(dma((SEMS,)))
        if name in (W_R, W_Q, VEC):
            many["P"].append(vmem((4, 8, *unit), kind))
        if name not in (W_I, W_E):
            many["RC"].append(vmem((4, 4, *unit), kind))
        many["R1"].append(vmem(unit if plane else (4, *unit), kind))
        many["R2"].append(vmem((2, *unit) if plane else (4, 2, *unit), kind))
        many["RZ"].append(vmem((3, 4, *unit) if plane else (3, *unit), kind))
    for _ in SUMS:
        many["RS"].append(dma((SEMS,)))
        many["RQ"].append(dma((SEMS,)))
    return shapes, many


class Store:
    def __init__(self, refs):
        shapes, many = scratch_list()
        refs = list(refs)
        for name in shapes:
            setattr(self, name, refs.pop(0))
        for name, listed in many.items():
            setattr(self, name, [refs.pop(0) for _ in listed])
        self.P = self.G[:3] + self.P


def position_table():
    step = np.arange(16, dtype=np.float64)[:, None]
    channel = np.arange(256)
    angle = step * np.power(10000.0, -(channel // 2) / 128.0)
    whole = np.where(channel % 2 == 0, np.sin(angle), np.cos(angle)).astype(np.float32)
    high = whole.astype(jnp.bfloat16)
    rest = whole - high.astype(np.float32)
    middle = rest.astype(jnp.bfloat16)
    low = (rest - middle.astype(np.float32)).astype(jnp.bfloat16)
    return np.concatenate([high, middle, low], axis=0)


def fused_body(
    tokens, visible, lengths, first_gain, first_shift, input_weight, query_bias, value_bias,
    output_weight, output_bias, second_gain, second_shift, expand_weight, expand_bias,
    reduce_weight, reduce_bias, cotangent,
):
    chunks = jnp.concatenate(
        [
            jnp.stack(
                [first_gain, first_shift, query_bias, value_bias, output_bias, second_gain, second_shift, reduce_bias]
            ),
            expand_bias.reshape(4, CHUNK),
        ],
        axis=0,
    ).astype(F32)
    shard_V = jnp.pad(chunks, ((0, 20), (0, 32 - CHUNK))).reshape(8, 128)
    hbm = pl.BlockSpec(memory_space=pl.ANY)
    vmem = pl.BlockSpec(memory_space=pltpu.VMEM)
    smem = pl.BlockSpec(memory_space=pltpu.SMEM)
    shapes, many = scratch_list()
    results = [
        jax.ShapeDtypeStruct((4, 128, 768), BF16),
        jax.ShapeDtypeStruct((4, 128, 768), F32),
        jax.ShapeDtypeStruct(input_weight.shape, F32),
        jax.ShapeDtypeStruct(output_weight.shape, F32),
        jax.ShapeDtypeStruct(expand_weight.shape, F32),
        jax.ShapeDtypeStruct(reduce_weight.shape, F32),
        jax.ShapeDtypeStruct((8, 128), F32),
    ]
    layer_out, tokens_grad, grad_I, grad_O, grad_E, grad_R, grad_V = pl.pallas_call(
        fused_kernel,
        name="layer",
        out_shape=results,
        in_specs=[smem, hbm, hbm, vmem, vmem, vmem, vmem, vmem, vmem, vmem],
        out_specs=[hbm, hbm, vmem, vmem, vmem, vmem, vmem],
        scratch_shapes=[*shapes.values(), *(shape for listed in many.values() for shape in listed)],
        compiler_params=pltpu.CompilerParams(
            collective_id=0, has_side_effects=True, vmem_limit_bytes=VMEM_BYTES
        ),
    )(
        lengths, tokens[:, 0], cotangent[:, 0], visible, input_weight, output_weight, expand_weight,
        reduce_weight, shard_V, jnp.asarray(position_table()),
    )
    dealt = grad_V.reshape(32, 32)[:12, :CHUNK]
    return (
        layer_out[:, None], tokens_grad[:, None], dealt[0], dealt[1], grad_I, dealt[2], dealt[3], grad_O,
        dealt[4], dealt[5], dealt[6], grad_E, dealt[8:12].reshape(4 * CHUNK), grad_R, dealt[7],
    )


VMEM_BYTES = 67000000


def solution(mesh):
    in_specs = (
        P("items", "seq", None, None),
        P("items", "seq", None),
        P("items"),
        P(("items", "seq")),
        P(("items", "seq")),
        P(("items", "seq"), None),
        P(("items", "seq")),
        P(("items", "seq")),
        P(("items", "seq"), None),
        P(("items", "seq")),
        P(("items", "seq")),
        P(("items", "seq")),
        P(("items", "seq"), None),
        P(("items", "seq")),
        P(("items", "seq"), None),
        P(("items", "seq")),
        P("items", "seq", None, None),
    )
    out_specs = (
        P("items", "seq", None, None),
        P("items", "seq", None, None),
        P(("items", "seq")),
        P(("items", "seq")),
        P(("items", "seq"), None),
        P(("items", "seq")),
        P(("items", "seq")),
        P(("items", "seq"), None),
        P(("items", "seq")),
        P(("items", "seq")),
        P(("items", "seq")),
        P(("items", "seq"), None),
        P(("items", "seq")),
        P(("items", "seq"), None),
        P(("items", "seq")),
    )
    sizes = (mesh.shape["items"], mesh.shape["seq"])
    chosen = fused_body if sizes == (Z_SIZE * 4, 2) else general_body
    return jax.shard_map(chosen, mesh=mesh, in_specs=in_specs, out_specs=out_specs, check_vma=False)
```

```python
import functools

import jax
import jax.numpy as jnp
import numpy as np
from jax import lax
from jax.experimental import pallas as pl
from jax.experimental.pallas import tpu as pltpu
from jax.sharding import PartitionSpec as P

HD = 64
GRID = 14
MICRO = 2
ITEMS_MB = 2


EPSILON = 1e-06
SCORE_SCALE = 0.125


def layer_norm(rows_in, gain, shift):
    centre = rows_in - jnp.mean(rows_in, axis=-1, keepdims=True)
    spread = jnp.mean(centre * centre, axis=-1, keepdims=True)
    return centre * lax.rsqrt(spread + EPSILON) * gain + shift


def gelu_exact(value_in):
    return jax.nn.gelu(value_in, approximate=False)


def positions(index, model_width):
    channel = jnp.arange(model_width)
    portion = 3 * channel // model_width
    frequency = jnp.power(10000.0, -(channel % 256 // 2).astype(jnp.float32) / 128.0)
    which_frame = index // (GRID * GRID)
    which_row = index % (GRID * GRID) // GRID
    which_column = index % GRID
    coordinate = jnp.where(
        portion == 0,
        which_frame[..., None],
        jnp.where(portion == 1, which_row[..., None], which_column[..., None]),
    )
    angle = coordinate.astype(jnp.float32) * frequency
    return jnp.where(channel % 2 == 0, jnp.sin(angle), jnp.cos(angle))


def contract_rows(left, right):
    return lax.dot_general(
        left, right, (((0,), (0,)), ((), ())), preferred_element_type=jnp.float32
    )


def against(left, right):
    return lax.dot_general(
        left, right, (((1,), (1,)), ((), ())), preferred_element_type=jnp.float32
    )


def row_masks(lengths, block_rows, block_number):
    counts = (lengths + 1 - block_number) // 2
    return jnp.arange(block_rows)[None, :] < counts[:, None]


def micro_batch(gathered, tokens, visible, lengths, cotangent, seq_place):
    (
        first_gain,
        first_shift,
        input_weight,
        query_bias,
        value_bias,
        output_weight,
        output_bias,
        second_gain,
        second_shift,
        expand_weight,
        expand_bias,
        reduce_weight,
        reduce_bias,
    ) = gathered
    item_count, block_rows, model_width = tokens.shape
    head_count = model_width // HD
    total_rows = item_count * block_rows
    (
        first_gain,
        first_shift,
        query_bias,
        value_bias,
        output_bias,
        second_gain,
        second_shift,
        expand_bias,
        reduce_bias,
    ) = (
        vector.astype(jnp.float32)
        for vector in (
            first_gain,
            first_shift,
            query_bias,
            value_bias,
            output_bias,
            second_gain,
            second_shift,
            expand_bias,
            reduce_bias,
        )
    )
    query_live = row_masks(lengths, block_rows, seq_place).reshape(total_rows, 1)
    key_live = jnp.concatenate(
        [row_masks(lengths, block_rows, 0), row_masks(lengths, block_rows, 1)], axis=1
    )
    key_mask = key_live[:, None, None, :]
    entry = tokens.reshape(total_rows, model_width).astype(jnp.float32) + positions(
        visible.reshape(total_rows), model_width
    )
    normed, first_pull = jax.vjp(layer_norm, entry, first_gain, first_shift)
    normed_low = normed.astype(jnp.bfloat16)
    joined_bias = jnp.concatenate([query_bias, jnp.zeros_like(query_bias), value_bias])
    projected = (
        jnp.dot(normed_low, input_weight, preferred_element_type=jnp.float32) + joined_bias
    ).astype(jnp.bfloat16)
    queries = projected[:, :model_width].reshape(item_count, block_rows, head_count, HD)
    keys_here = projected[:, model_width : 2 * model_width].reshape(
        item_count, block_rows, model_width
    )
    values_here = projected[:, 2 * model_width :].reshape(item_count, block_rows, model_width)
    keys_all, values_all = (
        lax.all_gather(keys_here, "seq", axis=1, tiled=True),
        lax.all_gather(values_here, "seq", axis=1, tiled=True),
    )
    keys_all = keys_all.reshape(item_count, 2 * block_rows, head_count, HD)
    values_all = values_all.reshape(item_count, 2 * block_rows, head_count, HD)
    scores = (
        jnp.einsum("cqhd,ckhd->chqk", queries, keys_all, preferred_element_type=jnp.float32)
        * SCORE_SCALE
    )
    scores = jnp.where(key_mask, scores, -1e30)
    row_max = jnp.max(scores, axis=-1, keepdims=True)
    exponent = jnp.exp(scores - row_max)
    row_total = jnp.sum(exponent, axis=-1, keepdims=True)
    attention_low = (exponent / row_total).astype(jnp.bfloat16)
    log_total = row_max + jnp.log(row_total)
    attended = jnp.einsum(
        "chqk,ckhd->cqhd", attention_low, values_all, preferred_element_type=jnp.float32
    )
    attended = attended.reshape(total_rows, model_width).astype(jnp.bfloat16)
    middle = (
        entry + jnp.dot(attended, output_weight, preferred_element_type=jnp.float32) + output_bias
    )
    second, second_pull = jax.vjp(layer_norm, middle, second_gain, second_shift)
    second_low = second.astype(jnp.bfloat16)
    expanded = jnp.dot(second_low, expand_weight, preferred_element_type=jnp.float32) + expand_bias
    activated, gelu_pull = jax.vjp(gelu_exact, expanded)
    activated_low = activated.astype(jnp.bfloat16)
    result = (
        middle
        + jnp.dot(activated_low, reduce_weight, preferred_element_type=jnp.float32)
        + reduce_bias
    )
    layer_out = jnp.where(query_live, result, 0.0).astype(jnp.bfloat16)
    incoming = jnp.where(
        query_live, cotangent.reshape(total_rows, model_width).astype(jnp.float32), 0.0
    )
    incoming_low = incoming.astype(jnp.bfloat16)
    reduce_weight_grad = contract_rows(activated_low, incoming_low)
    reduce_bias_grad = jnp.sum(incoming, axis=0)
    activated_grad = against(incoming_low, reduce_weight)
    expanded_grad = gelu_pull(activated_grad)[0].astype(jnp.bfloat16)
    expand_weight_grad = contract_rows(second_low, expanded_grad)
    expand_bias_grad = jnp.sum(expanded_grad.astype(jnp.float32), axis=0)
    second_grad = against(expanded_grad, expand_weight)
    middle_part, second_gain_grad, second_shift_grad = second_pull(second_grad)
    middle_grad = incoming + middle_part
    branch_grad = middle_grad.astype(jnp.bfloat16)
    output_weight_grad = contract_rows(attended, branch_grad)
    output_bias_grad = jnp.sum(branch_grad.astype(jnp.float32), axis=0)
    attended_grad = against(branch_grad, output_weight).astype(jnp.bfloat16)
    attended_grad = attended_grad.reshape(item_count, block_rows, head_count, HD)
    scores = (
        jnp.einsum("cqhd,ckhd->chqk", queries, keys_all, preferred_element_type=jnp.float32)
        * SCORE_SCALE
    )
    scores = jnp.where(key_mask, scores, -1e30)
    attention_full = jnp.exp(scores - log_total)
    attention_low = attention_full.astype(jnp.bfloat16)
    weight_grad = jnp.einsum(
        "cqhd,ckhd->chqk", attended_grad, values_all, preferred_element_type=jnp.float32
    )
    row_inner = jnp.sum(attention_full * weight_grad, axis=-1, keepdims=True)
    scores_grad = (attention_full * (weight_grad - row_inner)).astype(jnp.bfloat16)
    query_grad = (
        jnp.einsum("chqk,ckhd->cqhd", scores_grad, keys_all, preferred_element_type=jnp.float32)
        * SCORE_SCALE
    )
    key_terms = (
        jnp.einsum("chqk,cqhd->ckhd", scores_grad, queries, preferred_element_type=jnp.float32)
        * SCORE_SCALE
    )
    value_terms = jnp.einsum(
        "chqk,cqhd->ckhd", attention_low, attended_grad, preferred_element_type=jnp.float32
    )
    key_grad, value_grad = (
        lax.psum_scatter(
            key_terms.reshape(item_count, 2 * block_rows, model_width).astype(jnp.bfloat16),
            "seq",
            scatter_dimension=1,
            tiled=True,
        ).astype(jnp.float32),
        lax.psum_scatter(
            value_terms.reshape(item_count, 2 * block_rows, model_width).astype(jnp.bfloat16),
            "seq",
            scatter_dimension=1,
            tiled=True,
        ).astype(jnp.float32),
    )
    projected_grad = jnp.concatenate(
        [
            query_grad.reshape(total_rows, model_width),
            key_grad.reshape(total_rows, model_width),
            value_grad.reshape(total_rows, model_width),
        ],
        axis=1,
    ).astype(jnp.bfloat16)
    input_weight_grad = contract_rows(normed_low, projected_grad)
    projected_sums = jnp.sum(projected_grad.astype(jnp.float32), axis=0)
    query_bias_grad = projected_sums[:model_width]
    value_bias_grad = projected_sums[2 * model_width :]
    normed_grad = against(projected_grad, input_weight)
    entry_part, first_gain_grad, first_shift_grad = first_pull(normed_grad)
    tokens_grad = middle_grad + entry_part
    grads = (
        first_gain_grad,
        first_shift_grad,
        input_weight_grad,
        query_bias_grad,
        value_bias_grad,
        output_weight_grad,
        output_bias_grad,
        second_gain_grad,
        second_shift_grad,
        expand_weight_grad,
        expand_bias_grad,
        reduce_weight_grad,
        reduce_bias_grad,
    )
    return (layer_out, tokens_grad, grads)


def general_body(
    tokens,
    visible,
    lengths,
    first_gain,
    first_shift,
    input_weight,
    query_bias,
    value_bias,
    output_weight,
    output_bias,
    second_gain,
    second_shift,
    expand_weight,
    expand_bias,
    reduce_weight,
    reduce_bias,
    cotangent,
):
    shards = (
        first_gain,
        first_shift,
        input_weight,
        query_bias,
        value_bias,
        output_weight,
        output_bias,
        second_gain,
        second_shift,
        expand_weight,
        expand_bias,
        reduce_weight,
        reduce_bias,
    )
    seq_place = lax.axis_index("seq")
    block_rows = tokens.shape[2]
    model_width = tokens.shape[3]
    outputs_list = []
    gradients_list = []
    totals = None
    for micro_index in range(MICRO):
        first_item = micro_index * ITEMS_MB
        last_item = first_item + ITEMS_MB
        gathered = (
            lax.all_gather(shards[0], ("items", "seq"), axis=0, tiled=True),
            lax.all_gather(shards[1], ("items", "seq"), axis=0, tiled=True),
            lax.all_gather(shards[2], ("items", "seq"), axis=0, tiled=True),
            lax.all_gather(shards[3], ("items", "seq"), axis=0, tiled=True),
            lax.all_gather(shards[4], ("items", "seq"), axis=0, tiled=True),
            lax.all_gather(shards[5], ("items", "seq"), axis=0, tiled=True),
            lax.all_gather(shards[6], ("items", "seq"), axis=0, tiled=True),
            lax.all_gather(shards[7], ("items", "seq"), axis=0, tiled=True),
            lax.all_gather(shards[8], ("items", "seq"), axis=0, tiled=True),
            lax.all_gather(shards[9], ("items", "seq"), axis=0, tiled=True),
            lax.all_gather(shards[10], ("items", "seq"), axis=0, tiled=True),
            lax.all_gather(shards[11], ("items", "seq"), axis=0, tiled=True),
            lax.all_gather(shards[12], ("items", "seq"), axis=0, tiled=True),
        )
        layer_out, tokens_grad, grads = micro_batch(
            gathered,
            tokens[first_item:last_item, 0],
            visible[first_item:last_item, 0],
            lengths[first_item:last_item],
            cotangent[first_item:last_item, 0],
            seq_place,
        )
        outputs_list.append(layer_out)
        gradients_list.append(tokens_grad)
        shares = (
            lax.psum_scatter(grads[0], ("items", "seq"), scatter_dimension=0, tiled=True),
            lax.psum_scatter(grads[1], ("items", "seq"), scatter_dimension=0, tiled=True),
            lax.psum_scatter(grads[2], ("items", "seq"), scatter_dimension=0, tiled=True),
            lax.psum_scatter(grads[3], ("items", "seq"), scatter_dimension=0, tiled=True),
            lax.psum_scatter(grads[4], ("items", "seq"), scatter_dimension=0, tiled=True),
            lax.psum_scatter(grads[5], ("items", "seq"), scatter_dimension=0, tiled=True),
            lax.psum_scatter(grads[6], ("items", "seq"), scatter_dimension=0, tiled=True),
            lax.psum_scatter(grads[7], ("items", "seq"), scatter_dimension=0, tiled=True),
            lax.psum_scatter(grads[8], ("items", "seq"), scatter_dimension=0, tiled=True),
            lax.psum_scatter(grads[9], ("items", "seq"), scatter_dimension=0, tiled=True),
            lax.psum_scatter(grads[10], ("items", "seq"), scatter_dimension=0, tiled=True),
            lax.psum_scatter(grads[11], ("items", "seq"), scatter_dimension=0, tiled=True),
            lax.psum_scatter(grads[12], ("items", "seq"), scatter_dimension=0, tiled=True),
        )
        totals = (
            shares
            if totals is None
            else tuple((earlier + later for earlier, later in zip(totals, shares)))
        )
    item_count = tokens.shape[0]
    layer_out = jnp.concatenate(outputs_list, axis=0).reshape(
        item_count, 1, block_rows, model_width
    )
    tokens_grad = jnp.concatenate(gradients_list, axis=0).reshape(
        item_count, 1, block_rows, model_width
    )
    return (
        layer_out,
        tokens_grad,
        totals[0],
        totals[1],
        totals[2],
        totals[3],
        totals[4],
        totals[5],
        totals[6],
        totals[7],
        totals[8],
        totals[9],
        totals[10],
        totals[11],
        totals[12],
    )


Z_SIZE = 4
F32 = jnp.float32
BF16 = jnp.bfloat16
MESH = pl.DeviceIdType.MESH
CHUNK = 24
W_I, W_O, W_E, W_R, W_Q, VEC = TENSORS = range(6)
GATHER_X = (3, 3, 3, 3, None, 2)
D_IA, D_IB, D_O, D_EA, D_EB, D_R, D_Q, D_V = SUMS = range(8)
REDUCE_X = (3, 3, 3, 3, 3, 2, None, 2)
SEMS = 20
VECTORS = 8


def nn(left, right):
    return lax.dot_general(left, right, (((1,), (0,)), ((), ())), preferred_element_type=F32)


def nt(left, right):
    return lax.dot_general(left, right, (((1,), (1,)), ((), ())), preferred_element_type=F32)


def tn(left, right):
    return lax.dot_general(left, right, (((0,), (0,)), ((), ())), preferred_element_type=F32)


def lanes(start, size):
    return pl.ds(pl.multiple_of(start, 128), size)


def rows_at(start, size):
    return pl.ds(pl.multiple_of(start, 128), size)


class Place:
    def __init__(self):
        item = lax.axis_index("items")
        self.y = lax.axis_index("seq")
        self.z = item // 4
        self.x = (item // 2) % 2
        self.c = item % 2

    def device(self, z, x, c, y):
        return ((z * 2 + x) * 2 + c, y)

    def to_z(self, k):
        return self.device(lax.rem(self.z + k, Z_SIZE), self.x, self.c, self.y)

    @property
    def to_x(self):
        return self.device(self.z, 1 - self.x, self.c, self.y)

    @property
    def to_y(self):
        return self.device(self.z, self.x, self.c, 1 - self.y)

    @property
    def to_c(self):
        return self.device(self.z, self.x, 1 - self.c, self.y)

    def column(self, flip_x, flip_c, flip_y):
        x = 1 - self.x if flip_x else self.x
        c = 1 - self.c if flip_c else self.c
        y = 1 - self.y if flip_y else self.y
        return x * 4 + c * 2 + y

    def quarter(self, flip_x, flip_y):
        x = 1 - self.x if flip_x else self.x
        y = 1 - self.y if flip_y else self.y
        return x * 2 + y


def remote(src, dst, send, recv, device):
    return pltpu.make_async_remote_copy(
        src_ref=src, dst_ref=dst, send_sem=send, recv_sem=recv, device_id=device, device_id_type=MESH
    )


class Gather:
    def __init__(self, here, buf, send, recv, share):
        self.here, self.buf, self.send, self.recv = here, buf, send, recv
        self.share = share
        self.open = []

    def copy(self, slot, index, device):
        ref = self.buf.at[slot]
        return remote(ref, ref, self.send.at[index], self.recv.at[index], device)

    def push(self, slot, index, device):
        made = self.copy(slot, index, device)
        made.start()
        self.open.append(made)

    def pull(self, slot, index):
        self.copy(slot, index, self.here.to_x).wait_recv()

    def behind(self, k):
        return lax.rem(self.here.z + (Z_SIZE - k), Z_SIZE)

    def own(self):
        return (self.here.z, self.here.column(0, 0, 0))

    def begin_z(self):
        for k in (1, 3, 2):
            self.push(self.own(), k - 1, self.here.to_z(k))

    def begin_x(self):
        self.push(self.own(), 3, self.here.to_x)

    def begin_y(self):
        self.push(self.own(), 7, self.here.to_y)

    def pass_on(self, k):
        here = self.here
        slot = (self.behind(k), here.column(0, 0, 0))
        self.pull(slot, k - 1)
        self.push(slot, 3 + k, here.to_x)
        self.push(slot, 7 + k, here.to_y)

    def own_to_core(self):
        here = self.here
        self.push((slice(None), here.column(0, 0, 0)), 15, here.to_c)

    def relay(self, k):
        here = self.here
        from_x = (self.behind(k), here.column(1, 0, 0))
        from_y = (self.behind(k), here.column(0, 0, 1))
        self.pull(from_x, 3 + k)
        self.pull(from_y, 7 + k)
        if k < self.share:
            self.push(from_y, 11 + k, here.to_x)
        else:
            self.push(from_x, 11 + k, here.to_y)

    def sides_to_core(self):
        here = self.here
        self.push((slice(None), here.column(1, 0, 0)), 16, here.to_c)
        self.push((slice(None), here.column(0, 0, 1)), 17, here.to_c)

    def corner(self):
        here = self.here
        for k in range(4):
            self.pull((self.behind(k), here.column(1, 0, 1)), 11 + k)
        self.push((slice(None), here.column(1, 0, 1)), 18, here.to_c)

    def from_core(self):
        here = self.here
        for index, (fx, fy) in ((15, (0, 0)), (16, (1, 0)), (17, (0, 1)), (18, (1, 1))):
            self.pull((slice(None), here.column(fx, 1, fy)), index)

    def drain(self):
        for made in self.open:
            made.wait_send()
        self.open = []


class PlaneGather(Gather):
    def halves(self):
        wide = self.buf.shape[-1] // 2
        return slice(0, wide), slice(wide, 2 * wide)

    def begin_x(self):
        self.push(self.own(), 0, self.here.to_x)

    def begin_y(self):
        self.push(self.own(), 1, self.here.to_y)

    def along_z(self, column, first):
        for k in (1, 3, 2):
            self.push((self.here.z, column), first + k - 1, self.here.to_z(k))

    def own_along_z(self):
        self.along_z(self.here.column(0, 0, 0), 4)

    def relay(self):
        here = self.here
        left, right = self.halves()
        from_x, from_y = here.column(1, 0, 0), here.column(0, 0, 1)
        self.pull((here.z, from_x), 0)
        self.push((here.z, from_x, slice(None), right), 3, here.to_y)
        self.pull((here.z, from_y), 1)
        self.push((here.z, from_y, slice(None), left), 2, here.to_x)
        self.along_z(from_x, 7)
        self.along_z(from_y, 10)

    def corner(self):
        here = self.here
        left, right = self.halves()
        corner = here.column(1, 0, 1)
        self.pull((here.z, corner, slice(None), left), 2)
        self.pull((here.z, corner, slice(None), right), 3)
        self.along_z(corner, 13)

    def to_core(self, part):
        here = self.here
        flips = ((0, 0), (1, 0), (0, 1), (1, 1))[part]
        column = here.column(flips[0], 0, flips[1])
        for k in (1, 3, 2):
            self.pull((self.behind(k), column), 4 + 3 * part + k - 1)
        self.push((slice(None), column), 16 + part, here.to_c)

    def from_core(self):
        here = self.here
        for index, (fx, fy) in enumerate(((0, 0), (1, 0), (0, 1), (1, 1))):
            self.pull((slice(None), here.column(fx, 1, fy)), 16 + index)


QUARTERS = ((1, 1), (1, 0), (0, 1), (0, 0))


class Reduce:
    def __init__(self, here, part, core, relay, sides, ends, send, recv, share):
        self.here, self.part, self.core, self.sides_in, self.ends = here, part, core, sides, ends
        self.share = share
        self.relay_in = relay
        self.send, self.recv = send, recv
        self.open = []

    def push(self, src, dst, index, device):
        made = remote(src, dst, self.send.at[index], self.recv.at[index], device)
        made.start()
        self.open.append(made)

    def pull(self, dst, index):
        remote(dst, dst, self.send.at[index], self.recv.at[index], self.here.to_x).wait_recv()

    def add(self, column, first, last, *others):
        part = self.part

        def one(z, carry):
            total = part[z, column].astype(F32)
            for ref, index in others:
                total = total + ref[z, index].astype(F32)
            part[z, column] = total.astype(part.dtype)
            return carry

        lax.fori_loop(first, last, one, 0)

    def core_send(self, spare=None):
        here = self.here
        if spare is not None:
            pl.semaphore_wait(spare, 1)
        for index, (fx, fy) in enumerate(QUARTERS):
            self.push(
                self.part.at[:, here.column(fx, 1, fy)],
                self.core.at[:, here.quarter(fx, fy)],
                index,
                here.to_c,
            )

    def core_add(self, index):
        here, share = self.here, self.share
        fx, fy = QUARTERS[index]
        quarter, column = here.quarter(fx, fy), here.column(fx, 0, fy)
        self.pull(self.core.at[:, quarter], index)
        self.add(column, 0, 4, (self.core, quarter))
        part = self.part
        if index == 0:
            self.push(part.at[:share, column], self.relay_in.at[:share], 4, here.to_x)
            self.push(part.at[share:, column], self.relay_in.at[share:], 5, here.to_y)
        if index == 1:
            self.push(part.at[:share, column], self.sides_in.at[:share, 0], 6, here.to_x)
        if index == 2:
            self.push(part.at[share:, column], self.sides_in.at[share:, 1], 8, here.to_y)

    def relay(self):
        here, part, share = self.here, self.part, self.share
        to_x, to_y = here.column(1, 0, 0), here.column(0, 0, 1)

        def pair(z, column):
            total = part[z, column].astype(F32) + self.relay_in[z].astype(F32)
            part[z, column] = total.astype(part.dtype)

        self.pull(self.relay_in.at[share:], 5)
        for z in range(share, 4):
            pair(z, to_x)
        self.push(part.at[share:, to_x], self.sides_in.at[share:, 0], 7, here.to_x)
        self.pull(self.relay_in.at[:share], 4)

        def one(z, carry):
            pair(z, to_y)
            return carry

        lax.fori_loop(0, share, one, 0)
        self.push(part.at[:share, to_y], self.sides_in.at[:share, 1], 9, here.to_y)

    def sides(self):
        here, share = self.here, self.share
        for index, where in ((6, (slice(0, share), 0)), (8, (slice(share, 4), 1)),
                             (7, (slice(share, 4), 0)), (9, (slice(0, share), 1))):
            self.pull(self.sides_in.at[where], index)
        own = here.column(0, 0, 0)
        self.add(own, 0, 4, (self.sides_in, 0), (self.sides_in, 1))
        for k in (1, 3, 2):
            away = lax.rem(here.z + k, Z_SIZE)
            self.push(self.part.at[away, own], self.ends.at[k - 1], 9 + k, here.to_z(k))

    def finish(self):
        here = self.here
        for k in (1, 3, 2):
            self.pull(self.ends.at[k - 1], 9 + k)
        total = self.part[here.z, here.column(0, 0, 0)].astype(F32)
        for k in range(3):
            total = total + self.ends[k].astype(F32)
        return total

    def drain(self):
        for made in self.open:
            made.wait_send()
        self.open = []


class PlaneReduce(Reduce):
    def core_add(self, index):
        here = self.here
        fx, fy = QUARTERS[index]
        quarter, column = here.quarter(fx, fy), here.column(fx, 0, fy)
        self.pull(self.core.at[:, quarter], index)
        self.add(column, 0, 4, (self.core, quarter))
        for k in (1, 3, 2):
            away = lax.rem(here.z + k, Z_SIZE)
            self.push(
                self.part.at[away, column], self.ends.at[k - 1, index], 4 + 3 * index + k - 1, here.to_z(k)
            )

    def relay(self):
        here, part, z = self.here, self.part, self.here.z
        wide = part.shape[-1] // 2
        for index, (fx, fy) in enumerate(QUARTERS):
            column = here.column(fx, 0, fy)
            for k in (1, 3, 2):
                self.pull(self.ends.at[k - 1, index], 4 + 3 * index + k - 1)
            total = part[z, column].astype(F32)
            for k in range(3):
                total = total + self.ends[k, index].astype(F32)
            part[z, column] = total.astype(part.dtype)
            if index == 0:
                src, dst = part.at[z, column], self.relay_in
                self.push(src.at[:, :wide], dst.at[:, :wide], 16, here.to_x)
                self.push(src.at[:, wide:], dst.at[:, wide:], 17, here.to_y)

    def sides(self):
        here, part, z = self.here, self.part, self.here.z
        wide = part.shape[-1] // 2
        for index, cols, fx, fy, to in (
            (17, slice(wide, 2 * wide), 1, 0, here.to_x), (16, slice(0, wide), 0, 1, here.to_y)
        ):
            column = here.column(fx, 0, fy)
            self.pull(self.relay_in.at[:, cols], index)
            total = part[z, column, :, cols].astype(F32) + self.relay_in[:, cols].astype(F32)
            part[z, column, :, cols] = total.astype(part.dtype)
            self.push(part.at[z, column], self.sides_in.at[fy], 18 + fy, to)

    def finish(self):
        here = self.here
        total = self.part[here.z, here.column(0, 0, 0)].astype(F32)
        for index in range(2):
            self.pull(self.sides_in.at[index], 18 + index)
            total = total + self.sides_in[index].astype(F32)
        return total


def normalise(rows_in):
    centre = rows_in - jnp.mean(rows_in, axis=-1, keepdims=True)
    spread = jnp.mean(centre * centre, axis=-1, keepdims=True)
    inverse = lax.rsqrt(spread + EPSILON)
    return centre * inverse, inverse


def normalise_back(grad, unit, inverse):
    return inverse * (
        grad
        - jnp.mean(grad, axis=-1, keepdims=True)
        - unit * jnp.mean(grad * unit, axis=-1, keepdims=True)
    )


def spread_matrix(slot):
    lane = lax.broadcasted_iota(jnp.int32, (128, 768), 0)
    place = lax.broadcasted_iota(jnp.int32, (128, 768), 1)
    if slot is None:
        inside = lax.rem(place, 4 * CHUNK)
        wanted = 32 * (inside // CHUNK) + lax.rem(inside, CHUNK)
    else:
        wanted = 32 * slot + lax.rem(place, CHUNK)
    return jnp.where(lane == wanted, 1.0, 0.0).astype(BF16)


def owner_mask(each, first):
    device = lax.broadcasted_iota(jnp.int32, (32, 768), 0)
    place = lax.broadcasted_iota(jnp.int32, (32, 768), 1)
    return device == first + place // each


def collect(group, matrix, each, first):
    moved = nn(group.astype(BF16), matrix)
    return jnp.sum(jnp.where(owner_mask(each, first), moved, 0.0), axis=0, keepdims=True)


def deal(row, matrix, each, first):
    placed = jnp.where(owner_mask(each, first), row, 0.0)
    high = placed.astype(BF16)
    rest = placed - high.astype(F32)
    middle = rest.astype(BF16)
    low = (rest - middle.astype(F32)).astype(BF16)
    return nt(high, matrix) + nt(middle, matrix) + nt(low, matrix)


def one_hot(value):
    slot = lax.broadcasted_iota(jnp.int32, (16, 128), 0).astype(F32)
    ones = jnp.where(slot == value, 1.0, 0.0).astype(BF16)
    return jnp.concatenate([ones, ones, ones], axis=0)


def live_rows(count, block, number):
    slot = lax.broadcasted_iota(jnp.int32, (number, 1), 0)
    return slot < (count + 1 - block) // 2


def live_bias(count):
    slot = lax.broadcasted_iota(jnp.int32, (256, 1), 0)
    block = slot // 128
    return jnp.where(slot - 128 * block < (count + 1 - block) // 2, 0.0, -1e30)


def half_mask(head):
    return lax.broadcasted_iota(jnp.int32, (1, 128), 1) // HD == head


def fused_kernel(
    lengths, tokens, cotangent, seen, shard_I, shard_O, shard_E, shard_R, table,
    v0, v1, v2, v3, v4, v5, v6, v7, v8,
    layer_out, tokens_grad, grad_I, grad_O, grad_E, grad_R, grad_V, *refs,
):
    s = Store(refs)
    here = Place()
    z, x, c, y = here.z, here.x, here.c, here.y
    own = here.column(0, 0, 0)
    mine, other = pl.ds(2 * y, 2), pl.ds(2 * (1 - y), 2)
    sums = s.SUMS

    gather = [
        (PlaneGather if name == W_Q else Gather)(here, s.G[name], s.GS[name], s.GQ[name], GATHER_X[name])
        for name in TENSORS
    ]
    reduce = []
    for number, (name, cols, landing) in enumerate(PIECES):
        kind = PlaneReduce if name == W_Q else Reduce
        part, *bufs = [s.P[name], s.R1[name], s.R2[name], s.RZ[name]]
        core = s.RC[landing]
        if cols is not None:
            part, *bufs = [ref.at[(*(slice(None),) * (len(ref.shape) - 1), cols)] for ref in (part, *bufs)]
            core = core.at[:, :, :, : cols.stop - cols.start]
        reduce.append(kind(here, part, core, *bufs, s.RS[number], s.RQ[number], REDUCE_X[number]))

    def swap(src, dst, came, index):
        made = remote(src, dst, s.SWS.at[index], s.SWR.at[index], here.to_y)
        return made, remote(came, came, s.SWS.at[index], s.SWR.at[index], here.to_y)

    tok_out, tok_in = swap(tokens.at[other], s.TOK.at[:, y], s.TOK.at[:, 1 - y], 0)
    seen_out, seen_in = swap(s.AWAY, s.SEEN.at[:, y], s.SEEN.at[:, 1 - y], 1)
    cot_out, cot_in = swap(cotangent.at[other], s.INC.at[:, y], s.INC.at[:, 1 - y], 2)
    lay_out, lay_in = swap(s.TOK.at[:, 1 - y], layer_out.at[mine], layer_out.at[other], 3)
    grad_out, grad_in = swap(s.INC.at[:, 1 - y], s.TGR, s.TGR, 4)
    tok_copy = pltpu.make_async_copy(tokens.at[mine], s.TOK.at[:, y], s.LOC.at[0])
    cot_copy = pltpu.make_async_copy(cotangent.at[mine], s.INC.at[:, y], s.LOC.at[1])
    out_copy = pltpu.make_async_copy(s.TOK.at[:, y], layer_out.at[mine], s.LOC.at[2])
    near_copies = [
        pltpu.make_async_copy(
            s.ENT.at[rows_at(256 * it + 128 * y, 128)], tokens_grad.at[2 * y + it], s.LOC.at[3 + it]
        )
        for it in range(2)
    ]
    far_copies = [
        pltpu.make_async_copy(
            s.ENT.at[rows_at(256 * it + 128 * (1 - y), 128)], tokens_grad.at[2 * (1 - y) + it], s.LOC.at[5 + it]
        )
        for it in range(2)
    ]

    def vector(number):
        return s.ROWS[pl.ds(number, 1), :]

    def start():
        barrier = pltpu.get_barrier_semaphore()
        partners = [here.to_z(1), here.to_z(2), here.to_z(3), here.to_x, here.to_y, here.to_c]
        for device in partners:
            pl.semaphore_signal(barrier, inc=1, device_id=device, device_id_type=MESH)
        tok_copy.start()
        cot_copy.start()
        for name, shard in ((W_I, shard_I), (W_O, shard_O), (W_E, shard_E)):
            whole = shard[...].astype(F32)
            half = whole.shape[1] // 2
            unit = jnp.concatenate([whole[:, :half], whole[:, half:]], axis=0)
            s.G[name][z, own] = unit.astype(BF16)
        s.G[W_R][z, own] = shard_R[0:48, :]
        s.G[W_Q][z, own] = shard_R[48:96, :]
        s.STAGE[...] = jnp.zeros_like(s.STAGE)
        for number, ref in enumerate((v0, v1, v2, v3, v4, v5, v6, v7)):
            s.STAGE[number : number + 1, 0:CHUNK] = ref[...].astype(F32)
        s.STAGE[8:9, 0 : 4 * CHUNK] = v8[...].astype(F32)
        s.G[VEC][z, own] = jnp.zeros((8, 128), F32)
        for row in range(2):
            joined = s.STAGE[4 * row : 4 * row + 1, :]
            for slot in range(1, 4):
                joined = joined + pltpu.roll(s.STAGE[4 * row + slot : 4 * row + slot + 1, :], 32 * slot, 1)
            s.G[VEC][z, own, row : row + 1, :] = joined
        long_row = s.STAGE[8:9, :]
        lane = lax.broadcasted_iota(jnp.int32, (1, 128), 1)
        joined = jnp.zeros((1, 128), F32)
        for slot in range(4):
            moved = pltpu.roll(long_row, 8 * slot, 1) if slot else long_row
            inside = jnp.logical_and(lane >= 32 * slot, lane < 32 * slot + CHUNK)
            joined = jnp.where(inside, moved, joined)
        s.G[VEC][z, own, 2:3, :] = joined
        for it in range(2):
            s.SEEN[it, y] = jnp.broadcast_to(seen[2 * y + it], (8, 128))
            s.AWAY[it] = jnp.broadcast_to(seen[2 * (1 - y) + it], (8, 128))
        pl.semaphore_wait(barrier, len(partners))

    def vectors():
        for number in range(VECTORS):
            group = s.G[VEC][:, :, number // 4, :].reshape(32, 128)
            s.ROWS[pl.ds(number, 1), :] = collect(group, spread_matrix(number % 4), CHUNK, 0)
        group = s.G[VEC][:, :, 2, :].reshape(32, 128)
        for part in range(4):
            cols = slice(768 * part, 768 * part + 768)
            s.EB[:, cols] = collect(group, spread_matrix(None), 4 * CHUNK, 8 * part)
        s.PB[:, 0:768] = vector(2)
        s.PB[:, 768:1536] = jnp.zeros((1, 768), F32)
        s.PB[:, 1536:2304] = vector(3)
        sums[...] = jnp.zeros_like(sums)
        s.EBG[...] = jnp.zeros_like(s.EBG)

    def first_norm():
        def one(block, carry):
            it, half = block // 2, block % 2
            rows = rows_at(128 * block, 128)
            patch = s.SEEN[it, half][0:1, :].astype(F32)
            frame = jnp.floor((patch + 0.5) * (1.0 / (GRID * GRID)))
            inside = patch - frame * (GRID * GRID)
            line = jnp.floor((inside + 0.5) * (1.0 / GRID))
            across = inside - line * GRID
            place = jnp.concatenate([tn(one_hot(v), table[...]) for v in (frame, line, across)], axis=1)
            entry = s.TOK[it, half].astype(F32) + place
            s.ENT[rows, :] = entry
            unit, _ = normalise(entry)
            normed = (unit * vector(0) + vector(1)).astype(BF16)
            s.XB[rows, :] = normed
            s.NRMT[:, lanes(128 * block, 128)] = normed.T
            return carry

        lax.fori_loop(0, 4, one, 0, unroll=4)

    def spread_rows(name, target):
        buf = s.G[name]
        half = target.shape[1] // 2

        def one(i, carry):
            zz, pair = i // 4, 2 * (i % 4)
            even = buf[zz, pair].astype(F32)
            odd = buf[zz, pair + 1].astype(F32)
            rows = pl.ds(pl.multiple_of(48 * i, 16), 48)
            target[rows, :half] = jnp.concatenate([even[:24], odd[:24]], axis=0).astype(BF16)
            target[rows, half:] = jnp.concatenate([even[24:], odd[24:]], axis=0).astype(BF16)
            return carry

        lax.fori_loop(0, 16, one, 0)

    def project():
        def one(n, carry):
            cols = lanes(1152 * n, 1152)
            s.PRJ[:, cols] = (nn(s.XB[...], s.WI[:, cols]) + s.PB[:, cols]).astype(BF16)
            return carry

        lax.fori_loop(0, 2, one, 0)

    def attend(first, last):
        def one(step, carry):
            it, pair = step // 6, step % 6
            rows = rows_at(256 * it, 256)
            cols = lanes(128 * pair, 128)
            q = s.PRJ[rows, cols]
            k = s.PRJ[rows, lanes(768 + 128 * pair, 128)]
            v = s.PRJ[rows, lanes(1536 + 128 * pair, 128)]
            bias = live_bias(lengths[2 * y + it])
            total = jnp.zeros((128, 256), F32)
            for head in range(2):
                mask = half_mask(head)
                scores = nt(jnp.where(mask, k, 0), q) * SCORE_SCALE + bias
                exponent = jnp.exp(scores - jnp.max(scores, axis=0, keepdims=True))
                attention = exponent * (1.0 / jnp.sum(exponent, axis=0, keepdims=True))
                low = attention.astype(BF16)
                s.ATN[2 * step + head] = low
                total = total + tn(jnp.where(mask, v, 0), low)
            s.ATTT[cols, rows] = total.astype(BF16)
            s.XB[rows, cols] = total.T.astype(BF16)
            return carry

        lax.fori_loop(first, last, one, 0, unroll=3)

    def second_norm():
        def one(it, carry):
            rows = rows_at(256 * it, 256)
            middle = s.ENT[rows, :] + nn(s.XB[rows, :], s.WO[...]) + vector(4)
            s.MID[rows, :] = middle
            unit, _ = normalise(middle)
            second = (unit * vector(5) + vector(6)).astype(BF16)
            s.XB[rows, :] = second
            s.SECT[:, rows] = second.T
            return carry

        lax.fori_loop(0, 2, one, 0, unroll=2)

    def expand(first, last):
        def one(step, carry):
            n, it = step // 2, step % 2
            cols = lanes(768 * n, 768)
            rows = rows_at(256 * it, 256)
            expanded = nn(s.XB[rows, :], s.WE[:, cols]) + s.EB[:, cols]
            normal = 0.5 * (1.0 + lax.erf(expanded * 0.7071067811865476))
            density = jnp.exp(-0.5 * expanded * expanded) * 0.3989422804014327
            s.ACT[rows, cols] = (expanded * normal).astype(BF16)
            s.GP[rows, cols] = (normal + expanded * density).astype(BF16)
            return carry

        lax.fori_loop(first, last, one, 0)

    def take_in():
        def one(block, carry):
            it, half = block // 2, block % 2
            live = live_rows(lengths[2 * y + it], half, 128)
            incoming = jnp.where(live, s.INC[it, half].astype(F32), 0.0)
            s.INC[it, half] = incoming.astype(BF16)
            sums[7:8, :] += jnp.sum(incoming, axis=0, keepdims=True)
            return carry

        lax.fori_loop(0, 4, one, 0)

    def reduce_weight_grad():
        def one(f, carry):
            zz, xx = f // 2, f % 2
            moved = s.ACT[:, lanes(384 * f, 384)].T
            part = nn(moved, s.INC[...].reshape(512, 768))
            units = part.reshape(4, 96, 768).astype(BF16)
            s.P[W_R][zz, pl.ds(4 * xx, 4)] = units[:, :48]
            s.P[W_Q][zz, pl.ds(4 * xx, 4)] = units[:, 48:]
            return carry

        lax.fori_loop(0, 8, one, 0, unroll=2)

    def reduce_rows(zz):
        return jnp.concatenate([s.G[W_R][zz], s.G[W_Q][zz]], axis=1).reshape(768, 768)

    def expanded_grad(first, last):
        def one(step, carry):
            zz, it = step // 2, step % 2
            rows = rows_at(256 * it, 256)
            cols = lanes(768 * zz, 768)
            incoming = s.INC[it].reshape(256, 768)
            grad = (nt(incoming, reduce_rows(zz)) * s.GP[rows, cols].astype(F32)).astype(BF16)
            s.GP[rows, cols] = grad
            s.EBG[:, cols] += jnp.sum(grad.astype(F32), axis=0, keepdims=True)
            return carry

        lax.fori_loop(first, last, one, 0, unroll=4)

    def weight_grad(name, moved, grad, first, last):
        part, wide = s.P[name], 384
        half = UNITS[name][1]

        def one(step, carry):
            n, m = step // 2, step % 2
            left = grad[:, lanes(wide * n, wide)]
            right = grad[:, lanes(half + wide * n, wide)]
            block = nn(moved[rows_at(384 * m, 384), :], jnp.concatenate([left, right], axis=1))
            for j in range(8):
                for side in range(2):
                    rows = slice(48 * j + 24 * side, 48 * j + 24 * side + 24)
                    unit = jnp.concatenate([block[rows, :wide], block[rows, wide:]], axis=0)
                    part[2 * m + j // 4, 2 * (j % 4) + side, :, lanes(wide * n, wide)] = unit.astype(BF16)
            return carry

        if first == 0:
            gather[name].drain()
        lax.fori_loop(2 * first, 2 * last, one, 0, unroll=2)

    def finish_rows():
        def one(it, carry):
            rows = rows_at(256 * it, 256)
            out = s.MID[rows, :] + vector(7)
            for zz in range(4):
                out = out + nn(s.ACT[rows, 768 * zz : 768 * zz + 768], reduce_rows(zz))
            for half in range(2):
                live = live_rows(lengths[2 * y + it], half, 128)
                s.TOK[it, half] = jnp.where(live, out[128 * half : 128 * half + 128], 0.0).astype(BF16)
            return carry

        tok_out.wait_send()
        lax.fori_loop(0, 2, one, 0)
        out_copy.start()

    def middle_back():
        def one(it, carry):
            rows = rows_at(256 * it, 256)
            grad = nt(s.GP[rows, :], s.WE[...])
            unit, inverse = normalise(s.MID[rows, :])
            sums[5:6, :] += jnp.sum(grad * unit, axis=0, keepdims=True)
            sums[6:7, :] += jnp.sum(grad, axis=0, keepdims=True)
            incoming = s.INC[it].reshape(256, 768).astype(F32)
            middle_grad = incoming + normalise_back(grad * vector(5), unit, inverse)
            s.MID[rows, :] = middle_grad
            branch = middle_grad.astype(BF16)
            s.XB[rows, :] = branch
            sums[4:5, :] += jnp.sum(branch.astype(F32), axis=0, keepdims=True)
            return carry

        lax.fori_loop(0, 2, one, 0)

    def attended_back():
        def one(it, carry):
            rows = rows_at(256 * it, 256)
            s.XB[rows, :] = nt(s.XB[rows, :], s.WO[...]).astype(BF16)
            return carry

        lax.fori_loop(0, 2, one, 0, unroll=2)

    def attend_back(first, last):
        def one(step, carry):
            it, pair = step // 6, step % 6
            rows = rows_at(256 * it, 256)
            cols = lanes(128 * pair, 128)
            k_cols, v_cols = lanes(768 + 128 * pair, 128), lanes(1536 + 128 * pair, 128)
            q = s.PRJ[rows, cols]
            k = s.PRJ[rows, k_cols]
            v = s.PRJ[rows, v_cols]
            grad = s.XB[rows, cols]
            query_grad = jnp.zeros((128, 256), F32)
            key_grad = jnp.zeros((256, 128), F32)
            value_grad = jnp.zeros((256, 128), F32)
            for head in range(2):
                mask = half_mask(head)
                mine_grad = jnp.where(mask, grad, 0)
                weight_back = nt(v, mine_grad)
                low = s.ATN[2 * step + head]
                attention = low.astype(F32)
                inner = jnp.sum(attention * weight_back, axis=0, keepdims=True)
                scores_grad = (attention * (weight_back - inner)).astype(BF16)
                query_grad = query_grad + tn(jnp.where(mask, k, 0), scores_grad)
                key_grad = key_grad + nn(scores_grad, jnp.where(mask, q, 0))
                value_grad = value_grad + nn(low, mine_grad)
            query_low = (query_grad * SCORE_SCALE).T.astype(BF16)
            value_low = value_grad.astype(BF16)
            s.PRJ[rows, cols] = query_low
            s.PRJ[rows, k_cols] = (key_grad * SCORE_SCALE).astype(BF16)
            s.PRJ[rows, v_cols] = value_low
            sums[2:3, cols] += jnp.sum(query_low.astype(F32), axis=0, keepdims=True)
            sums[3:4, cols] += jnp.sum(value_low.astype(F32), axis=0, keepdims=True)
            return carry

        lax.fori_loop(first, last, one, 0, unroll=6)

    def entry_back(half):
        rows = [rows_at(256 * it + 128 * half, 128) for it in range(2)]

        def both(ref):
            return jnp.concatenate([ref[r, :] for r in rows], axis=0)

        grad = nt(both(s.PRJ), s.WI[...])
        unit, inverse = normalise(both(s.ENT))
        sums[0:1, :] += jnp.sum(grad * unit, axis=0, keepdims=True)
        sums[1:2, :] += jnp.sum(grad, axis=0, keepdims=True)
        return rows, both(s.MID) + normalise_back(grad * vector(0), unit, inverse)

    def entry_back_far():
        _, out = entry_back(1 - y)
        cot_out.wait_send()
        for it in range(2):
            s.INC[it, 1 - y] = out[128 * it : 128 * it + 128].astype(BF16)

    def entry_back_near():
        rows, out = entry_back(y)
        for it in range(2):
            s.ENT[rows[it], :] = out[128 * it : 128 * it + 128]
        for copy in near_copies:
            copy.start()

    def deal_sums():
        group = None
        for number in range(VECTORS):
            dealt = deal(sums[number : number + 1, :], spread_matrix(number % 4), CHUNK, 0)
            group = dealt if number % 4 == 0 else group + dealt
            if number % 4 == 3:
                s.P[VEC][:, :, number // 4, :] = group.reshape(4, 8, 128)
        group = jnp.zeros((32, 128), F32)
        for part in range(4):
            row = s.EBG[:, 768 * part : 768 * part + 768]
            group = group + deal(row, spread_matrix(None), 4 * CHUNK, 8 * part)
        s.P[VEC][:, :, 2, :] = group.reshape(4, 8, 128)
        for row in range(3, 8):
            s.P[VEC][:, :, row, :] = jnp.zeros((4, 8, 128), F32)

    def give_spare(index):
        pl.semaphore_signal(s.SPARE.at[index], inc=1, device_id=here.to_c, device_id_type=MESH)

    def place_grad(number, ref):
        cols = PIECES[number][1]
        half = ref.shape[1] // 2
        if cols is None:
            cols = slice(0, half)
        total = reduce[number].finish()
        ref[:, cols] = total[:24]
        ref[:, half + cols.start : half + cols.stop] = total[24:]

    def take_grad():
        grad_in.wait_recv()
        for it in range(2):
            s.ENT[rows_at(256 * it + 128 * (1 - y), 128), :] = s.TGR[it].astype(F32)
        for copy in far_copies:
            copy.start()

    def end():
        for made in (seen_out, lay_out, grad_out):
            made.wait_send()
        out_copy.wait()
        for copy in near_copies + far_copies:
            copy.wait()
        for one in (*gather, *reduce):
            one.drain()

    start()
    tok_out.start()
    gather[VEC].begin_x()
    gather[W_O].begin_x()
    gather[VEC].begin_z()
    gather[VEC].begin_y()
    gather[W_O].begin_y()
    seen_out.start()
    gather[W_E].begin_x()
    gather[W_I].begin_y()
    gather[W_Q].begin_x()
    gather[W_I].begin_x()
    gather[W_I].begin_z()
    gather[W_I].pass_on(1)
    gather[VEC].relay(0)
    gather[W_O].begin_z()
    gather[VEC].pass_on(1)
    gather[W_E].begin_z()
    gather[W_I].pass_on(3)
    gather[VEC].pass_on(2)
    gather[W_I].pass_on(2)
    seen_in.wait_recv()
    gather[VEC].pass_on(3)
    gather[W_I].relay(0)
    gather[VEC].relay(1)
    gather[W_Q].own_along_z()
    gather[W_E].begin_y()
    gather[VEC].own_to_core()
    gather[W_I].relay(1)
    gather[W_I].relay(3)
    gather[W_Q].begin_y()
    gather[W_O].pass_on(1)
    tok_copy.wait()
    tok_in.wait_recv()
    gather[W_I].relay(2)
    gather[VEC].relay(3)
    gather[VEC].relay(2)
    gather[W_O].pass_on(3)
    gather[W_O].pass_on(2)
    gather[W_R].begin_z()
    gather[W_I].sides_to_core()
    gather[W_E].relay(0)
    gather[W_E].pass_on(3)
    gather[W_E].pass_on(1)
    gather[VEC].sides_to_core()
    gather[W_O].relay(3)
    gather[W_E].pass_on(2)
    gather[W_I].corner()
    gather[VEC].corner()
    gather[W_I].own_to_core()
    gather[W_E].own_to_core()
    gather[W_E].relay(3)
    gather[W_O].relay(2)
    gather[VEC].from_core()
    vectors()
    gather[W_O].relay(1)
    gather[W_O].relay(0)
    gather[W_I].from_core()
    gather[W_O].own_to_core()
    gather[W_R].begin_y()
    gather[W_O].sides_to_core()
    spread_rows(W_I, s.WI)
    first_norm()
    gather[W_Q].relay()
    gather[W_E].relay(1)
    project()
    attend(0, 6)
    gather[W_E].relay(2)
    gather[W_E].sides_to_core()
    gather[W_R].begin_x()
    gather[W_R].pass_on(2)
    gather[W_O].corner()
    gather[W_R].pass_on(1)
    attend(6, 12)
    gather[W_Q].corner()
    gather[W_R].pass_on(3)
    cot_out.start()
    gather[W_E].corner()
    gather[W_Q].to_core(0)
    gather[W_O].from_core()
    spread_rows(W_O, s.WO)
    gather[W_Q].to_core(1)
    second_norm()
    gather[W_R].relay(0)
    gather[W_E].from_core()
    spread_rows(W_E, s.WE)
    expand(0, 4)
    gather[W_R].relay(2)
    expand(4, 8)
    gather[W_R].relay(3)
    gather[W_R].relay(1)
    gather[W_Q].to_core(2)
    cot_copy.wait()
    cot_in.wait_recv()
    gather[W_R].sides_to_core()
    gather[W_R].own_to_core()
    gather[W_Q].to_core(3)
    take_in()
    gather[W_R].corner()
    reduce_weight_grad()
    reduce[D_R].core_send()
    gather[W_Q].from_core()
    gather[W_R].from_core()
    expanded_grad(0, 4)
    reduce[D_R].core_add(0)
    reduce[D_Q].core_send()
    expanded_grad(4, 8)
    reduce[D_R].core_add(1)
    reduce[D_R].core_add(2)
    reduce[D_R].core_add(3)
    give_spare(0)
    reduce[D_Q].core_add(0)
    weight_grad(W_E, s.SECT, s.GP, 0, 2)
    reduce[D_Q].core_add(1)
    reduce[D_EA].core_send(s.SPARE.at[0])
    reduce[D_R].relay()
    reduce[D_Q].core_add(2)
    finish_rows()
    reduce[D_EA].core_add(0)
    weight_grad(W_E, s.SECT, s.GP, 2, 4)
    lay_out.start()
    reduce[D_EA].core_add(1)
    middle_back()
    reduce[D_Q].core_add(3)
    give_spare(1)
    reduce[D_EB].core_send(s.SPARE.at[1])
    weight_grad(W_O, s.ATTT, s.XB, 0, 1)
    reduce[D_EA].core_add(2)
    attended_back()
    reduce[D_EA].relay()
    reduce[D_EB].core_add(0)
    reduce[D_R].sides()
    attend_back(0, 6)
    reduce[D_EB].core_add(1)
    attend_back(6, 12)
    weight_grad(W_I, s.NRMT, s.PRJ, 0, 2)
    reduce[D_EB].core_add(2)
    weight_grad(W_I, s.NRMT, s.PRJ, 2, 3)
    reduce[D_EB].relay()
    reduce[D_EA].core_add(3)
    give_spare(2)
    reduce[D_IA].core_send(s.SPARE.at[2])
    reduce[D_EA].sides()
    reduce[D_EB].core_add(3)
    give_spare(3)
    reduce[D_IA].core_add(0)
    reduce[D_IB].core_send(s.SPARE.at[3])
    reduce[D_O].core_send()
    entry_back_far()
    reduce[D_O].core_add(0)
    reduce[D_IA].core_add(1)
    reduce[D_IA].core_add(2)
    entry_back_near()
    reduce[D_IA].relay()
    deal_sums()
    reduce[D_EB].sides()
    reduce[D_IB].core_add(0)
    reduce[D_Q].relay()
    reduce[D_V].core_send()
    place_grad(D_EA, grad_E)
    reduce[D_V].core_add(0)
    reduce[D_V].core_add(1)
    reduce[D_O].core_add(1)
    reduce[D_O].core_add(2)
    lay_in.wait_recv()
    reduce[D_O].relay()
    reduce[D_IA].core_add(3)
    reduce[D_IB].core_add(1)
    reduce[D_IA].sides()
    reduce[D_IB].core_add(2)
    reduce[D_V].core_add(2)
    grad_R[0:48, :] = reduce[D_R].finish()
    reduce[D_O].core_add(3)
    reduce[D_IB].relay()
    reduce[D_IB].core_add(3)
    reduce[D_V].core_add(3)
    place_grad(D_EB, grad_E)
    reduce[D_V].relay()
    reduce[D_Q].sides()
    grad_out.start()
    reduce[D_O].sides()
    reduce[D_IB].sides()
    grad_R[48:96, :] = reduce[D_Q].finish()
    place_grad(D_O, grad_O)
    reduce[D_V].sides()
    place_grad(D_IB, grad_I)
    place_grad(D_IA, grad_I)
    grad_V[...] = reduce[D_V].finish()
    take_grad()
    end()


UNITS = ((48, 1152), (48, 384), (48, 1536), (48, 768), (48, 768), (8, 128))


PIECES = (
    (W_I, slice(0, 768), 1),
    (W_I, slice(768, 1152), 2),
    (W_O, None, 0),
    (W_E, slice(0, 768), 1),
    (W_E, slice(768, 1536), 2),
    (W_R, None, 1),
    (W_Q, None, 2),
    (VEC, None, 3),
)


def scratch_list():
    dma, vmem = pltpu.SemaphoreType.DMA, pltpu.VMEM
    shapes = dict(
        SWS=dma((5,)),
        SWR=dma((5,)),
        LOC=dma((7,)),
        SPARE=pltpu.SemaphoreType.REGULAR((4,)),
        TOK=vmem((2, 2, 128, 768), BF16),
        INC=vmem((2, 2, 128, 768), BF16),
        SEEN=vmem((2, 2, 8, 128), jnp.int32),
        AWAY=vmem((2, 8, 128), jnp.int32),
        ROWS=vmem((8, 768), F32),
        STAGE=vmem((16, 128), F32),
        EB=vmem((1, 3072), F32),
        PB=vmem((1, 2304), F32),
        SUMS=vmem((8, 768), F32),
        EBG=vmem((1, 3072), F32),
        WI=vmem((768, 2304), BF16),
        WO=vmem((768, 768), BF16),
        WE=vmem((768, 3072), BF16),
        ENT=vmem((512, 768), F32),
        MID=vmem((512, 768), F32),
        XB=vmem((512, 768), BF16),
        NRMT=vmem((768, 512), BF16),
        ATTT=vmem((768, 512), BF16),
        SECT=vmem((768, 512), BF16),
        PRJ=vmem((512, 2304), BF16),
        ATN=vmem((24, 256, 256), BF16),
        ACT=vmem((512, 3072), BF16),
        GP=vmem((512, 3072), BF16),
        TGR=vmem((2, 128, 768), BF16),
    )
    many = dict(G=[], GS=[], GQ=[], P=[], RC=[], R1=[], R2=[], RZ=[], RS=[], RQ=[])
    for name in TENSORS:
        kind = F32 if name == VEC else BF16
        unit = UNITS[name]
        plane = name == W_Q
        many["G"].append(vmem((4, 8, *unit), kind))
        many["GS"].append(dma((SEMS,)))
        many["GQ"].append(dma((SEMS,)))
        if name in (W_R, W_Q, VEC):
            many["P"].append(vmem((4, 8, *unit), kind))
        if name not in (W_I, W_E):
            many["RC"].append(vmem((4, 4, *unit), kind))
        many["R1"].append(vmem(unit if plane else (4, *unit), kind))
        many["R2"].append(vmem((2, *unit) if plane else (4, 2, *unit), kind))
        many["RZ"].append(vmem((3, 4, *unit) if plane else (3, *unit), kind))
    for _ in SUMS:
        many["RS"].append(dma((SEMS,)))
        many["RQ"].append(dma((SEMS,)))
    return shapes, many


class Store:
    def __init__(self, refs):
        shapes, many = scratch_list()
        refs = list(refs)
        for name in shapes:
            setattr(self, name, refs.pop(0))
        for name, listed in many.items():
            setattr(self, name, [refs.pop(0) for _ in listed])
        self.P = self.G[:3] + self.P


def position_table():
    step = np.arange(16, dtype=np.float64)[:, None]
    channel = np.arange(256)
    angle = step * np.power(10000.0, -(channel // 2) / 128.0)
    whole = np.where(channel % 2 == 0, np.sin(angle), np.cos(angle)).astype(np.float32)
    high = whole.astype(jnp.bfloat16)
    rest = whole - high.astype(np.float32)
    middle = rest.astype(jnp.bfloat16)
    low = (rest - middle.astype(np.float32)).astype(jnp.bfloat16)
    return np.concatenate([high, middle, low], axis=0)


def hand_over(*refs):
    given, vectors_in, results, rows = refs[:6], refs[6], refs[7:13], refs[13:22]
    holds, sems = refs[22:28], refs[28]
    steps = []
    for src, hold, dst in zip(given, holds, results):
        parts = src.shape[0] if len(src.shape) == 3 else 1
        for part in range(parts):
            where = part if parts > 1 else slice(None)
            number = len(steps)
            steps.append((
                pltpu.make_async_copy(src.at[where], hold.at[where], sems.at[0, number]),
                pltpu.make_async_copy(hold.at[where], dst.at[where], sems.at[1, number]),
            ))
    for first, _ in steps:
        first.start()
    for number in range(VECTORS):
        slot = number % 4
        rows[number][...] = vectors_in[number // 4 : number // 4 + 1, 32 * slot : 32 * slot + CHUNK]
    row = vectors_in[2:3, :]
    lane = lax.broadcasted_iota(jnp.int32, (1, 128), 1)
    joined = row
    for slot in range(1, 4):
        joined = jnp.where(lane >= CHUNK * slot, pltpu.roll(row, 128 - 8 * slot, 1), joined)
    rows[8][...] = joined[:, : 4 * CHUNK]
    for first, second in steps:
        first.wait()
        second.start()
    for _, second in steps:
        second.wait()


def fused_body(
    tokens, visible, lengths, first_gain, first_shift, input_weight, query_bias, value_bias,
    output_weight, output_bias, second_gain, second_shift, expand_weight, expand_bias,
    reduce_weight, reduce_bias, cotangent,
):
    hbm = pl.BlockSpec(memory_space=pl.ANY)
    vmem = pl.BlockSpec(memory_space=pltpu.VMEM)
    smem = pl.BlockSpec(memory_space=pltpu.SMEM)
    shapes, many = scratch_list()
    results = [
        jax.ShapeDtypeStruct((4, 128, 768), BF16),
        jax.ShapeDtypeStruct((4, 128, 768), F32),
        jax.ShapeDtypeStruct(input_weight.shape, F32),
        jax.ShapeDtypeStruct(output_weight.shape, F32),
        jax.ShapeDtypeStruct(expand_weight.shape, F32),
        jax.ShapeDtypeStruct(reduce_weight.shape, F32),
        jax.ShapeDtypeStruct((8, 128), F32),
    ]
    layer_out, tokens_grad, grad_I, grad_O, grad_E, grad_R, grad_V = pl.pallas_call(
        fused_kernel,
        name="layer",
        out_shape=results,
        in_specs=[smem, hbm, hbm] + [vmem] * 15,
        out_specs=[hbm, hbm, vmem, vmem, vmem, vmem, vmem],
        scratch_shapes=[*shapes.values(), *(shape for listed in many.values() for shape in listed)],
        compiler_params=pltpu.CompilerParams(
            collective_id=0, has_side_effects=True, vmem_limit_bytes=VMEM_BYTES
        ),
    )(
        lengths, tokens[:, 0], cotangent[:, 0], visible, input_weight, output_weight, expand_weight,
        reduce_weight, jnp.asarray(position_table()),
        *(
            vector.reshape(1, -1)
            for vector in (
                first_gain, first_shift, query_bias, value_bias, output_bias, second_gain, second_shift,
                reduce_bias, expand_bias,
            )
        ),
    )
    parts = (layer_out, tokens_grad, grad_I, grad_O, grad_E, grad_R)
    row, long_row = jax.ShapeDtypeStruct((1, CHUNK), F32), jax.ShapeDtypeStruct((1, 4 * CHUNK), F32)
    layer_out, tokens_grad, grad_I, grad_O, grad_E, grad_R, *rows = pl.pallas_call(
        hand_over,
        name="hand_over",
        out_shape=[jax.ShapeDtypeStruct(part.shape, part.dtype) for part in parts] + [row] * VECTORS + [long_row],
        in_specs=[hbm] * 6 + [vmem],
        out_specs=[hbm] * 6 + [vmem] * 9,
        scratch_shapes=[pltpu.VMEM(part.shape, part.dtype) for part in parts] + [pltpu.SemaphoreType.DMA((2, 12))],
    )(*parts, grad_V)
    dealt = [row.reshape(-1) for row in rows]
    return (
        layer_out[:, None], tokens_grad[:, None], dealt[0], dealt[1], grad_I, dealt[2], dealt[3], grad_O,
        dealt[4], dealt[5], dealt[6], grad_E, dealt[8], grad_R, dealt[7],
    )


VMEM_BYTES = 67000000


def solution(mesh):
    in_specs = (
        P("items", "seq", None, None),
        P("items", "seq", None),
        P("items"),
        P(("items", "seq")),
        P(("items", "seq")),
        P(("items", "seq"), None),
        P(("items", "seq")),
        P(("items", "seq")),
        P(("items", "seq"), None),
        P(("items", "seq")),
        P(("items", "seq")),
        P(("items", "seq")),
        P(("items", "seq"), None),
        P(("items", "seq")),
        P(("items", "seq"), None),
        P(("items", "seq")),
        P("items", "seq", None, None),
    )
    out_specs = (
        P("items", "seq", None, None),
        P("items", "seq", None, None),
        P(("items", "seq")),
        P(("items", "seq")),
        P(("items", "seq"), None),
        P(("items", "seq")),
        P(("items", "seq")),
        P(("items", "seq"), None),
        P(("items", "seq")),
        P(("items", "seq")),
        P(("items", "seq")),
        P(("items", "seq"), None),
        P(("items", "seq")),
        P(("items", "seq"), None),
        P(("items", "seq")),
    )
    sizes = (mesh.shape["items"], mesh.shape["seq"])
    chosen = fused_body if sizes == (Z_SIZE * 4, 2) else general_body
    return jax.shard_map(chosen, mesh=mesh, in_specs=in_specs, out_specs=out_specs, check_vma=False)
```

```python
import functools

import jax
import jax.numpy as jnp
import numpy as np
from jax import lax
from jax.experimental import pallas as pl
from jax.experimental.pallas import tpu as pltpu
from jax.sharding import PartitionSpec as P

HD = 64
GRID = 14
MICRO = 2
ITEMS_MB = 2


EPSILON = 1e-06
SCORE_SCALE = 0.125


def layer_norm(rows_in, gain, shift):
    centre = rows_in - jnp.mean(rows_in, axis=-1, keepdims=True)
    spread = jnp.mean(centre * centre, axis=-1, keepdims=True)
    return centre * lax.rsqrt(spread + EPSILON) * gain + shift


def gelu_exact(value_in):
    return jax.nn.gelu(value_in, approximate=False)


def positions(index, model_width):
    channel = jnp.arange(model_width)
    portion = 3 * channel // model_width
    frequency = jnp.power(10000.0, -(channel % 256 // 2).astype(jnp.float32) / 128.0)
    which_frame = index // (GRID * GRID)
    which_row = index % (GRID * GRID) // GRID
    which_column = index % GRID
    coordinate = jnp.where(
        portion == 0,
        which_frame[..., None],
        jnp.where(portion == 1, which_row[..., None], which_column[..., None]),
    )
    angle = coordinate.astype(jnp.float32) * frequency
    return jnp.where(channel % 2 == 0, jnp.sin(angle), jnp.cos(angle))


def contract_rows(left, right):
    return lax.dot_general(
        left, right, (((0,), (0,)), ((), ())), preferred_element_type=jnp.float32
    )


def against(left, right):
    return lax.dot_general(
        left, right, (((1,), (1,)), ((), ())), preferred_element_type=jnp.float32
    )


def row_masks(lengths, block_rows, block_number):
    counts = (lengths + 1 - block_number) // 2
    return jnp.arange(block_rows)[None, :] < counts[:, None]


def micro_batch(gathered, tokens, visible, lengths, cotangent, seq_place):
    (
        first_gain,
        first_shift,
        input_weight,
        query_bias,
        value_bias,
        output_weight,
        output_bias,
        second_gain,
        second_shift,
        expand_weight,
        expand_bias,
        reduce_weight,
        reduce_bias,
    ) = gathered
    item_count, block_rows, model_width = tokens.shape
    head_count = model_width // HD
    total_rows = item_count * block_rows
    (
        first_gain,
        first_shift,
        query_bias,
        value_bias,
        output_bias,
        second_gain,
        second_shift,
        expand_bias,
        reduce_bias,
    ) = (
        vector.astype(jnp.float32)
        for vector in (
            first_gain,
            first_shift,
            query_bias,
            value_bias,
            output_bias,
            second_gain,
            second_shift,
            expand_bias,
            reduce_bias,
        )
    )
    query_live = row_masks(lengths, block_rows, seq_place).reshape(total_rows, 1)
    key_live = jnp.concatenate(
        [row_masks(lengths, block_rows, 0), row_masks(lengths, block_rows, 1)], axis=1
    )
    key_mask = key_live[:, None, None, :]
    entry = tokens.reshape(total_rows, model_width).astype(jnp.float32) + positions(
        visible.reshape(total_rows), model_width
    )
    normed, first_pull = jax.vjp(layer_norm, entry, first_gain, first_shift)
    normed_low = normed.astype(jnp.bfloat16)
    joined_bias = jnp.concatenate([query_bias, jnp.zeros_like(query_bias), value_bias])
    projected = (
        jnp.dot(normed_low, input_weight, preferred_element_type=jnp.float32) + joined_bias
    ).astype(jnp.bfloat16)
    queries = projected[:, :model_width].reshape(item_count, block_rows, head_count, HD)
    keys_here = projected[:, model_width : 2 * model_width].reshape(
        item_count, block_rows, model_width
    )
    values_here = projected[:, 2 * model_width :].reshape(item_count, block_rows, model_width)
    keys_all, values_all = (
        lax.all_gather(keys_here, "seq", axis=1, tiled=True),
        lax.all_gather(values_here, "seq", axis=1, tiled=True),
    )
    keys_all = keys_all.reshape(item_count, 2 * block_rows, head_count, HD)
    values_all = values_all.reshape(item_count, 2 * block_rows, head_count, HD)
    scores = (
        jnp.einsum("cqhd,ckhd->chqk", queries, keys_all, preferred_element_type=jnp.float32)
        * SCORE_SCALE
    )
    scores = jnp.where(key_mask, scores, -1e30)
    row_max = jnp.max(scores, axis=-1, keepdims=True)
    exponent = jnp.exp(scores - row_max)
    row_total = jnp.sum(exponent, axis=-1, keepdims=True)
    attention_low = (exponent / row_total).astype(jnp.bfloat16)
    log_total = row_max + jnp.log(row_total)
    attended = jnp.einsum(
        "chqk,ckhd->cqhd", attention_low, values_all, preferred_element_type=jnp.float32
    )
    attended = attended.reshape(total_rows, model_width).astype(jnp.bfloat16)
    middle = (
        entry + jnp.dot(attended, output_weight, preferred_element_type=jnp.float32) + output_bias
    )
    second, second_pull = jax.vjp(layer_norm, middle, second_gain, second_shift)
    second_low = second.astype(jnp.bfloat16)
    expanded = jnp.dot(second_low, expand_weight, preferred_element_type=jnp.float32) + expand_bias
    activated, gelu_pull = jax.vjp(gelu_exact, expanded)
    activated_low = activated.astype(jnp.bfloat16)
    result = (
        middle
        + jnp.dot(activated_low, reduce_weight, preferred_element_type=jnp.float32)
        + reduce_bias
    )
    layer_out = jnp.where(query_live, result, 0.0).astype(jnp.bfloat16)
    incoming = jnp.where(
        query_live, cotangent.reshape(total_rows, model_width).astype(jnp.float32), 0.0
    )
    incoming_low = incoming.astype(jnp.bfloat16)
    reduce_weight_grad = contract_rows(activated_low, incoming_low)
    reduce_bias_grad = jnp.sum(incoming, axis=0)
    activated_grad = against(incoming_low, reduce_weight)
    expanded_grad = gelu_pull(activated_grad)[0].astype(jnp.bfloat16)
    expand_weight_grad = contract_rows(second_low, expanded_grad)
    expand_bias_grad = jnp.sum(expanded_grad.astype(jnp.float32), axis=0)
    second_grad = against(expanded_grad, expand_weight)
    middle_part, second_gain_grad, second_shift_grad = second_pull(second_grad)
    middle_grad = incoming + middle_part
    branch_grad = middle_grad.astype(jnp.bfloat16)
    output_weight_grad = contract_rows(attended, branch_grad)
    output_bias_grad = jnp.sum(branch_grad.astype(jnp.float32), axis=0)
    attended_grad = against(branch_grad, output_weight).astype(jnp.bfloat16)
    attended_grad = attended_grad.reshape(item_count, block_rows, head_count, HD)
    scores = (
        jnp.einsum("cqhd,ckhd->chqk", queries, keys_all, preferred_element_type=jnp.float32)
        * SCORE_SCALE
    )
    scores = jnp.where(key_mask, scores, -1e30)
    attention_full = jnp.exp(scores - log_total)
    attention_low = attention_full.astype(jnp.bfloat16)
    weight_grad = jnp.einsum(
        "cqhd,ckhd->chqk", attended_grad, values_all, preferred_element_type=jnp.float32
    )
    row_inner = jnp.sum(attention_full * weight_grad, axis=-1, keepdims=True)
    scores_grad = (attention_full * (weight_grad - row_inner)).astype(jnp.bfloat16)
    query_grad = (
        jnp.einsum("chqk,ckhd->cqhd", scores_grad, keys_all, preferred_element_type=jnp.float32)
        * SCORE_SCALE
    )
    key_terms = (
        jnp.einsum("chqk,cqhd->ckhd", scores_grad, queries, preferred_element_type=jnp.float32)
        * SCORE_SCALE
    )
    value_terms = jnp.einsum(
        "chqk,cqhd->ckhd", attention_low, attended_grad, preferred_element_type=jnp.float32
    )
    key_grad, value_grad = (
        lax.psum_scatter(
            key_terms.reshape(item_count, 2 * block_rows, model_width).astype(jnp.bfloat16),
            "seq",
            scatter_dimension=1,
            tiled=True,
        ).astype(jnp.float32),
        lax.psum_scatter(
            value_terms.reshape(item_count, 2 * block_rows, model_width).astype(jnp.bfloat16),
            "seq",
            scatter_dimension=1,
            tiled=True,
        ).astype(jnp.float32),
    )
    projected_grad = jnp.concatenate(
        [
            query_grad.reshape(total_rows, model_width),
            key_grad.reshape(total_rows, model_width),
            value_grad.reshape(total_rows, model_width),
        ],
        axis=1,
    ).astype(jnp.bfloat16)
    input_weight_grad = contract_rows(normed_low, projected_grad)
    projected_sums = jnp.sum(projected_grad.astype(jnp.float32), axis=0)
    query_bias_grad = projected_sums[:model_width]
    value_bias_grad = projected_sums[2 * model_width :]
    normed_grad = against(projected_grad, input_weight)
    entry_part, first_gain_grad, first_shift_grad = first_pull(normed_grad)
    tokens_grad = middle_grad + entry_part
    grads = (
        first_gain_grad,
        first_shift_grad,
        input_weight_grad,
        query_bias_grad,
        value_bias_grad,
        output_weight_grad,
        output_bias_grad,
        second_gain_grad,
        second_shift_grad,
        expand_weight_grad,
        expand_bias_grad,
        reduce_weight_grad,
        reduce_bias_grad,
    )
    return (layer_out, tokens_grad, grads)


def general_body(
    tokens,
    visible,
    lengths,
    first_gain,
    first_shift,
    input_weight,
    query_bias,
    value_bias,
    output_weight,
    output_bias,
    second_gain,
    second_shift,
    expand_weight,
    expand_bias,
    reduce_weight,
    reduce_bias,
    cotangent,
):
    shards = (
        first_gain,
        first_shift,
        input_weight,
        query_bias,
        value_bias,
        output_weight,
        output_bias,
        second_gain,
        second_shift,
        expand_weight,
        expand_bias,
        reduce_weight,
        reduce_bias,
    )
    seq_place = lax.axis_index("seq")
    block_rows = tokens.shape[2]
    model_width = tokens.shape[3]
    outputs_list = []
    gradients_list = []
    totals = None
    for micro_index in range(MICRO):
        first_item = micro_index * ITEMS_MB
        last_item = first_item + ITEMS_MB
        gathered = (
            lax.all_gather(shards[0], ("items", "seq"), axis=0, tiled=True),
            lax.all_gather(shards[1], ("items", "seq"), axis=0, tiled=True),
            lax.all_gather(shards[2], ("items", "seq"), axis=0, tiled=True),
            lax.all_gather(shards[3], ("items", "seq"), axis=0, tiled=True),
            lax.all_gather(shards[4], ("items", "seq"), axis=0, tiled=True),
            lax.all_gather(shards[5], ("items", "seq"), axis=0, tiled=True),
            lax.all_gather(shards[6], ("items", "seq"), axis=0, tiled=True),
            lax.all_gather(shards[7], ("items", "seq"), axis=0, tiled=True),
            lax.all_gather(shards[8], ("items", "seq"), axis=0, tiled=True),
            lax.all_gather(shards[9], ("items", "seq"), axis=0, tiled=True),
            lax.all_gather(shards[10], ("items", "seq"), axis=0, tiled=True),
            lax.all_gather(shards[11], ("items", "seq"), axis=0, tiled=True),
            lax.all_gather(shards[12], ("items", "seq"), axis=0, tiled=True),
        )
        layer_out, tokens_grad, grads = micro_batch(
            gathered,
            tokens[first_item:last_item, 0],
            visible[first_item:last_item, 0],
            lengths[first_item:last_item],
            cotangent[first_item:last_item, 0],
            seq_place,
        )
        outputs_list.append(layer_out)
        gradients_list.append(tokens_grad)
        shares = (
            lax.psum_scatter(grads[0], ("items", "seq"), scatter_dimension=0, tiled=True),
            lax.psum_scatter(grads[1], ("items", "seq"), scatter_dimension=0, tiled=True),
            lax.psum_scatter(grads[2], ("items", "seq"), scatter_dimension=0, tiled=True),
            lax.psum_scatter(grads[3], ("items", "seq"), scatter_dimension=0, tiled=True),
            lax.psum_scatter(grads[4], ("items", "seq"), scatter_dimension=0, tiled=True),
            lax.psum_scatter(grads[5], ("items", "seq"), scatter_dimension=0, tiled=True),
            lax.psum_scatter(grads[6], ("items", "seq"), scatter_dimension=0, tiled=True),
            lax.psum_scatter(grads[7], ("items", "seq"), scatter_dimension=0, tiled=True),
            lax.psum_scatter(grads[8], ("items", "seq"), scatter_dimension=0, tiled=True),
            lax.psum_scatter(grads[9], ("items", "seq"), scatter_dimension=0, tiled=True),
            lax.psum_scatter(grads[10], ("items", "seq"), scatter_dimension=0, tiled=True),
            lax.psum_scatter(grads[11], ("items", "seq"), scatter_dimension=0, tiled=True),
            lax.psum_scatter(grads[12], ("items", "seq"), scatter_dimension=0, tiled=True),
        )
        totals = (
            shares
            if totals is None
            else tuple((earlier + later for earlier, later in zip(totals, shares)))
        )
    item_count = tokens.shape[0]
    layer_out = jnp.concatenate(outputs_list, axis=0).reshape(
        item_count, 1, block_rows, model_width
    )
    tokens_grad = jnp.concatenate(gradients_list, axis=0).reshape(
        item_count, 1, block_rows, model_width
    )
    return (
        layer_out,
        tokens_grad,
        totals[0],
        totals[1],
        totals[2],
        totals[3],
        totals[4],
        totals[5],
        totals[6],
        totals[7],
        totals[8],
        totals[9],
        totals[10],
        totals[11],
        totals[12],
    )


Z_SIZE = 4
F32 = jnp.float32
BF16 = jnp.bfloat16
MESH = pl.DeviceIdType.MESH
CHUNK = 24
W_I, W_O, W_E, W_R, W_Q, VEC = TENSORS = range(6)
GATHER_X = (3, 3, 3, 3, None, 2)
D_IA, D_IB, D_O, D_EA, D_EB, D_R, D_Q, D_V = SUMS = range(8)
REDUCE_X = (3, 3, 3, 3, 3, 3, None, 2)
SEMS = 24
R_ROWS, Q_ROWS = 32, 64
VECTORS = 8


def nn(left, right):
    return lax.dot_general(left, right, (((1,), (0,)), ((), ())), preferred_element_type=F32)


def nt(left, right):
    return lax.dot_general(left, right, (((1,), (1,)), ((), ())), preferred_element_type=F32)


def tn(left, right):
    return lax.dot_general(left, right, (((0,), (0,)), ((), ())), preferred_element_type=F32)


def lanes(start, size):
    return pl.ds(pl.multiple_of(start, 128), size)


def rows_at(start, size):
    return pl.ds(pl.multiple_of(start, 128), size)


class Place:
    def __init__(self):
        item = lax.axis_index("items")
        self.y = lax.axis_index("seq")
        self.z = item // 4
        self.x = (item // 2) % 2
        self.c = item % 2

    def device(self, z, x, c, y):
        return ((z * 2 + x) * 2 + c, y)

    def to_z(self, k):
        return self.device(lax.rem(self.z + k, Z_SIZE), self.x, self.c, self.y)

    @property
    def inner(self):
        return jnp.logical_or(self.z == 1, self.z == 2)

    @property
    def outer(self):
        return jnp.logical_or(self.z == 0, self.z == 3)

    def near(self, k):
        return None if k == 2 else self.z != (0 if k == 3 else 3)

    def at_z(self, z):
        return self.device(z, self.x, self.c, self.y)

    @property
    def to_x(self):
        return self.device(self.z, 1 - self.x, self.c, self.y)

    @property
    def to_y(self):
        return self.device(self.z, self.x, self.c, 1 - self.y)

    @property
    def to_c(self):
        return self.device(self.z, self.x, 1 - self.c, self.y)

    def column(self, flip_x, flip_c, flip_y):
        x = 1 - self.x if flip_x else self.x
        c = 1 - self.c if flip_c else self.c
        y = 1 - self.y if flip_y else self.y
        return x * 4 + c * 2 + y

    def quarter(self, flip_x, flip_y):
        x = 1 - self.x if flip_x else self.x
        y = 1 - self.y if flip_y else self.y
        return x * 2 + y


def remote(src, dst, send, recv, device):
    return pltpu.make_async_remote_copy(
        src_ref=src, dst_ref=dst, send_sem=send, recv_sem=recv, device_id=device, device_id_type=MESH
    )


def under(condition, action):
    if condition is None:
        action()
    else:
        pl.when(condition)(action)


class Gather:
    def __init__(self, here, buf, send, recv, share):
        self.here, self.buf, self.send, self.recv = here, buf, send, recv
        self.share = share
        self.open = []

    def copy(self, slot, index, device, recv=None):
        ref = self.buf.at[slot]
        recv = index if recv is None else recv
        return remote(ref, ref, self.send.at[index], self.recv.at[recv], device)

    def push(self, slot, index, device, when=None, recv=None):
        made = self.copy(slot, index, device, recv)
        under(when, made.start)
        self.open.append((made, when))

    def along(self, slot, first):
        for k in (1, 3, 2):
            self.push(slot, first + k - 1, self.here.to_z(k), self.here.near(k))

    def hand_on(self, slot, first, index):
        up = self.here.z == 2
        device = self.here.at_z(jnp.where(up, 3, 0))
        self.push(slot, index, device, self.here.inner, first + jnp.where(up, 2, 0))

    def pull(self, slot, index):
        self.copy(slot, index, self.here.to_x).wait_recv()

    def behind(self, k):
        return lax.rem(self.here.z + (Z_SIZE - k), Z_SIZE)

    def own(self):
        return (self.here.z, self.here.column(0, 0, 0))

    def begin_z(self):
        self.along(self.own(), 0)

    def begin_x(self):
        self.push(self.own(), 3, self.here.to_x)

    def begin_y(self):
        self.push(self.own(), 7, self.here.to_y)

    def pass_on(self, k):
        here = self.here
        slot = (self.behind(k), here.column(0, 0, 0))
        self.pull(slot, k - 1)
        if k == 2:
            self.hand_on(slot, 0, 19)
        self.push(slot, 3 + k, here.to_x)
        self.push(slot, 7 + k, here.to_y)

    def own_to_core(self):
        here = self.here
        self.push((slice(None), here.column(0, 0, 0)), 15, here.to_c)

    def relay(self, k):
        here = self.here
        from_x = (self.behind(k), here.column(1, 0, 0))
        from_y = (self.behind(k), here.column(0, 0, 1))
        self.pull(from_x, 3 + k)
        self.pull(from_y, 7 + k)
        if k < self.share:
            self.push(from_y, 11 + k, here.to_x)
        else:
            self.push(from_x, 11 + k, here.to_y)

    def sides_to_core(self):
        here = self.here
        self.push((slice(None), here.column(1, 0, 0)), 16, here.to_c)
        self.push((slice(None), here.column(0, 0, 1)), 17, here.to_c)

    def corner(self):
        here = self.here
        for k in range(4):
            self.pull((self.behind(k), here.column(1, 0, 1)), 11 + k)
        self.push((slice(None), here.column(1, 0, 1)), 18, here.to_c)

    def from_core(self):
        here = self.here
        for index, (fx, fy) in ((15, (0, 0)), (16, (1, 0)), (17, (0, 1)), (18, (1, 1))):
            self.pull((slice(None), here.column(fx, 1, fy)), index)

    def drain(self):
        for made, when in self.open:
            under(when, made.wait_send)
        self.open = []


class PlaneGather(Gather):
    def halves(self):
        wide = self.buf.shape[-1] // 2
        return slice(0, wide), slice(wide, 2 * wide)

    def begin_x(self):
        self.push(self.own(), 0, self.here.to_x)

    def begin_y(self):
        self.push(self.own(), 1, self.here.to_y)

    def along_z(self, column, first):
        self.along((self.here.z, column), first)

    def own_along_z(self):
        self.along_z(self.here.column(0, 0, 0), 4)

    def relay(self):
        here = self.here
        left, right = self.halves()
        from_x, from_y = here.column(1, 0, 0), here.column(0, 0, 1)
        self.pull((here.z, from_x), 0)
        self.push((here.z, from_x, slice(None), right), 3, here.to_y)
        self.pull((here.z, from_y), 1)
        self.push((here.z, from_y, slice(None), left), 2, here.to_x)
        self.along_z(from_x, 7)
        self.along_z(from_y, 10)

    def corner(self):
        here = self.here
        left, right = self.halves()
        corner = here.column(1, 0, 1)
        self.pull((here.z, corner, slice(None), left), 2)
        self.pull((here.z, corner, slice(None), right), 3)
        self.along_z(corner, 13)

    def pass_z(self, part):
        flips = ((0, 0), (1, 0), (0, 1), (1, 1))[part]
        slot = (self.behind(2), self.here.column(flips[0], 0, flips[1]))
        self.pull(slot, 5 + 3 * part)
        self.hand_on(slot, 4 + 3 * part, 20 + part)

    def to_core(self, part):
        here = self.here
        flips = ((0, 0), (1, 0), (0, 1), (1, 1))[part]
        column = here.column(flips[0], 0, flips[1])
        for k in (1, 3):
            self.pull((self.behind(k), column), 4 + 3 * part + k - 1)
        self.push((slice(None), column), 16 + part, here.to_c)

    def from_core(self):
        here = self.here
        for index, (fx, fy) in enumerate(((0, 0), (1, 0), (0, 1), (1, 1))):
            self.pull((slice(None), here.column(fx, 1, fy)), 16 + index)


QUARTERS = ((1, 1), (1, 0), (0, 1), (0, 0))


class Reduce:
    def __init__(self, here, part, core, relay, sides, ends, middle, send, recv, share):
        self.here, self.part, self.core, self.sides_in, self.ends = here, part, core, sides, ends
        self.middle = middle
        self.share = share
        self.relay_in = relay
        self.send, self.recv = send, recv
        self.open = []

    def push(self, src, dst, index, device, when=None):
        made = remote(src, dst, self.send.at[index], self.recv.at[index], device)
        under(when, made.start)
        self.open.append((made, when))

    def across(self, column, ends, middle, first, index):
        here, z = self.here, self.here.z
        for k in (1, 3):
            away = lax.rem(z + k, Z_SIZE)
            self.push(self.part.at[away, column], ends[k - 1], first + k - 1, here.to_z(k), here.near(k))
        inner = here.at_z(jnp.where(z == 0, 1, 2))
        self.push(self.part.at[3 - z, column], middle, index, inner, here.outer)
        away = lax.rem(z + 2, Z_SIZE)
        self.push(self.part.at[away, column], ends[1], first + 1, here.to_z(2), here.outer)

    def add_middle(self, column, ends, middle, first, index):
        here = self.here
        away = lax.rem(here.z + 2, Z_SIZE)

        def add():
            self.pull(middle, index)
            total = self.part[away, column].astype(F32) + middle[...].astype(F32)
            self.part[away, column] = total.astype(self.part.dtype)

        pl.when(here.inner)(add)
        self.push(self.part.at[away, column], ends[1], first + 1, here.to_z(2), here.inner)

    def take_ends(self, ends, first):
        self.pull(ends[1], first + 1)
        for k, missing in ((1, 0), (3, 3)):
            ref = ends[k - 1]

            def clear(ref=ref):
                ref[...] = jnp.zeros(ref.shape, ref.dtype)

            pl.when(self.here.z != missing)(functools.partial(self.pull, ref, first + k - 1))
            pl.when(self.here.z == missing)(clear)

    def three_ends(self):
        return [self.ends.at[k] for k in range(3)]

    def pull(self, dst, index):
        remote(dst, dst, self.send.at[index], self.recv.at[index], self.here.to_x).wait_recv()

    def add(self, column, first, last, *others):
        part = self.part

        def one(z, carry):
            total = part[z, column].astype(F32)
            for ref, index in others:
                total = total + ref[z, index].astype(F32)
            part[z, column] = total.astype(part.dtype)
            return carry

        lax.fori_loop(first, last, one, 0)

    def core_send(self, spare=None, first=0, last=4):
        here = self.here
        if spare is not None:
            pl.semaphore_wait(spare, 1)
        for index in range(first, last):
            fx, fy = QUARTERS[index]
            self.push(
                self.part.at[:, here.column(fx, 1, fy)],
                self.core.at[:, here.quarter(fx, fy)],
                index,
                here.to_c,
            )

    def core_add(self, index):
        here, share = self.here, self.share
        fx, fy = QUARTERS[index]
        quarter, column = here.quarter(fx, fy), here.column(fx, 0, fy)
        self.pull(self.core.at[:, quarter], index)
        self.add(column, 0, 4, (self.core, quarter))
        part = self.part
        if index == 0:
            self.push(part.at[:share, column], self.relay_in.at[:share], 4, here.to_x)
            self.push(part.at[share:, column], self.relay_in.at[share:], 5, here.to_y)
        if index == 1:
            self.push(part.at[:share, column], self.sides_in.at[:share, 0], 6, here.to_x)
        if index == 2:
            self.push(part.at[share:, column], self.sides_in.at[share:, 1], 8, here.to_y)

    def relay(self):
        here, part, share = self.here, self.part, self.share
        to_x, to_y = here.column(1, 0, 0), here.column(0, 0, 1)

        def pair(z, column):
            total = part[z, column].astype(F32) + self.relay_in[z].astype(F32)
            part[z, column] = total.astype(part.dtype)

        self.pull(self.relay_in.at[share:], 5)
        for z in range(share, 4):
            pair(z, to_x)
        self.push(part.at[share:, to_x], self.sides_in.at[share:, 0], 7, here.to_x)
        self.pull(self.relay_in.at[:share], 4)

        def one(z, carry):
            pair(z, to_y)
            return carry

        lax.fori_loop(0, share, one, 0)
        self.push(part.at[:share, to_y], self.sides_in.at[:share, 1], 9, here.to_y)

    def sides(self):
        here, share = self.here, self.share
        for index, where in ((6, (slice(0, share), 0)), (8, (slice(share, 4), 1)),
                             (7, (slice(share, 4), 0)), (9, (slice(0, share), 1))):
            self.pull(self.sides_in.at[where], index)
        own = here.column(0, 0, 0)
        self.add(own, 0, 4, (self.sides_in, 0), (self.sides_in, 1))
        self.across(own, self.three_ends(), self.middle, 10, 13)

    def pass_z(self):
        self.add_middle(self.here.column(0, 0, 0), self.three_ends(), self.middle, 10, 13)

    def finish(self):
        here = self.here
        self.take_ends(self.three_ends(), 10)
        total = self.part[here.z, here.column(0, 0, 0)].astype(F32)
        for k in range(3):
            total = total + self.ends[k].astype(F32)
        return total

    def drain(self):
        for made, when in self.open:
            under(when, made.wait_send)
        self.open = []


class PlaneReduce(Reduce):
    def core_add(self, index):
        here = self.here
        fx, fy = QUARTERS[index]
        quarter, column = here.quarter(fx, fy), here.column(fx, 0, fy)
        self.pull(self.core.at[:, quarter], index)
        self.add(column, 0, 4, (self.core, quarter))
        self.across(column, self.column_ends(index), self.middle.at[index], 4 + 3 * index, 20 + index)

    def column_ends(self, index):
        return [self.ends.at[k, index] for k in range(3)]

    def pass_z(self, index):
        fx, fy = QUARTERS[index]
        column = self.here.column(fx, 0, fy)
        self.add_middle(column, self.column_ends(index), self.middle.at[index], 4 + 3 * index, 20 + index)

    def relay(self):
        here, part, z = self.here, self.part, self.here.z
        wide = part.shape[-1] // 2
        for index, (fx, fy) in enumerate(QUARTERS):
            column = here.column(fx, 0, fy)
            self.take_ends(self.column_ends(index), 4 + 3 * index)
            total = part[z, column].astype(F32)
            for k in range(3):
                total = total + self.ends[k, index].astype(F32)
            part[z, column] = total.astype(part.dtype)
            if index == 0:
                src, dst = part.at[z, column], self.relay_in
                self.push(src.at[:, :wide], dst.at[:, :wide], 16, here.to_x)
                self.push(src.at[:, wide:], dst.at[:, wide:], 17, here.to_y)

    def sides(self):
        here, part, z = self.here, self.part, self.here.z
        wide = part.shape[-1] // 2
        for index, cols, fx, fy, to in (
            (17, slice(wide, 2 * wide), 1, 0, here.to_x), (16, slice(0, wide), 0, 1, here.to_y)
        ):
            column = here.column(fx, 0, fy)
            self.pull(self.relay_in.at[:, cols], index)
            total = part[z, column, :, cols].astype(F32) + self.relay_in[:, cols].astype(F32)
            part[z, column, :, cols] = total.astype(part.dtype)
            self.push(part.at[z, column], self.sides_in.at[fy], 18 + fy, to)

    def finish(self):
        here = self.here
        total = self.part[here.z, here.column(0, 0, 0)].astype(F32)
        for index in range(2):
            self.pull(self.sides_in.at[index], 18 + index)
            total = total + self.sides_in[index].astype(F32)
        return total


def normalise(rows_in):
    centre = rows_in - jnp.mean(rows_in, axis=-1, keepdims=True)
    spread = jnp.mean(centre * centre, axis=-1, keepdims=True)
    inverse = lax.rsqrt(spread + EPSILON)
    return centre * inverse, inverse


def normalise_back(grad, unit, inverse):
    return inverse * (
        grad
        - jnp.mean(grad, axis=-1, keepdims=True)
        - unit * jnp.mean(grad * unit, axis=-1, keepdims=True)
    )


def spread_matrix(slot):
    lane = lax.broadcasted_iota(jnp.int32, (128, 768), 0)
    place = lax.broadcasted_iota(jnp.int32, (128, 768), 1)
    if slot is None:
        inside = lax.rem(place, 4 * CHUNK)
        wanted = 32 * (inside // CHUNK) + lax.rem(inside, CHUNK)
    else:
        wanted = 32 * slot + lax.rem(place, CHUNK)
    return jnp.where(lane == wanted, 1.0, 0.0).astype(BF16)


def owner_mask(each, first):
    device = lax.broadcasted_iota(jnp.int32, (32, 768), 0)
    place = lax.broadcasted_iota(jnp.int32, (32, 768), 1)
    return device == first + place // each


def collect(group, matrix, each, first):
    moved = nn(group.astype(BF16), matrix)
    return jnp.sum(jnp.where(owner_mask(each, first), moved, 0.0), axis=0, keepdims=True)


def deal(row, matrix, each, first):
    placed = jnp.where(owner_mask(each, first), row, 0.0)
    high = placed.astype(BF16)
    rest = placed - high.astype(F32)
    middle = rest.astype(BF16)
    low = (rest - middle.astype(F32)).astype(BF16)
    return nt(high, matrix) + nt(middle, matrix) + nt(low, matrix)


def one_hot(value):
    slot = lax.broadcasted_iota(jnp.int32, (16, 128), 0).astype(F32)
    ones = jnp.where(slot == value, 1.0, 0.0).astype(BF16)
    return jnp.concatenate([ones, ones, ones], axis=0)


def live_rows(count, block, number):
    slot = lax.broadcasted_iota(jnp.int32, (number, 1), 0)
    return slot < (count + 1 - block) // 2


def live_bias(count):
    slot = lax.broadcasted_iota(jnp.int32, (256, 1), 0)
    block = slot // 128
    return jnp.where(slot - 128 * block < (count + 1 - block) // 2, 0.0, -1e30)


def half_mask(head):
    return lax.broadcasted_iota(jnp.int32, (1, 128), 1) // HD == head


def fused_kernel(
    lengths, tokens, cotangent, seen, shard_I, shard_O, shard_E, shard_R, table,
    v0, v1, v2, v3, v4, v5, v6, v7, v8,
    layer_out, tokens_grad, grad_I, grad_O, grad_E, grad_R, grad_V, *refs,
):
    s = Store(refs)
    here = Place()
    z, x, c, y = here.z, here.x, here.c, here.y
    own = here.column(0, 0, 0)
    mine, other = pl.ds(2 * y, 2), pl.ds(2 * (1 - y), 2)
    sums = s.SUMS

    gather = [
        (PlaneGather if name == W_Q else Gather)(here, s.G[name], s.GS[name], s.GQ[name], GATHER_X[name])
        for name in TENSORS
    ]
    reduce = []
    for number, (name, cols, landing) in enumerate(PIECES):
        kind = PlaneReduce if name == W_Q else Reduce
        part, *bufs = [s.P[name], s.R1[name], s.R2[name], s.RZ[name], s.RM[name]]
        core = s.RC[landing].at[:, :, : UNITS[name][0]]
        if cols is not None:
            part, *bufs = [ref.at[(*(slice(None),) * (len(ref.shape) - 1), cols)] for ref in (part, *bufs)]
            core = core.at[:, :, :, : cols.stop - cols.start]
        reduce.append(kind(here, part, core, *bufs, s.RS[number], s.RQ[number], REDUCE_X[number]))

    def swap(src, dst, came, index):
        made = remote(src, dst, s.SWS.at[index], s.SWR.at[index], here.to_y)
        return made, remote(came, came, s.SWS.at[index], s.SWR.at[index], here.to_y)

    tok_out, tok_in = swap(tokens.at[other], s.TOK.at[:, y], s.TOK.at[:, 1 - y], 0)
    seen_out, seen_in = swap(s.AWAY, s.SEEN.at[:, y], s.SEEN.at[:, 1 - y], 1)
    cot_out, cot_in = swap(cotangent.at[other], s.INC.at[:, y], s.INC.at[:, 1 - y], 2)
    lay_out, lay_in = swap(s.TOK.at[:, 1 - y], layer_out.at[mine], layer_out.at[other], 3)
    grad_out, grad_in = swap(s.INC.at[:, 1 - y], s.TOK.at[:, y], s.TOK.at[:, 1 - y], 4)
    tok_copy = pltpu.make_async_copy(tokens.at[mine], s.TOK.at[:, y], s.LOC.at[0])
    cot_copy = pltpu.make_async_copy(cotangent.at[mine], s.INC.at[:, y], s.LOC.at[1])
    out_copy = pltpu.make_async_copy(s.TOK.at[:, y], layer_out.at[mine], s.LOC.at[2])
    near_copies = [
        pltpu.make_async_copy(
            s.ENT.at[rows_at(256 * it + 128 * y, 128)], tokens_grad.at[2 * y + it], s.LOC.at[3 + it]
        )
        for it in range(2)
    ]
    far_copies = [
        pltpu.make_async_copy(
            s.ENT.at[rows_at(256 * it + 128 * (1 - y), 128)], tokens_grad.at[2 * (1 - y) + it], s.LOC.at[5 + it]
        )
        for it in range(2)
    ]

    def vector(number):
        return s.ROWS[pl.ds(number, 1), :]

    def start():
        barrier = pltpu.get_barrier_semaphore()
        partners = [here.to_z(1), here.to_z(2), here.to_z(3), here.to_x, here.to_y, here.to_c]
        for device in partners:
            pl.semaphore_signal(barrier, inc=1, device_id=device, device_id_type=MESH)
        tok_copy.start()
        cot_copy.start()
        for name, shard in ((W_I, shard_I), (W_O, shard_O), (W_E, shard_E)):
            whole = shard[...].astype(F32)
            half = whole.shape[1] // 2
            unit = jnp.concatenate([whole[:, :half], whole[:, half:]], axis=0)
            s.G[name][z, own] = unit.astype(BF16)
        s.G[W_R][z, own] = shard_R[0:R_ROWS, :]
        s.G[W_Q][z, own] = shard_R[R_ROWS:96, :]
        s.STAGE[...] = jnp.zeros_like(s.STAGE)
        for number, ref in enumerate((v0, v1, v2, v3, v4, v5, v6, v7)):
            s.STAGE[number : number + 1, 0:CHUNK] = ref[...].astype(F32)
        s.STAGE[8:9, 0 : 4 * CHUNK] = v8[...].astype(F32)
        s.G[VEC][z, own] = jnp.zeros((8, 128), F32)
        for row in range(2):
            joined = s.STAGE[4 * row : 4 * row + 1, :]
            for slot in range(1, 4):
                joined = joined + pltpu.roll(s.STAGE[4 * row + slot : 4 * row + slot + 1, :], 32 * slot, 1)
            s.G[VEC][z, own, row : row + 1, :] = joined
        long_row = s.STAGE[8:9, :]
        lane = lax.broadcasted_iota(jnp.int32, (1, 128), 1)
        joined = jnp.zeros((1, 128), F32)
        for slot in range(4):
            moved = pltpu.roll(long_row, 8 * slot, 1) if slot else long_row
            inside = jnp.logical_and(lane >= 32 * slot, lane < 32 * slot + CHUNK)
            joined = jnp.where(inside, moved, joined)
        s.G[VEC][z, own, 2:3, :] = joined
        for it in range(2):
            s.SEEN[it, y] = jnp.broadcast_to(seen[2 * y + it], (8, 128))
            s.AWAY[it] = jnp.broadcast_to(seen[2 * (1 - y) + it], (8, 128))
        pl.semaphore_wait(barrier, len(partners))

    def vectors():
        for number in range(VECTORS):
            group = s.G[VEC][:, :, number // 4, :].reshape(32, 128)
            s.ROWS[pl.ds(number, 1), :] = collect(group, spread_matrix(number % 4), CHUNK, 0)
        group = s.G[VEC][:, :, 2, :].reshape(32, 128)
        for part in range(4):
            cols = slice(768 * part, 768 * part + 768)
            s.EB[:, cols] = collect(group, spread_matrix(None), 4 * CHUNK, 8 * part)
        s.PB[:, 0:768] = vector(2)
        s.PB[:, 768:1536] = jnp.zeros((1, 768), F32)
        s.PB[:, 1536:2304] = vector(3)
        sums[...] = jnp.zeros_like(sums)
        s.EBG[...] = jnp.zeros_like(s.EBG)

    def first_norm():
        def one(block, carry):
            it, half = block // 2, block % 2
            rows = rows_at(128 * block, 128)
            patch = s.SEEN[it, half][0:1, :].astype(F32)
            frame = jnp.floor((patch + 0.5) * (1.0 / (GRID * GRID)))
            inside = patch - frame * (GRID * GRID)
            line = jnp.floor((inside + 0.5) * (1.0 / GRID))
            across = inside - line * GRID
            place = jnp.concatenate([tn(one_hot(v), table[...]) for v in (frame, line, across)], axis=1)
            entry = s.TOK[it, half].astype(F32) + place
            s.ENT[rows, :] = entry
            unit, _ = normalise(entry)
            normed = (unit * vector(0) + vector(1)).astype(BF16)
            s.XB[rows, :] = normed
            s.NRMT[:, lanes(128 * block, 128)] = normed.T
            return carry

        lax.fori_loop(0, 4, one, 0, unroll=4)

    def spread_rows(name, target):
        buf = s.G[name]
        half = target.shape[1] // 2

        def one(i, carry):
            zz, pair = i // 4, 2 * (i % 4)
            even = buf[zz, pair].astype(F32)
            odd = buf[zz, pair + 1].astype(F32)
            rows = pl.ds(pl.multiple_of(48 * i, 16), 48)
            target[rows, :half] = jnp.concatenate([even[:24], odd[:24]], axis=0).astype(BF16)
            target[rows, half:] = jnp.concatenate([even[24:], odd[24:]], axis=0).astype(BF16)
            return carry

        lax.fori_loop(0, 16, one, 0)

    def project():
        def one(n, carry):
            cols = lanes(1152 * n, 1152)
            s.PRJ[:, cols] = (nn(s.XB[...], s.WI[:, cols]) + s.PB[:, cols]).astype(BF16)
            return carry

        lax.fori_loop(0, 2, one, 0)

    def attend(first, last):
        def one(step, carry):
            it, pair = step // 6, step % 6
            rows = rows_at(256 * it, 256)
            cols = lanes(128 * pair, 128)
            q = s.PRJ[rows, cols]
            k = s.PRJ[rows, lanes(768 + 128 * pair, 128)]
            v = s.PRJ[rows, lanes(1536 + 128 * pair, 128)]
            bias = live_bias(lengths[2 * y + it])
            total = jnp.zeros((128, 256), F32)
            for head in range(2):
                mask = half_mask(head)
                scores = nt(jnp.where(mask, k, 0), q) * SCORE_SCALE + bias
                exponent = jnp.exp(scores - jnp.max(scores, axis=0, keepdims=True))
                attention = exponent * (1.0 / jnp.sum(exponent, axis=0, keepdims=True))
                low = attention.astype(BF16)
                s.ATN[2 * step + head] = low
                total = total + tn(jnp.where(mask, v, 0), low)
            s.ATTT[cols, rows] = total.astype(BF16)
            s.XB[rows, cols] = total.T.astype(BF16)
            return carry

        lax.fori_loop(first, last, one, 0, unroll=3)

    def second_norm():
        def one(it, carry):
            rows = rows_at(256 * it, 256)
            middle = s.ENT[rows, :] + nn(s.XB[rows, :], s.WO[...]) + vector(4)
            s.MID[rows, :] = middle
            unit, _ = normalise(middle)
            second = (unit * vector(5) + vector(6)).astype(BF16)
            s.XB[rows, :] = second
            s.SECT[:, rows] = second.T
            return carry

        lax.fori_loop(0, 2, one, 0, unroll=2)

    def expand(first, last):
        def one(step, carry):
            n, it = step // 2, step % 2
            cols = lanes(768 * n, 768)
            rows = rows_at(256 * it, 256)
            expanded = nn(s.XB[rows, :], s.WE[:, cols]) + s.EB[:, cols]
            normal = 0.5 * (1.0 + lax.erf(expanded * 0.7071067811865476))
            density = jnp.exp(-0.5 * expanded * expanded) * 0.3989422804014327
            s.ACT[rows, cols] = (expanded * normal).astype(BF16)
            s.GP[rows, cols] = (normal + expanded * density).astype(BF16)
            return carry

        lax.fori_loop(first, last, one, 0)

    def take_in():
        def one(block, carry):
            it, half = block // 2, block % 2
            live = live_rows(lengths[2 * y + it], half, 128)
            incoming = jnp.where(live, s.INC[it, half].astype(F32), 0.0)
            s.INC[it, half] = incoming.astype(BF16)
            sums[7:8, :] += jnp.sum(incoming, axis=0, keepdims=True)
            return carry

        lax.fori_loop(0, 4, one, 0)

    def reduce_weight_grad(xx):
        def one(zz, carry):
            moved = s.ACT[:, lanes(768 * zz + 384 * xx, 384)].T
            part = nn(moved, s.INC[...].reshape(512, 768))
            units = part.reshape(4, 96, 768).astype(BF16)
            s.P[W_R][zz, pl.ds(4 * xx, 4)] = units[:, :R_ROWS]
            s.P[W_Q][zz, pl.ds(4 * xx, 4)] = units[:, R_ROWS:]
            return carry

        lax.fori_loop(0, 4, one, 0, unroll=2)

    def reduce_rows(zz):
        return jnp.concatenate([s.G[W_R][zz], s.G[W_Q][zz]], axis=1).reshape(768, 768)

    def expanded_grad(first, last):
        def one(step, carry):
            zz, it = step // 2, step % 2
            rows = rows_at(256 * it, 256)
            cols = lanes(768 * zz, 768)
            incoming = s.INC[it].reshape(256, 768)
            grad = (nt(incoming, reduce_rows(zz)) * s.GP[rows, cols].astype(F32)).astype(BF16)
            s.GP[rows, cols] = grad
            s.EBG[:, cols] += jnp.sum(grad.astype(F32), axis=0, keepdims=True)
            return carry

        lax.fori_loop(first, last, one, 0, unroll=4)

    def weight_grad(name, moved, grad, first, last):
        part, wide = s.P[name], 384
        half = UNITS[name][1]

        def one(step, carry):
            n, m = step // 2, step % 2
            left = grad[:, lanes(wide * n, wide)]
            right = grad[:, lanes(half + wide * n, wide)]
            block = nn(moved[rows_at(384 * m, 384), :], jnp.concatenate([left, right], axis=1))
            for j in range(8):
                for side in range(2):
                    rows = slice(48 * j + 24 * side, 48 * j + 24 * side + 24)
                    unit = jnp.concatenate([block[rows, :wide], block[rows, wide:]], axis=0)
                    part[2 * m + j // 4, 2 * (j % 4) + side, :, lanes(wide * n, wide)] = unit.astype(BF16)
            return carry

        if first == 0:
            gather[name].drain()
        lax.fori_loop(2 * first, 2 * last, one, 0, unroll=2)

    def finish_rows():
        def one(it, carry):
            rows = rows_at(256 * it, 256)
            out = s.MID[rows, :] + vector(7)
            for zz in range(4):
                out = out + nn(s.ACT[rows, 768 * zz : 768 * zz + 768], reduce_rows(zz))
            for half in range(2):
                live = live_rows(lengths[2 * y + it], half, 128)
                s.TOK[it, half] = jnp.where(live, out[128 * half : 128 * half + 128], 0.0).astype(BF16)
            return carry

        tok_out.wait_send()
        lax.fori_loop(0, 2, one, 0)
        out_copy.start()

    def middle_back():
        def one(it, carry):
            rows = rows_at(256 * it, 256)
            grad = nt(s.GP[rows, :], s.WE[...])
            unit, inverse = normalise(s.MID[rows, :])
            sums[5:6, :] += jnp.sum(grad * unit, axis=0, keepdims=True)
            sums[6:7, :] += jnp.sum(grad, axis=0, keepdims=True)
            incoming = s.INC[it].reshape(256, 768).astype(F32)
            middle_grad = incoming + normalise_back(grad * vector(5), unit, inverse)
            s.MID[rows, :] = middle_grad
            branch = middle_grad.astype(BF16)
            s.XB[rows, :] = branch
            sums[4:5, :] += jnp.sum(branch.astype(F32), axis=0, keepdims=True)
            return carry

        lax.fori_loop(0, 2, one, 0)

    def attended_back():
        def one(it, carry):
            rows = rows_at(256 * it, 256)
            s.XB[rows, :] = nt(s.XB[rows, :], s.WO[...]).astype(BF16)
            return carry

        lax.fori_loop(0, 2, one, 0, unroll=2)

    def attend_back(first, last):
        def one(step, carry):
            it, pair = step // 6, step % 6
            rows = rows_at(256 * it, 256)
            cols = lanes(128 * pair, 128)
            k_cols, v_cols = lanes(768 + 128 * pair, 128), lanes(1536 + 128 * pair, 128)
            q = s.PRJ[rows, cols]
            k = s.PRJ[rows, k_cols]
            v = s.PRJ[rows, v_cols]
            grad = s.XB[rows, cols]
            query_grad = jnp.zeros((128, 256), F32)
            key_grad = jnp.zeros((256, 128), F32)
            value_grad = jnp.zeros((256, 128), F32)
            for head in range(2):
                mask = half_mask(head)
                mine_grad = jnp.where(mask, grad, 0)
                weight_back = nt(v, mine_grad)
                low = s.ATN[2 * step + head]
                attention = low.astype(F32)
                inner = jnp.sum(attention * weight_back, axis=0, keepdims=True)
                scores_grad = (attention * (weight_back - inner)).astype(BF16)
                query_grad = query_grad + tn(jnp.where(mask, k, 0), scores_grad)
                key_grad = key_grad + nn(scores_grad, jnp.where(mask, q, 0))
                value_grad = value_grad + nn(low, mine_grad)
            query_low = (query_grad * SCORE_SCALE).T.astype(BF16)
            value_low = value_grad.astype(BF16)
            s.PRJ[rows, cols] = query_low
            s.PRJ[rows, k_cols] = (key_grad * SCORE_SCALE).astype(BF16)
            s.PRJ[rows, v_cols] = value_low
            sums[2:3, cols] += jnp.sum(query_low.astype(F32), axis=0, keepdims=True)
            sums[3:4, cols] += jnp.sum(value_low.astype(F32), axis=0, keepdims=True)
            return carry

        lax.fori_loop(first, last, one, 0, unroll=6)

    def entry_back(half):
        rows = [rows_at(256 * it + 128 * half, 128) for it in range(2)]

        def both(ref):
            return jnp.concatenate([ref[r, :] for r in rows], axis=0)

        grad = nt(both(s.PRJ), s.WI[...])
        unit, inverse = normalise(both(s.ENT))
        sums[0:1, :] += jnp.sum(grad * unit, axis=0, keepdims=True)
        sums[1:2, :] += jnp.sum(grad, axis=0, keepdims=True)
        return rows, both(s.MID) + normalise_back(grad * vector(0), unit, inverse)

    def entry_back_far():
        _, out = entry_back(1 - y)
        cot_out.wait_send()
        for it in range(2):
            s.INC[it, 1 - y] = out[128 * it : 128 * it + 128].astype(BF16)

    def entry_back_near():
        rows, out = entry_back(y)
        for it in range(2):
            s.ENT[rows[it], :] = out[128 * it : 128 * it + 128]
        for copy in near_copies:
            copy.start()

    def deal_sums():
        group = None
        for number in range(VECTORS):
            dealt = deal(sums[number : number + 1, :], spread_matrix(number % 4), CHUNK, 0)
            group = dealt if number % 4 == 0 else group + dealt
            if number % 4 == 3:
                s.P[VEC][:, :, number // 4, :] = group.reshape(4, 8, 128)
        group = jnp.zeros((32, 128), F32)
        for part in range(4):
            row = s.EBG[:, 768 * part : 768 * part + 768]
            group = group + deal(row, spread_matrix(None), 4 * CHUNK, 8 * part)
        s.P[VEC][:, :, 2, :] = group.reshape(4, 8, 128)
        for row in range(3, 8):
            s.P[VEC][:, :, row, :] = jnp.zeros((4, 8, 128), F32)

    def give_spare(index):
        pl.semaphore_signal(s.SPARE.at[index], inc=1, device_id=here.to_c, device_id_type=MESH)

    def place_grad(number, ref):
        cols = PIECES[number][1]
        half = ref.shape[1] // 2
        if cols is None:
            cols = slice(0, half)
        total = reduce[number].finish()
        ref[:, cols] = total[:24]
        ref[:, half + cols.start : half + cols.stop] = total[24:]

    def take_grad():
        grad_in.wait_recv()
        for it in range(2):
            s.ENT[rows_at(256 * it + 128 * (1 - y), 128), :] = s.TOK[it, 1 - y].astype(F32)
        for copy in far_copies:
            copy.start()

    def free_tokens():
        lay_out.wait_send()
        out_copy.wait()
        lay_in.wait_recv()
        pl.semaphore_signal(s.SPARE.at[4], inc=1, device_id=here.to_y, device_id_type=MESH)

    def send_grad():
        pl.semaphore_wait(s.SPARE.at[4], 1)
        grad_out.start()

    def end():
        for made in (seen_out, grad_out):
            made.wait_send()
        for copy in near_copies + far_copies:
            copy.wait()
        for one in (*gather, *reduce):
            one.drain()

    start()
    gather[W_I].begin_x()
    gather[W_O].begin_x()
    gather[W_E].begin_y()
    gather[W_Q].begin_x()
    gather[W_E].begin_x()
    gather[W_I].begin_y()
    gather[W_I].begin_z()
    gather[W_Q].begin_y()
    gather[W_I].relay(0)
    gather[W_O].begin_y()
    tok_out.start()
    gather[W_I].pass_on(2)
    gather[VEC].begin_z()
    gather[W_I].pass_on(1)
    gather[W_O].begin_z()
    gather[VEC].begin_y()
    gather[W_I].pass_on(3)
    gather[W_I].own_to_core()
    gather[W_E].begin_z()
    gather[VEC].begin_x()
    gather[VEC].pass_on(2)
    seen_out.start()
    gather[W_E].relay(0)
    gather[VEC].pass_on(3)
    gather[W_O].pass_on(1)
    gather[VEC].pass_on(1)
    gather[W_O].pass_on(2)
    gather[W_Q].relay()
    tok_copy.wait()
    tok_in.wait_recv()
    gather[W_I].relay(2)
    gather[VEC].relay(0)
    gather[W_O].pass_on(3)
    gather[VEC].relay(3)
    gather[W_I].relay(3)
    gather[W_I].relay(1)
    gather[VEC].relay(1)
    gather[VEC].own_to_core()
    gather[VEC].relay(2)
    gather[W_I].sides_to_core()
    gather[W_O].relay(0)
    gather[W_E].pass_on(2)
    gather[W_R].begin_z()
    gather[W_E].pass_on(1)
    gather[VEC].sides_to_core()
    gather[W_E].pass_on(3)
    gather[W_O].relay(1)
    gather[W_O].relay(3)
    gather[W_Q].pass_z(1)
    gather[VEC].corner()
    gather[VEC].from_core()
    seen_in.wait_recv()
    gather[W_R].begin_y()
    vectors()
    gather[W_O].relay(2)
    gather[W_I].corner()
    gather[W_O].sides_to_core()
    gather[W_Q].corner()
    gather[W_I].from_core()
    gather[W_Q].pass_z(2)
    gather[W_E].relay(1)
    spread_rows(W_I, s.WI)
    gather[W_O].own_to_core()
    first_norm()
    gather[W_E].own_to_core()
    gather[W_E].relay(2)
    gather[W_R].begin_x()
    gather[W_Q].to_core(1)
    gather[W_R].pass_on(2)
    project()
    gather[W_O].corner()
    gather[W_E].relay(3)
    attend(0, 6)
    cot_out.start()
    gather[W_Q].pass_z(3)
    gather[W_E].sides_to_core()
    gather[W_O].from_core()
    gather[W_Q].own_along_z()
    attend(6, 12)
    gather[W_E].corner()
    gather[W_R].pass_on(3)
    spread_rows(W_O, s.WO)
    second_norm()
    gather[W_Q].to_core(2)
    gather[W_R].relay(0)
    gather[W_Q].to_core(3)
    gather[W_R].pass_on(1)
    gather[W_R].own_to_core()
    gather[W_R].relay(2)
    gather[W_E].from_core()
    spread_rows(W_E, s.WE)
    expand(0, 4)
    gather[W_Q].pass_z(0)
    expand(4, 8)
    gather[W_R].relay(1)
    gather[W_R].relay(3)
    cot_copy.wait()
    cot_in.wait_recv()
    gather[W_Q].to_core(0)
    gather[W_R].sides_to_core()
    take_in()
    reduce_weight_grad(1 - x)
    reduce[D_R].core_send(None, 0, 2)
    gather[W_R].corner()
    reduce_weight_grad(x)
    reduce[D_R].core_add(0)
    reduce[D_R].core_send(None, 2, 4)
    reduce[D_Q].core_send(None, 2, 4)
    gather[W_Q].from_core()
    reduce[D_R].core_add(1)
    reduce[D_Q].core_send(None, 0, 2)
    gather[W_R].from_core()
    expanded_grad(0, 4)
    reduce[D_R].core_add(2)
    expanded_grad(4, 8)
    weight_grad(W_E, s.SECT, s.GP, 0, 2)
    reduce[D_Q].core_add(0)
    reduce[D_R].core_add(3)
    give_spare(0)
    reduce[D_R].relay()
    reduce[D_EA].core_send(s.SPARE.at[0])
    weight_grad(W_E, s.SECT, s.GP, 2, 4)
    reduce[D_EA].core_add(0)
    finish_rows()
    lay_out.start()
    reduce[D_Q].core_add(1)
    reduce[D_EA].core_add(1)
    reduce[D_Q].core_add(2)
    reduce[D_Q].pass_z(0)
    reduce[D_Q].core_add(3)
    give_spare(1)
    reduce[D_EB].core_send(s.SPARE.at[1])
    middle_back()
    reduce[D_EB].core_add(0)
    reduce[D_EB].core_add(1)
    weight_grad(W_O, s.ATTT, s.XB, 0, 1)
    reduce[D_EA].core_add(2)
    attended_back()
    reduce[D_EA].relay()
    reduce[D_O].core_send()
    attend_back(0, 6)
    attend_back(6, 12)
    reduce[D_EB].core_add(2)
    reduce[D_EB].relay()
    weight_grad(W_I, s.NRMT, s.PRJ, 0, 2)
    reduce[D_O].core_add(0)
    weight_grad(W_I, s.NRMT, s.PRJ, 2, 3)
    reduce[D_EA].core_add(3)
    give_spare(2)
    reduce[D_IA].core_send(s.SPARE.at[2])
    reduce[D_Q].pass_z(2)
    reduce[D_O].core_add(1)
    reduce[D_Q].pass_z(1)
    reduce[D_EA].sides()
    free_tokens()
    reduce[D_IA].core_add(0)
    reduce[D_EB].core_add(3)
    give_spare(3)
    reduce[D_R].sides()
    entry_back_far()
    reduce[D_O].core_add(2)
    reduce[D_IA].core_add(1)
    reduce[D_Q].pass_z(3)
    reduce[D_IB].core_send(s.SPARE.at[3])
    reduce[D_IA].core_add(2)
    reduce[D_O].relay()
    entry_back_near()
    reduce[D_IB].core_add(0)
    reduce[D_R].pass_z()
    reduce[D_EB].sides()
    reduce[D_IA].relay()
    deal_sums()
    reduce[D_V].core_send()
    reduce[D_V].core_add(0)
    reduce[D_EB].pass_z()
    reduce[D_V].core_add(1)
    reduce[D_O].core_add(3)
    reduce[D_IB].core_add(1)
    reduce[D_IB].core_add(2)
    reduce[D_IA].core_add(3)
    reduce[D_IB].core_add(3)
    reduce[D_EA].pass_z()
    reduce[D_V].core_add(2)
    reduce[D_Q].relay()
    reduce[D_O].sides()
    reduce[D_IB].relay()
    reduce[D_V].core_add(3)
    reduce[D_IA].sides()
    reduce[D_V].relay()
    send_grad()
    grad_R[0:R_ROWS, :] = reduce[D_R].finish()
    reduce[D_IA].pass_z()
    reduce[D_O].pass_z()
    reduce[D_IB].sides()
    reduce[D_V].sides()
    place_grad(D_IA, grad_I)
    place_grad(D_EA, grad_E)
    reduce[D_V].pass_z()
    reduce[D_Q].sides()
    place_grad(D_O, grad_O)
    reduce[D_IB].pass_z()
    grad_V[...] = reduce[D_V].finish()
    place_grad(D_IB, grad_I)
    take_grad()
    place_grad(D_EB, grad_E)
    grad_R[R_ROWS:96, :] = reduce[D_Q].finish()
    end()


UNITS = ((48, 1152), (48, 384), (48, 1536), (R_ROWS, 768), (Q_ROWS, 768), (8, 128))


PIECES = (
    (W_I, slice(0, 768), 1),
    (W_I, slice(768, 1152), 2),
    (W_O, None, 0),
    (W_E, slice(0, 768), 1),
    (W_E, slice(768, 1536), 2),
    (W_R, None, 1),
    (W_Q, None, 2),
    (VEC, None, 3),
)


def scratch_list():
    dma, vmem = pltpu.SemaphoreType.DMA, pltpu.VMEM
    shapes = dict(
        SWS=dma((5,)),
        SWR=dma((5,)),
        LOC=dma((7,)),
        SPARE=pltpu.SemaphoreType.REGULAR((5,)),
        TOK=vmem((2, 2, 128, 768), BF16),
        INC=vmem((2, 2, 128, 768), BF16),
        SEEN=vmem((2, 2, 8, 128), jnp.int32),
        AWAY=vmem((2, 8, 128), jnp.int32),
        ROWS=vmem((8, 768), F32),
        STAGE=vmem((16, 128), F32),
        EB=vmem((1, 3072), F32),
        PB=vmem((1, 2304), F32),
        SUMS=vmem((8, 768), F32),
        EBG=vmem((1, 3072), F32),
        WI=vmem((768, 2304), BF16),
        WO=vmem((768, 768), BF16),
        WE=vmem((768, 3072), BF16),
        ENT=vmem((512, 768), F32),
        MID=vmem((512, 768), F32),
        XB=vmem((512, 768), BF16),
        NRMT=vmem((768, 512), BF16),
        ATTT=vmem((768, 512), BF16),
        SECT=vmem((768, 512), BF16),
        PRJ=vmem((512, 2304), BF16),
        ATN=vmem((24, 256, 256), BF16),
        ACT=vmem((512, 3072), BF16),
        GP=vmem((512, 3072), BF16),
    )
    many = dict(G=[], GS=[], GQ=[], P=[], RC=[], R1=[], R2=[], RZ=[], RM=[], RS=[], RQ=[])
    for name in TENSORS:
        kind = F32 if name == VEC else BF16
        unit = UNITS[name]
        plane = name == W_Q
        many["G"].append(vmem((4, 8, *unit), kind))
        many["GS"].append(dma((SEMS,)))
        many["GQ"].append(dma((SEMS,)))
        if name in (W_R, W_Q, VEC):
            many["P"].append(vmem((4, 8, *unit), kind))
        if name not in (W_I, W_E):
            room = (max(unit[0], 48), unit[1]) if name == W_R else unit
            many["RC"].append(vmem((4, 4, *room), kind))
        many["R1"].append(vmem(unit if plane else (4, *unit), kind))
        many["R2"].append(vmem((2, *unit) if plane else (4, 2, *unit), kind))
        many["RZ"].append(vmem((3, 4, *unit) if plane else (3, *unit), kind))
        many["RM"].append(vmem((4, *unit) if plane else unit, kind))
    for _ in SUMS:
        many["RS"].append(dma((SEMS,)))
        many["RQ"].append(dma((SEMS,)))
    return shapes, many


class Store:
    def __init__(self, refs):
        shapes, many = scratch_list()
        refs = list(refs)
        for name in shapes:
            setattr(self, name, refs.pop(0))
        for name, listed in many.items():
            setattr(self, name, [refs.pop(0) for _ in listed])
        self.P = self.G[:3] + self.P


def position_table():
    step = np.arange(16, dtype=np.float64)[:, None]
    channel = np.arange(256)
    angle = step * np.power(10000.0, -(channel // 2) / 128.0)
    whole = np.where(channel % 2 == 0, np.sin(angle), np.cos(angle)).astype(np.float32)
    high = whole.astype(jnp.bfloat16)
    rest = whole - high.astype(np.float32)
    middle = rest.astype(jnp.bfloat16)
    low = (rest - middle.astype(np.float32)).astype(jnp.bfloat16)
    return np.concatenate([high, middle, low], axis=0)


def hand_over(*refs):
    given, vectors_in, results, rows = refs[:6], refs[6], refs[7:13], refs[13:22]
    holds, sems = refs[22:28], refs[28]
    steps = []
    for src, hold, dst in zip(given, holds, results):
        parts = src.shape[0] if len(src.shape) == 3 else 1
        for part in range(parts):
            where = part if parts > 1 else slice(None)
            number = len(steps)
            steps.append((
                pltpu.make_async_copy(src.at[where], hold.at[where], sems.at[0, number]),
                pltpu.make_async_copy(hold.at[where], dst.at[where], sems.at[1, number]),
            ))
    for first, _ in steps:
        first.start()
    for number in range(VECTORS):
        slot = number % 4
        rows[number][...] = vectors_in[number // 4 : number // 4 + 1, 32 * slot : 32 * slot + CHUNK]
    row = vectors_in[2:3, :]
    lane = lax.broadcasted_iota(jnp.int32, (1, 128), 1)
    joined = row
    for slot in range(1, 4):
        joined = jnp.where(lane >= CHUNK * slot, pltpu.roll(row, 128 - 8 * slot, 1), joined)
    rows[8][...] = joined[:, : 4 * CHUNK]
    for first, second in steps:
        first.wait()
        second.start()
    for _, second in steps:
        second.wait()


def fused_body(
    tokens, visible, lengths, first_gain, first_shift, input_weight, query_bias, value_bias,
    output_weight, output_bias, second_gain, second_shift, expand_weight, expand_bias,
    reduce_weight, reduce_bias, cotangent,
):
    hbm = pl.BlockSpec(memory_space=pl.ANY)
    vmem = pl.BlockSpec(memory_space=pltpu.VMEM)
    smem = pl.BlockSpec(memory_space=pltpu.SMEM)
    shapes, many = scratch_list()
    results = [
        jax.ShapeDtypeStruct((4, 128, 768), BF16),
        jax.ShapeDtypeStruct((4, 128, 768), F32),
        jax.ShapeDtypeStruct(input_weight.shape, F32),
        jax.ShapeDtypeStruct(output_weight.shape, F32),
        jax.ShapeDtypeStruct(expand_weight.shape, F32),
        jax.ShapeDtypeStruct(reduce_weight.shape, F32),
        jax.ShapeDtypeStruct((8, 128), F32),
    ]
    layer_out, tokens_grad, grad_I, grad_O, grad_E, grad_R, grad_V = pl.pallas_call(
        fused_kernel,
        name="layer",
        out_shape=results,
        in_specs=[smem, hbm, hbm] + [vmem] * 15,
        out_specs=[hbm, hbm, vmem, vmem, vmem, vmem, vmem],
        scratch_shapes=[*shapes.values(), *(shape for listed in many.values() for shape in listed)],
        compiler_params=pltpu.CompilerParams(
            collective_id=0, has_side_effects=True, vmem_limit_bytes=VMEM_BYTES
        ),
    )(
        lengths, tokens[:, 0], cotangent[:, 0], visible, input_weight, output_weight, expand_weight,
        reduce_weight, jnp.asarray(position_table()),
        *(
            vector.reshape(1, -1)
            for vector in (
                first_gain, first_shift, query_bias, value_bias, output_bias, second_gain, second_shift,
                reduce_bias, expand_bias,
            )
        ),
    )
    parts = (layer_out, tokens_grad, grad_I, grad_O, grad_E, grad_R)
    row, long_row = jax.ShapeDtypeStruct((1, CHUNK), F32), jax.ShapeDtypeStruct((1, 4 * CHUNK), F32)
    layer_out, tokens_grad, grad_I, grad_O, grad_E, grad_R, *rows = pl.pallas_call(
        hand_over,
        name="hand_over",
        out_shape=[jax.ShapeDtypeStruct(part.shape, part.dtype) for part in parts] + [row] * VECTORS + [long_row],
        in_specs=[hbm] * 6 + [vmem],
        out_specs=[hbm] * 6 + [vmem] * 9,
        scratch_shapes=[pltpu.VMEM(part.shape, part.dtype) for part in parts] + [pltpu.SemaphoreType.DMA((2, 12))],
    )(*parts, grad_V)
    dealt = [row.reshape(-1) for row in rows]
    return (
        layer_out[:, None], tokens_grad[:, None], dealt[0], dealt[1], grad_I, dealt[2], dealt[3], grad_O,
        dealt[4], dealt[5], dealt[6], grad_E, dealt[8], grad_R, dealt[7],
    )


VMEM_BYTES = 67000000


def solution(mesh):
    in_specs = (
        P("items", "seq", None, None),
        P("items", "seq", None),
        P("items"),
        P(("items", "seq")),
        P(("items", "seq")),
        P(("items", "seq"), None),
        P(("items", "seq")),
        P(("items", "seq")),
        P(("items", "seq"), None),
        P(("items", "seq")),
        P(("items", "seq")),
        P(("items", "seq")),
        P(("items", "seq"), None),
        P(("items", "seq")),
        P(("items", "seq"), None),
        P(("items", "seq")),
        P("items", "seq", None, None),
    )
    out_specs = (
        P("items", "seq", None, None),
        P("items", "seq", None, None),
        P(("items", "seq")),
        P(("items", "seq")),
        P(("items", "seq"), None),
        P(("items", "seq")),
        P(("items", "seq")),
        P(("items", "seq"), None),
        P(("items", "seq")),
        P(("items", "seq")),
        P(("items", "seq")),
        P(("items", "seq"), None),
        P(("items", "seq")),
        P(("items", "seq"), None),
        P(("items", "seq")),
    )
    sizes = (mesh.shape["items"], mesh.shape["seq"])
    chosen = fused_body if sizes == (Z_SIZE * 4, 2) else general_body
    return jax.shard_map(chosen, mesh=mesh, in_specs=in_specs, out_specs=out_specs, check_vma=False)
```

```python
import functools

import jax
import jax.numpy as jnp
import numpy as np
from jax import lax
from jax.experimental import pallas as pl
from jax.experimental.pallas import tpu as pltpu
from jax.sharding import PartitionSpec as P

HD = 64
GRID = 14
MICRO = 2
ITEMS_MB = 2


EPSILON = 1e-06
SCORE_SCALE = 0.125


def layer_norm(rows_in, gain, shift):
    centre = rows_in - jnp.mean(rows_in, axis=-1, keepdims=True)
    spread = jnp.mean(centre * centre, axis=-1, keepdims=True)
    return centre * lax.rsqrt(spread + EPSILON) * gain + shift


def gelu_exact(value_in):
    return jax.nn.gelu(value_in, approximate=False)


def positions(index, model_width):
    channel = jnp.arange(model_width)
    portion = 3 * channel // model_width
    frequency = jnp.power(10000.0, -(channel % 256 // 2).astype(jnp.float32) / 128.0)
    which_frame = index // (GRID * GRID)
    which_row = index % (GRID * GRID) // GRID
    which_column = index % GRID
    coordinate = jnp.where(
        portion == 0,
        which_frame[..., None],
        jnp.where(portion == 1, which_row[..., None], which_column[..., None]),
    )
    angle = coordinate.astype(jnp.float32) * frequency
    return jnp.where(channel % 2 == 0, jnp.sin(angle), jnp.cos(angle))


def contract_rows(left, right):
    return lax.dot_general(
        left, right, (((0,), (0,)), ((), ())), preferred_element_type=jnp.float32
    )


def against(left, right):
    return lax.dot_general(
        left, right, (((1,), (1,)), ((), ())), preferred_element_type=jnp.float32
    )


def row_masks(lengths, block_rows, block_number):
    counts = (lengths + 1 - block_number) // 2
    return jnp.arange(block_rows)[None, :] < counts[:, None]


def micro_batch(gathered, tokens, visible, lengths, cotangent, seq_place):
    (
        first_gain,
        first_shift,
        input_weight,
        query_bias,
        value_bias,
        output_weight,
        output_bias,
        second_gain,
        second_shift,
        expand_weight,
        expand_bias,
        reduce_weight,
        reduce_bias,
    ) = gathered
    item_count, block_rows, model_width = tokens.shape
    head_count = model_width // HD
    total_rows = item_count * block_rows
    (
        first_gain,
        first_shift,
        query_bias,
        value_bias,
        output_bias,
        second_gain,
        second_shift,
        expand_bias,
        reduce_bias,
    ) = (
        vector.astype(jnp.float32)
        for vector in (
            first_gain,
            first_shift,
            query_bias,
            value_bias,
            output_bias,
            second_gain,
            second_shift,
            expand_bias,
            reduce_bias,
        )
    )
    query_live = row_masks(lengths, block_rows, seq_place).reshape(total_rows, 1)
    key_live = jnp.concatenate(
        [row_masks(lengths, block_rows, 0), row_masks(lengths, block_rows, 1)], axis=1
    )
    key_mask = key_live[:, None, None, :]
    entry = tokens.reshape(total_rows, model_width).astype(jnp.float32) + positions(
        visible.reshape(total_rows), model_width
    )
    normed, first_pull = jax.vjp(layer_norm, entry, first_gain, first_shift)
    normed_low = normed.astype(jnp.bfloat16)
    joined_bias = jnp.concatenate([query_bias, jnp.zeros_like(query_bias), value_bias])
    projected = (
        jnp.dot(normed_low, input_weight, preferred_element_type=jnp.float32) + joined_bias
    ).astype(jnp.bfloat16)
    queries = projected[:, :model_width].reshape(item_count, block_rows, head_count, HD)
    keys_here = projected[:, model_width : 2 * model_width].reshape(
        item_count, block_rows, model_width
    )
    values_here = projected[:, 2 * model_width :].reshape(item_count, block_rows, model_width)
    keys_all, values_all = (
        lax.all_gather(keys_here, "seq", axis=1, tiled=True),
        lax.all_gather(values_here, "seq", axis=1, tiled=True),
    )
    keys_all = keys_all.reshape(item_count, 2 * block_rows, head_count, HD)
    values_all = values_all.reshape(item_count, 2 * block_rows, head_count, HD)
    scores = (
        jnp.einsum("cqhd,ckhd->chqk", queries, keys_all, preferred_element_type=jnp.float32)
        * SCORE_SCALE
    )
    scores = jnp.where(key_mask, scores, -1e30)
    row_max = jnp.max(scores, axis=-1, keepdims=True)
    exponent = jnp.exp(scores - row_max)
    row_total = jnp.sum(exponent, axis=-1, keepdims=True)
    attention_low = (exponent / row_total).astype(jnp.bfloat16)
    log_total = row_max + jnp.log(row_total)
    attended = jnp.einsum(
        "chqk,ckhd->cqhd", attention_low, values_all, preferred_element_type=jnp.float32
    )
    attended = attended.reshape(total_rows, model_width).astype(jnp.bfloat16)
    middle = (
        entry + jnp.dot(attended, output_weight, preferred_element_type=jnp.float32) + output_bias
    )
    second, second_pull = jax.vjp(layer_norm, middle, second_gain, second_shift)
    second_low = second.astype(jnp.bfloat16)
    expanded = jnp.dot(second_low, expand_weight, preferred_element_type=jnp.float32) + expand_bias
    activated, gelu_pull = jax.vjp(gelu_exact, expanded)
    activated_low = activated.astype(jnp.bfloat16)
    result = (
        middle
        + jnp.dot(activated_low, reduce_weight, preferred_element_type=jnp.float32)
        + reduce_bias
    )
    layer_out = jnp.where(query_live, result, 0.0).astype(jnp.bfloat16)
    incoming = jnp.where(
        query_live, cotangent.reshape(total_rows, model_width).astype(jnp.float32), 0.0
    )
    incoming_low = incoming.astype(jnp.bfloat16)
    reduce_weight_grad = contract_rows(activated_low, incoming_low)
    reduce_bias_grad = jnp.sum(incoming, axis=0)
    activated_grad = against(incoming_low, reduce_weight)
    expanded_grad = gelu_pull(activated_grad)[0].astype(jnp.bfloat16)
    expand_weight_grad = contract_rows(second_low, expanded_grad)
    expand_bias_grad = jnp.sum(expanded_grad.astype(jnp.float32), axis=0)
    second_grad = against(expanded_grad, expand_weight)
    middle_part, second_gain_grad, second_shift_grad = second_pull(second_grad)
    middle_grad = incoming + middle_part
    branch_grad = middle_grad.astype(jnp.bfloat16)
    output_weight_grad = contract_rows(attended, branch_grad)
    output_bias_grad = jnp.sum(branch_grad.astype(jnp.float32), axis=0)
    attended_grad = against(branch_grad, output_weight).astype(jnp.bfloat16)
    attended_grad = attended_grad.reshape(item_count, block_rows, head_count, HD)
    scores = (
        jnp.einsum("cqhd,ckhd->chqk", queries, keys_all, preferred_element_type=jnp.float32)
        * SCORE_SCALE
    )
    scores = jnp.where(key_mask, scores, -1e30)
    attention_full = jnp.exp(scores - log_total)
    attention_low = attention_full.astype(jnp.bfloat16)
    weight_grad = jnp.einsum(
        "cqhd,ckhd->chqk", attended_grad, values_all, preferred_element_type=jnp.float32
    )
    row_inner = jnp.sum(attention_full * weight_grad, axis=-1, keepdims=True)
    scores_grad = (attention_full * (weight_grad - row_inner)).astype(jnp.bfloat16)
    query_grad = (
        jnp.einsum("chqk,ckhd->cqhd", scores_grad, keys_all, preferred_element_type=jnp.float32)
        * SCORE_SCALE
    )
    key_terms = (
        jnp.einsum("chqk,cqhd->ckhd", scores_grad, queries, preferred_element_type=jnp.float32)
        * SCORE_SCALE
    )
    value_terms = jnp.einsum(
        "chqk,cqhd->ckhd", attention_low, attended_grad, preferred_element_type=jnp.float32
    )
    key_grad, value_grad = (
        lax.psum_scatter(
            key_terms.reshape(item_count, 2 * block_rows, model_width).astype(jnp.bfloat16),
            "seq",
            scatter_dimension=1,
            tiled=True,
        ).astype(jnp.float32),
        lax.psum_scatter(
            value_terms.reshape(item_count, 2 * block_rows, model_width).astype(jnp.bfloat16),
            "seq",
            scatter_dimension=1,
            tiled=True,
        ).astype(jnp.float32),
    )
    projected_grad = jnp.concatenate(
        [
            query_grad.reshape(total_rows, model_width),
            key_grad.reshape(total_rows, model_width),
            value_grad.reshape(total_rows, model_width),
        ],
        axis=1,
    ).astype(jnp.bfloat16)
    input_weight_grad = contract_rows(normed_low, projected_grad)
    projected_sums = jnp.sum(projected_grad.astype(jnp.float32), axis=0)
    query_bias_grad = projected_sums[:model_width]
    value_bias_grad = projected_sums[2 * model_width :]
    normed_grad = against(projected_grad, input_weight)
    entry_part, first_gain_grad, first_shift_grad = first_pull(normed_grad)
    tokens_grad = middle_grad + entry_part
    grads = (
        first_gain_grad,
        first_shift_grad,
        input_weight_grad,
        query_bias_grad,
        value_bias_grad,
        output_weight_grad,
        output_bias_grad,
        second_gain_grad,
        second_shift_grad,
        expand_weight_grad,
        expand_bias_grad,
        reduce_weight_grad,
        reduce_bias_grad,
    )
    return (layer_out, tokens_grad, grads)


def general_body(
    tokens,
    visible,
    lengths,
    first_gain,
    first_shift,
    input_weight,
    query_bias,
    value_bias,
    output_weight,
    output_bias,
    second_gain,
    second_shift,
    expand_weight,
    expand_bias,
    reduce_weight,
    reduce_bias,
    cotangent,
):
    shards = (
        first_gain,
        first_shift,
        input_weight,
        query_bias,
        value_bias,
        output_weight,
        output_bias,
        second_gain,
        second_shift,
        expand_weight,
        expand_bias,
        reduce_weight,
        reduce_bias,
    )
    seq_place = lax.axis_index("seq")
    block_rows = tokens.shape[2]
    model_width = tokens.shape[3]
    outputs_list = []
    gradients_list = []
    totals = None
    for micro_index in range(MICRO):
        first_item = micro_index * ITEMS_MB
        last_item = first_item + ITEMS_MB
        gathered = (
            lax.all_gather(shards[0], ("items", "seq"), axis=0, tiled=True),
            lax.all_gather(shards[1], ("items", "seq"), axis=0, tiled=True),
            lax.all_gather(shards[2], ("items", "seq"), axis=0, tiled=True),
            lax.all_gather(shards[3], ("items", "seq"), axis=0, tiled=True),
            lax.all_gather(shards[4], ("items", "seq"), axis=0, tiled=True),
            lax.all_gather(shards[5], ("items", "seq"), axis=0, tiled=True),
            lax.all_gather(shards[6], ("items", "seq"), axis=0, tiled=True),
            lax.all_gather(shards[7], ("items", "seq"), axis=0, tiled=True),
            lax.all_gather(shards[8], ("items", "seq"), axis=0, tiled=True),
            lax.all_gather(shards[9], ("items", "seq"), axis=0, tiled=True),
            lax.all_gather(shards[10], ("items", "seq"), axis=0, tiled=True),
            lax.all_gather(shards[11], ("items", "seq"), axis=0, tiled=True),
            lax.all_gather(shards[12], ("items", "seq"), axis=0, tiled=True),
        )
        layer_out, tokens_grad, grads = micro_batch(
            gathered,
            tokens[first_item:last_item, 0],
            visible[first_item:last_item, 0],
            lengths[first_item:last_item],
            cotangent[first_item:last_item, 0],
            seq_place,
        )
        outputs_list.append(layer_out)
        gradients_list.append(tokens_grad)
        shares = (
            lax.psum_scatter(grads[0], ("items", "seq"), scatter_dimension=0, tiled=True),
            lax.psum_scatter(grads[1], ("items", "seq"), scatter_dimension=0, tiled=True),
            lax.psum_scatter(grads[2], ("items", "seq"), scatter_dimension=0, tiled=True),
            lax.psum_scatter(grads[3], ("items", "seq"), scatter_dimension=0, tiled=True),
            lax.psum_scatter(grads[4], ("items", "seq"), scatter_dimension=0, tiled=True),
            lax.psum_scatter(grads[5], ("items", "seq"), scatter_dimension=0, tiled=True),
            lax.psum_scatter(grads[6], ("items", "seq"), scatter_dimension=0, tiled=True),
            lax.psum_scatter(grads[7], ("items", "seq"), scatter_dimension=0, tiled=True),
            lax.psum_scatter(grads[8], ("items", "seq"), scatter_dimension=0, tiled=True),
            lax.psum_scatter(grads[9], ("items", "seq"), scatter_dimension=0, tiled=True),
            lax.psum_scatter(grads[10], ("items", "seq"), scatter_dimension=0, tiled=True),
            lax.psum_scatter(grads[11], ("items", "seq"), scatter_dimension=0, tiled=True),
            lax.psum_scatter(grads[12], ("items", "seq"), scatter_dimension=0, tiled=True),
        )
        totals = (
            shares
            if totals is None
            else tuple((earlier + later for earlier, later in zip(totals, shares)))
        )
    item_count = tokens.shape[0]
    layer_out = jnp.concatenate(outputs_list, axis=0).reshape(
        item_count, 1, block_rows, model_width
    )
    tokens_grad = jnp.concatenate(gradients_list, axis=0).reshape(
        item_count, 1, block_rows, model_width
    )
    return (
        layer_out,
        tokens_grad,
        totals[0],
        totals[1],
        totals[2],
        totals[3],
        totals[4],
        totals[5],
        totals[6],
        totals[7],
        totals[8],
        totals[9],
        totals[10],
        totals[11],
        totals[12],
    )


Z_SIZE = 4
F32 = jnp.float32
BF16 = jnp.bfloat16
MESH = pl.DeviceIdType.MESH
CHUNK = 24
W_I, W_O, W_E, W_R, W_Q, VEC = TENSORS = range(6)
GATHER_X = (3, 3, 3, 3, None, 2)
D_IA, D_IB, D_O, D_EA, D_EB, D_R, D_Q, D_V = SUMS = range(8)
REDUCE_X = (3, 3, 3, 3, 3, 3, None, 2)
SEMS = 24
R_ROWS, Q_ROWS = 32, 64
VECTORS = 8


def nn(left, right):
    return lax.dot_general(left, right, (((1,), (0,)), ((), ())), preferred_element_type=F32)


def nt(left, right):
    return lax.dot_general(left, right, (((1,), (1,)), ((), ())), preferred_element_type=F32)


def tn(left, right):
    return lax.dot_general(left, right, (((0,), (0,)), ((), ())), preferred_element_type=F32)


def lanes(start, size):
    return pl.ds(pl.multiple_of(start, 128), size)


def rows_at(start, size):
    return pl.ds(pl.multiple_of(start, 128), size)


class Place:
    def __init__(self):
        item = lax.axis_index("items")
        self.y = lax.axis_index("seq")
        self.z = item // 4
        self.x = (item // 2) % 2
        self.c = item % 2

    def device(self, z, x, c, y):
        return ((z * 2 + x) * 2 + c, y)

    def to_z(self, k):
        return self.device(lax.rem(self.z + k, Z_SIZE), self.x, self.c, self.y)

    @property
    def inner(self):
        return jnp.logical_or(self.z == 1, self.z == 2)

    @property
    def outer(self):
        return jnp.logical_or(self.z == 0, self.z == 3)

    def near(self, k):
        return None if k == 2 else self.z != (0 if k == 3 else 3)

    def at_z(self, z):
        return self.device(z, self.x, self.c, self.y)

    @property
    def to_x(self):
        return self.device(self.z, 1 - self.x, self.c, self.y)

    @property
    def to_y(self):
        return self.device(self.z, self.x, self.c, 1 - self.y)

    @property
    def to_c(self):
        return self.device(self.z, self.x, 1 - self.c, self.y)

    def column(self, flip_x, flip_c, flip_y):
        x = 1 - self.x if flip_x else self.x
        c = 1 - self.c if flip_c else self.c
        y = 1 - self.y if flip_y else self.y
        return x * 4 + c * 2 + y

    def quarter(self, flip_x, flip_y):
        x = 1 - self.x if flip_x else self.x
        y = 1 - self.y if flip_y else self.y
        return x * 2 + y


def remote(src, dst, send, recv, device):
    return pltpu.make_async_remote_copy(
        src_ref=src, dst_ref=dst, send_sem=send, recv_sem=recv, device_id=device, device_id_type=MESH
    )


def under(condition, action):
    if condition is None:
        action()
    else:
        pl.when(condition)(action)


class Gather:
    def __init__(self, here, buf, send, recv, share):
        self.here, self.buf, self.send, self.recv = here, buf, send, recv
        self.share = share
        self.open = []

    def copy(self, slot, index, device, recv=None):
        ref = self.buf.at[slot]
        recv = index if recv is None else recv
        return remote(ref, ref, self.send.at[index], self.recv.at[recv], device)

    def push(self, slot, index, device, when=None, recv=None):
        made = self.copy(slot, index, device, recv)
        under(when, made.start)
        self.open.append((made, when))

    def along(self, slot, first):
        for k in (1, 3, 2):
            self.push(slot, first + k - 1, self.here.to_z(k), self.here.near(k))

    def hand_on(self, slot, first, index):
        up = self.here.z == 2
        device = self.here.at_z(jnp.where(up, 3, 0))
        self.push(slot, index, device, self.here.inner, first + jnp.where(up, 2, 0))

    def pull(self, slot, index):
        self.copy(slot, index, self.here.to_x).wait_recv()

    def behind(self, k):
        return lax.rem(self.here.z + (Z_SIZE - k), Z_SIZE)

    def own(self):
        return (self.here.z, self.here.column(0, 0, 0))

    def begin_z(self):
        self.along(self.own(), 0)

    def begin_x(self):
        self.push(self.own(), 3, self.here.to_x)

    def begin_y(self):
        self.push(self.own(), 7, self.here.to_y)

    def pass_on(self, k):
        here = self.here
        slot = (self.behind(k), here.column(0, 0, 0))
        self.pull(slot, k - 1)
        if k == 2:
            self.hand_on(slot, 0, 19)
        self.push(slot, 3 + k, here.to_x)
        self.push(slot, 7 + k, here.to_y)

    def own_to_core(self):
        here = self.here
        self.push((slice(None), here.column(0, 0, 0)), 15, here.to_c)

    def relay(self, k):
        here = self.here
        from_x = (self.behind(k), here.column(1, 0, 0))
        from_y = (self.behind(k), here.column(0, 0, 1))
        self.pull(from_x, 3 + k)
        self.pull(from_y, 7 + k)
        if k < self.share:
            self.push(from_y, 11 + k, here.to_x)
        else:
            self.push(from_x, 11 + k, here.to_y)

    def sides_to_core(self):
        here = self.here
        self.push((slice(None), here.column(1, 0, 0)), 16, here.to_c)
        self.push((slice(None), here.column(0, 0, 1)), 17, here.to_c)

    def corner(self):
        here = self.here
        for k in range(4):
            self.pull((self.behind(k), here.column(1, 0, 1)), 11 + k)
        self.push((slice(None), here.column(1, 0, 1)), 18, here.to_c)

    def from_core(self):
        here = self.here
        for index, (fx, fy) in ((15, (0, 0)), (16, (1, 0)), (17, (0, 1)), (18, (1, 1))):
            self.pull((slice(None), here.column(fx, 1, fy)), index)

    def drain(self):
        for made, when in self.open:
            under(when, made.wait_send)
        self.open = []


class PlaneGather(Gather):
    def halves(self):
        wide = self.buf.shape[-1] // 2
        return slice(0, wide), slice(wide, 2 * wide)

    def begin_x(self):
        self.push(self.own(), 0, self.here.to_x)

    def begin_y(self):
        self.push(self.own(), 1, self.here.to_y)

    def along_z(self, column, first):
        self.along((self.here.z, column), first)

    def own_along_z(self):
        self.along_z(self.here.column(0, 0, 0), 4)

    def relay(self):
        here = self.here
        left, right = self.halves()
        from_x, from_y = here.column(1, 0, 0), here.column(0, 0, 1)
        self.pull((here.z, from_x), 0)
        self.push((here.z, from_x, slice(None), right), 3, here.to_y)
        self.pull((here.z, from_y), 1)
        self.push((here.z, from_y, slice(None), left), 2, here.to_x)
        self.along_z(from_x, 7)
        self.along_z(from_y, 10)

    def corner(self):
        here = self.here
        left, right = self.halves()
        corner = here.column(1, 0, 1)
        self.pull((here.z, corner, slice(None), left), 2)
        self.pull((here.z, corner, slice(None), right), 3)
        self.along_z(corner, 13)

    def pass_z(self, part):
        flips = ((0, 0), (1, 0), (0, 1), (1, 1))[part]
        slot = (self.behind(2), self.here.column(flips[0], 0, flips[1]))
        self.pull(slot, 5 + 3 * part)
        self.hand_on(slot, 4 + 3 * part, 20 + part)

    def to_core(self, part):
        here = self.here
        flips = ((0, 0), (1, 0), (0, 1), (1, 1))[part]
        column = here.column(flips[0], 0, flips[1])
        for k in (1, 3):
            self.pull((self.behind(k), column), 4 + 3 * part + k - 1)
        self.push((slice(None), column), 16 + part, here.to_c)

    def from_core(self):
        here = self.here
        for index, (fx, fy) in enumerate(((0, 0), (1, 0), (0, 1), (1, 1))):
            self.pull((slice(None), here.column(fx, 1, fy)), 16 + index)


QUARTERS = ((1, 1), (1, 0), (0, 1), (0, 0))


class Reduce:
    def __init__(self, here, part, core, relay, sides, ends, middle, send, recv, share):
        self.here, self.part, self.core, self.sides_in, self.ends = here, part, core, sides, ends
        self.middle = middle
        self.share = share
        self.relay_in = relay
        self.send, self.recv = send, recv
        self.open = []

    def push(self, src, dst, index, device, when=None):
        made = remote(src, dst, self.send.at[index], self.recv.at[index], device)
        under(when, made.start)
        self.open.append((made, when))

    def across(self, column, ends, middle, first, index):
        here, z = self.here, self.here.z
        for k in (1, 3):
            away = lax.rem(z + k, Z_SIZE)
            self.push(self.part.at[away, column], ends[k - 1], first + k - 1, here.to_z(k), here.near(k))
        inner = here.at_z(jnp.where(z == 0, 1, 2))
        self.push(self.part.at[3 - z, column], middle, index, inner, here.outer)
        away = lax.rem(z + 2, Z_SIZE)
        self.push(self.part.at[away, column], ends[1], first + 1, here.to_z(2), here.outer)

    def add_middle(self, column, ends, middle, first, index):
        here = self.here
        away = lax.rem(here.z + 2, Z_SIZE)

        def add():
            self.pull(middle, index)
            total = self.part[away, column].astype(F32) + middle[...].astype(F32)
            self.part[away, column] = total.astype(self.part.dtype)

        pl.when(here.inner)(add)
        self.push(self.part.at[away, column], ends[1], first + 1, here.to_z(2), here.inner)

    def take_ends(self, ends, first):
        self.pull(ends[1], first + 1)
        for k, missing in ((1, 0), (3, 3)):
            ref = ends[k - 1]

            def clear(ref=ref):
                ref[...] = jnp.zeros(ref.shape, ref.dtype)

            pl.when(self.here.z != missing)(functools.partial(self.pull, ref, first + k - 1))
            pl.when(self.here.z == missing)(clear)

    def three_ends(self):
        return [self.ends.at[k] for k in range(3)]

    def pull(self, dst, index):
        remote(dst, dst, self.send.at[index], self.recv.at[index], self.here.to_x).wait_recv()

    def add(self, column, first, last, *others):
        part = self.part

        def one(z, carry):
            total = part[z, column].astype(F32)
            for ref, index in others:
                total = total + ref[z, index].astype(F32)
            part[z, column] = total.astype(part.dtype)
            return carry

        lax.fori_loop(first, last, one, 0)

    def core_send(self, spare=None, first=0, last=4):
        here = self.here
        if spare is not None:
            pl.semaphore_wait(spare, 1)
        for index in range(first, last):
            fx, fy = QUARTERS[index]
            self.push(
                self.part.at[:, here.column(fx, 1, fy)],
                self.core.at[:, here.quarter(fx, fy)],
                index,
                here.to_c,
            )

    def core_add(self, index):
        here, share = self.here, self.share
        fx, fy = QUARTERS[index]
        quarter, column = here.quarter(fx, fy), here.column(fx, 0, fy)
        self.pull(self.core.at[:, quarter], index)
        self.add(column, 0, 4, (self.core, quarter))
        part = self.part
        if index == 0:
            self.push(part.at[:share, column], self.relay_in.at[:share], 4, here.to_x)
            self.push(part.at[share:, column], self.relay_in.at[share:], 5, here.to_y)
        if index == 1:
            self.push(part.at[:share, column], self.sides_in.at[:share, 0], 6, here.to_x)
        if index == 2:
            self.push(part.at[share:, column], self.sides_in.at[share:, 1], 8, here.to_y)

    def relay(self):
        here, part, share = self.here, self.part, self.share
        to_x, to_y = here.column(1, 0, 0), here.column(0, 0, 1)

        def pair(z, column):
            total = part[z, column].astype(F32) + self.relay_in[z].astype(F32)
            part[z, column] = total.astype(part.dtype)

        self.pull(self.relay_in.at[share:], 5)
        for z in range(share, 4):
            pair(z, to_x)
        self.push(part.at[share:, to_x], self.sides_in.at[share:, 0], 7, here.to_x)
        self.pull(self.relay_in.at[:share], 4)

        def one(z, carry):
            pair(z, to_y)
            return carry

        lax.fori_loop(0, share, one, 0)
        self.push(part.at[:share, to_y], self.sides_in.at[:share, 1], 9, here.to_y)

    def sides(self):
        here, share = self.here, self.share
        for index, where in ((6, (slice(0, share), 0)), (8, (slice(share, 4), 1)),
                             (7, (slice(share, 4), 0)), (9, (slice(0, share), 1))):
            self.pull(self.sides_in.at[where], index)
        own = here.column(0, 0, 0)
        self.add(own, 0, 4, (self.sides_in, 0), (self.sides_in, 1))
        self.across(own, self.three_ends(), self.middle, 10, 13)

    def pass_z(self):
        self.add_middle(self.here.column(0, 0, 0), self.three_ends(), self.middle, 10, 13)

    def finish(self):
        here = self.here
        self.take_ends(self.three_ends(), 10)
        total = self.part[here.z, here.column(0, 0, 0)].astype(F32)
        for k in range(3):
            total = total + self.ends[k].astype(F32)
        return total

    def drain(self):
        for made, when in self.open:
            under(when, made.wait_send)
        self.open = []


class PlaneReduce(Reduce):
    def core_add(self, index):
        here = self.here
        fx, fy = QUARTERS[index]
        quarter, column = here.quarter(fx, fy), here.column(fx, 0, fy)
        self.pull(self.core.at[:, quarter], index)
        self.add(column, 0, 4, (self.core, quarter))
        self.across(column, self.column_ends(index), self.middle.at[index], 4 + 3 * index, 20 + index)

    def column_ends(self, index):
        return [self.ends.at[k, index] for k in range(3)]

    def pass_z(self, index):
        fx, fy = QUARTERS[index]
        column = self.here.column(fx, 0, fy)
        self.add_middle(column, self.column_ends(index), self.middle.at[index], 4 + 3 * index, 20 + index)

    def relay(self):
        here, part, z = self.here, self.part, self.here.z
        wide = part.shape[-1] // 2
        for index, (fx, fy) in enumerate(QUARTERS):
            column = here.column(fx, 0, fy)
            self.take_ends(self.column_ends(index), 4 + 3 * index)
            total = part[z, column].astype(F32)
            for k in range(3):
                total = total + self.ends[k, index].astype(F32)
            part[z, column] = total.astype(part.dtype)
            if index == 0:
                src, dst = part.at[z, column], self.relay_in
                self.push(src.at[:, :wide], dst.at[:, :wide], 16, here.to_x)
                self.push(src.at[:, wide:], dst.at[:, wide:], 17, here.to_y)

    def sides(self):
        here, part, z = self.here, self.part, self.here.z
        wide = part.shape[-1] // 2
        for index, cols, fx, fy, to in (
            (17, slice(wide, 2 * wide), 1, 0, here.to_x), (16, slice(0, wide), 0, 1, here.to_y)
        ):
            column = here.column(fx, 0, fy)
            self.pull(self.relay_in.at[:, cols], index)
            total = part[z, column, :, cols].astype(F32) + self.relay_in[:, cols].astype(F32)
            part[z, column, :, cols] = total.astype(part.dtype)
            self.push(part.at[z, column], self.sides_in.at[fy], 18 + fy, to)

    def finish(self):
        here = self.here
        total = self.part[here.z, here.column(0, 0, 0)].astype(F32)
        for index in range(2):
            self.pull(self.sides_in.at[index], 18 + index)
            total = total + self.sides_in[index].astype(F32)
        return total


def normalise(rows_in):
    centre = rows_in - jnp.mean(rows_in, axis=-1, keepdims=True)
    spread = jnp.mean(centre * centre, axis=-1, keepdims=True)
    inverse = lax.rsqrt(spread + EPSILON)
    return centre * inverse, inverse


def normalise_back(grad, unit, inverse):
    return inverse * (
        grad
        - jnp.mean(grad, axis=-1, keepdims=True)
        - unit * jnp.mean(grad * unit, axis=-1, keepdims=True)
    )


def spread_matrix(slot):
    lane = lax.broadcasted_iota(jnp.int32, (128, 768), 0)
    place = lax.broadcasted_iota(jnp.int32, (128, 768), 1)
    if slot is None:
        inside = lax.rem(place, 4 * CHUNK)
        wanted = 32 * (inside // CHUNK) + lax.rem(inside, CHUNK)
    else:
        wanted = 32 * slot + lax.rem(place, CHUNK)
    return jnp.where(lane == wanted, 1.0, 0.0).astype(BF16)


def owner_mask(each, first):
    device = lax.broadcasted_iota(jnp.int32, (32, 768), 0)
    place = lax.broadcasted_iota(jnp.int32, (32, 768), 1)
    return device == first + place // each


def collect(group, matrix, each, first):
    moved = nn(group.astype(BF16), matrix)
    return jnp.sum(jnp.where(owner_mask(each, first), moved, 0.0), axis=0, keepdims=True)


def deal(row, matrix, each, first):
    placed = jnp.where(owner_mask(each, first), row, 0.0)
    high = placed.astype(BF16)
    rest = placed - high.astype(F32)
    middle = rest.astype(BF16)
    low = (rest - middle.astype(F32)).astype(BF16)
    return nt(high, matrix) + nt(middle, matrix) + nt(low, matrix)


def one_hot(value):
    slot = lax.broadcasted_iota(jnp.int32, (16, 128), 0).astype(F32)
    ones = jnp.where(slot == value, 1.0, 0.0).astype(BF16)
    return jnp.concatenate([ones, ones, ones], axis=0)


def live_rows(count, block, number):
    slot = lax.broadcasted_iota(jnp.int32, (number, 1), 0)
    return slot < (count + 1 - block) // 2


def live_bias(count):
    slot = lax.broadcasted_iota(jnp.int32, (256, 1), 0)
    block = slot // 128
    return jnp.where(slot - 128 * block < (count + 1 - block) // 2, 0.0, -1e30)


def half_mask(head):
    return lax.broadcasted_iota(jnp.int32, (1, 128), 1) // HD == head


def fused_kernel(
    lengths, tokens, cotangent, seen, shard_I, shard_O, shard_E, shard_R, table,
    v0, v1, v2, v3, v4, v5, v6, v7, v8,
    layer_out, tokens_grad, grad_I, grad_O, grad_E, grad_R, grad_V, *refs,
):
    s = Store(refs)
    here = Place()
    z, x, c, y = here.z, here.x, here.c, here.y
    own = here.column(0, 0, 0)
    mine, other = pl.ds(2 * y, 2), pl.ds(2 * (1 - y), 2)
    sums = s.SUMS

    gather = [
        (PlaneGather if name == W_Q else Gather)(here, s.G[name], s.GS[name], s.GQ[name], GATHER_X[name])
        for name in TENSORS
    ]
    reduce = []
    for number, (name, cols, landing) in enumerate(PIECES):
        kind = PlaneReduce if name == W_Q else Reduce
        part, *bufs = [s.P[name], s.R1[name], s.R2[name], s.RZ[name], s.RM[name]]
        core = s.RC[landing].at[:, :, : UNITS[name][0]]
        if cols is not None:
            part, *bufs = [ref.at[(*(slice(None),) * (len(ref.shape) - 1), cols)] for ref in (part, *bufs)]
            core = core.at[:, :, :, : cols.stop - cols.start]
        reduce.append(kind(here, part, core, *bufs, s.RS[number], s.RQ[number], REDUCE_X[number]))

    def swap(src, dst, came, index):
        made = remote(src, dst, s.SWS.at[index], s.SWR.at[index], here.to_y)
        return made, remote(came, came, s.SWS.at[index], s.SWR.at[index], here.to_y)

    tok_out, tok_in = swap(tokens.at[other], s.TOK.at[:, y], s.TOK.at[:, 1 - y], 0)
    seen_out, seen_in = swap(s.AWAY, s.SEEN.at[:, y], s.SEEN.at[:, 1 - y], 1)
    cot_out, cot_in = swap(cotangent.at[other], s.INC.at[:, y], s.INC.at[:, 1 - y], 2)
    lay_out, lay_in = swap(s.TOK.at[:, 1 - y], layer_out.at[mine], layer_out.at[other], 3)
    grad_out, grad_in = swap(s.INC.at[:, 1 - y], s.TOK.at[:, y], s.TOK.at[:, 1 - y], 4)
    tok_copy = pltpu.make_async_copy(tokens.at[mine], s.TOK.at[:, y], s.LOC.at[0])
    cot_copy = pltpu.make_async_copy(cotangent.at[mine], s.INC.at[:, y], s.LOC.at[1])
    out_copy = pltpu.make_async_copy(s.TOK.at[:, y], layer_out.at[mine], s.LOC.at[2])
    near_copies = [
        pltpu.make_async_copy(
            s.ENT.at[rows_at(256 * it + 128 * y, 128)], tokens_grad.at[2 * y + it], s.LOC.at[3 + it]
        )
        for it in range(2)
    ]
    far_copies = [
        pltpu.make_async_copy(
            s.ENT.at[rows_at(256 * it + 128 * (1 - y), 128)], tokens_grad.at[2 * (1 - y) + it], s.LOC.at[5 + it]
        )
        for it in range(2)
    ]

    def vector(number):
        return s.ROWS[pl.ds(number, 1), :]

    def start():
        barrier = pltpu.get_barrier_semaphore()
        partners = [here.to_z(1), here.to_z(2), here.to_z(3), here.to_x, here.to_y, here.to_c]
        for device in partners:
            pl.semaphore_signal(barrier, inc=1, device_id=device, device_id_type=MESH)
        tok_copy.start()
        cot_copy.start()
        for name, shard in ((W_I, shard_I), (W_O, shard_O), (W_E, shard_E)):
            whole = shard[...].astype(F32)
            half = whole.shape[1] // 2
            unit = jnp.concatenate([whole[:, :half], whole[:, half:]], axis=0)
            s.G[name][z, own] = unit.astype(BF16)
        s.G[W_R][z, own] = shard_R[0:R_ROWS, :]
        s.G[W_Q][z, own] = shard_R[R_ROWS:96, :]
        s.STAGE[...] = jnp.zeros_like(s.STAGE)
        for number, ref in enumerate((v0, v1, v2, v3, v4, v5, v6, v7)):
            s.STAGE[number : number + 1, 0:CHUNK] = ref[...].astype(F32)
        s.STAGE[8:9, 0 : 4 * CHUNK] = v8[...].astype(F32)
        s.G[VEC][z, own] = jnp.zeros((8, 128), F32)
        for row in range(2):
            joined = s.STAGE[4 * row : 4 * row + 1, :]
            for slot in range(1, 4):
                joined = joined + pltpu.roll(s.STAGE[4 * row + slot : 4 * row + slot + 1, :], 32 * slot, 1)
            s.G[VEC][z, own, row : row + 1, :] = joined
        long_row = s.STAGE[8:9, :]
        lane = lax.broadcasted_iota(jnp.int32, (1, 128), 1)
        joined = jnp.zeros((1, 128), F32)
        for slot in range(4):
            moved = pltpu.roll(long_row, 8 * slot, 1) if slot else long_row
            inside = jnp.logical_and(lane >= 32 * slot, lane < 32 * slot + CHUNK)
            joined = jnp.where(inside, moved, joined)
        s.G[VEC][z, own, 2:3, :] = joined
        for it in range(2):
            s.SEEN[it, y] = jnp.broadcast_to(seen[2 * y + it], (8, 128))
            s.AWAY[it] = jnp.broadcast_to(seen[2 * (1 - y) + it], (8, 128))
        pl.semaphore_wait(barrier, len(partners))

    def vectors():
        for number in range(VECTORS):
            group = s.G[VEC][:, :, number // 4, :].reshape(32, 128)
            s.ROWS[pl.ds(number, 1), :] = collect(group, spread_matrix(number % 4), CHUNK, 0)
        group = s.G[VEC][:, :, 2, :].reshape(32, 128)
        for part in range(4):
            cols = slice(768 * part, 768 * part + 768)
            s.EB[:, cols] = collect(group, spread_matrix(None), 4 * CHUNK, 8 * part)
        s.PB[:, 0:768] = vector(2)
        s.PB[:, 768:1536] = jnp.zeros((1, 768), F32)
        s.PB[:, 1536:2304] = vector(3)
        sums[...] = jnp.zeros_like(sums)
        s.EBG[...] = jnp.zeros_like(s.EBG)

    def first_norm():
        def one(block, carry):
            it, half = block // 2, block % 2
            rows = rows_at(128 * block, 128)
            patch = s.SEEN[it, half][0:1, :].astype(F32)
            frame = jnp.floor((patch + 0.5) * (1.0 / (GRID * GRID)))
            inside = patch - frame * (GRID * GRID)
            line = jnp.floor((inside + 0.5) * (1.0 / GRID))
            across = inside - line * GRID
            place = jnp.concatenate([tn(one_hot(v), table[...]) for v in (frame, line, across)], axis=1)
            entry = s.TOK[it, half].astype(F32) + place
            s.ENT[rows, :] = entry
            unit, _ = normalise(entry)
            normed = (unit * vector(0) + vector(1)).astype(BF16)
            s.XB[rows, :] = normed
            s.NRMT[:, lanes(128 * block, 128)] = normed.T
            return carry

        lax.fori_loop(0, 4, one, 0, unroll=4)

    def spread_rows(name, target):
        buf = s.G[name]
        half = target.shape[1] // 2

        def one(i, carry):
            zz, pair = i // 4, 2 * (i % 4)
            even = buf[zz, pair].astype(F32)
            odd = buf[zz, pair + 1].astype(F32)
            rows = pl.ds(pl.multiple_of(48 * i, 16), 48)
            target[rows, :half] = jnp.concatenate([even[:24], odd[:24]], axis=0).astype(BF16)
            target[rows, half:] = jnp.concatenate([even[24:], odd[24:]], axis=0).astype(BF16)
            return carry

        lax.fori_loop(0, 16, one, 0)

    def project():
        def one(n, carry):
            cols = lanes(1152 * n, 1152)
            s.PRJ[:, cols] = (nn(s.XB[...], s.WI[:, cols]) + s.PB[:, cols]).astype(BF16)
            return carry

        lax.fori_loop(0, 2, one, 0)

    def attend(first, last):
        def one(step, carry):
            it, pair = step // 6, step % 6
            rows = rows_at(256 * it, 256)
            cols = lanes(128 * pair, 128)
            q = s.PRJ[rows, cols]
            k = s.PRJ[rows, lanes(768 + 128 * pair, 128)]
            v = s.PRJ[rows, lanes(1536 + 128 * pair, 128)]
            bias = live_bias(lengths[2 * y + it])
            total = jnp.zeros((128, 256), F32)
            for head in range(2):
                mask = half_mask(head)
                scores = nt(jnp.where(mask, k, 0), q) * SCORE_SCALE + bias
                exponent = jnp.exp(scores - jnp.max(scores, axis=0, keepdims=True))
                attention = exponent * (1.0 / jnp.sum(exponent, axis=0, keepdims=True))
                low = attention.astype(BF16)
                s.ATN[2 * step + head] = low
                total = total + tn(jnp.where(mask, v, 0), low)
            s.ATTT[cols, rows] = total.astype(BF16)
            s.XB[rows, cols] = total.T.astype(BF16)
            return carry

        lax.fori_loop(first, last, one, 0, unroll=3)

    def second_norm():
        def one(it, carry):
            rows = rows_at(256 * it, 256)
            middle = s.ENT[rows, :] + nn(s.XB[rows, :], s.WO[...]) + vector(4)
            s.MID[rows, :] = middle
            unit, _ = normalise(middle)
            second = (unit * vector(5) + vector(6)).astype(BF16)
            s.XB[rows, :] = second
            s.SECT[:, rows] = second.T
            return carry

        lax.fori_loop(0, 2, one, 0, unroll=2)

    def expand(first, last):
        def one(step, carry):
            n, it = step // 2, step % 2
            cols = lanes(768 * n, 768)
            rows = rows_at(256 * it, 256)
            expanded = nn(s.XB[rows, :], s.WE[:, cols]) + s.EB[:, cols]
            normal = 0.5 * (1.0 + lax.erf(expanded * 0.7071067811865476))
            density = jnp.exp(-0.5 * expanded * expanded) * 0.3989422804014327
            s.ACT[rows, cols] = (expanded * normal).astype(BF16)
            s.GP[rows, cols] = (normal + expanded * density).astype(BF16)
            return carry

        lax.fori_loop(first, last, one, 0)

    def take_in():
        def one(block, carry):
            it, half = block // 2, block % 2
            live = live_rows(lengths[2 * y + it], half, 128)
            incoming = jnp.where(live, s.INC[it, half].astype(F32), 0.0)
            s.INC[it, half] = incoming.astype(BF16)
            sums[7:8, :] += jnp.sum(incoming, axis=0, keepdims=True)
            return carry

        lax.fori_loop(0, 4, one, 0)

    def reduce_weight_grad(xx):
        def one(zz, carry):
            moved = s.ACT[:, lanes(768 * zz + 384 * xx, 384)].T
            part = nn(moved, s.INC[...].reshape(512, 768))
            units = part.reshape(4, 96, 768).astype(BF16)
            s.P[W_R][zz, pl.ds(4 * xx, 4)] = units[:, :R_ROWS]
            s.P[W_Q][zz, pl.ds(4 * xx, 4)] = units[:, R_ROWS:]
            return carry

        lax.fori_loop(0, 4, one, 0, unroll=2)

    def reduce_rows(zz):
        return jnp.concatenate([s.G[W_R][zz], s.G[W_Q][zz]], axis=1).reshape(768, 768)

    def expanded_grad(first, last):
        def one(step, carry):
            zz, it = step // 2, step % 2
            rows = rows_at(256 * it, 256)
            cols = lanes(768 * zz, 768)
            incoming = s.INC[it].reshape(256, 768)
            grad = (nt(incoming, reduce_rows(zz)) * s.GP[rows, cols].astype(F32)).astype(BF16)
            s.GP[rows, cols] = grad
            s.EBG[:, cols] += jnp.sum(grad.astype(F32), axis=0, keepdims=True)
            return carry

        lax.fori_loop(first, last, one, 0, unroll=4)

    def weight_grad(name, moved, grad, first, last):
        part, wide = s.P[name], 384
        half = UNITS[name][1]

        def one(step, carry):
            n, m = step // 2, step % 2
            left = grad[:, lanes(wide * n, wide)]
            right = grad[:, lanes(half + wide * n, wide)]
            block = nn(moved[rows_at(384 * m, 384), :], jnp.concatenate([left, right], axis=1))
            for j in range(8):
                for side in range(2):
                    rows = slice(48 * j + 24 * side, 48 * j + 24 * side + 24)
                    unit = jnp.concatenate([block[rows, :wide], block[rows, wide:]], axis=0)
                    part[2 * m + j // 4, 2 * (j % 4) + side, :, lanes(wide * n, wide)] = unit.astype(BF16)
            return carry

        if first == 0:
            gather[name].drain()
        lax.fori_loop(2 * first, 2 * last, one, 0, unroll=2)

    def finish_rows():
        def one(it, carry):
            rows = rows_at(256 * it, 256)
            out = s.MID[rows, :] + vector(7)
            for zz in range(4):
                out = out + nn(s.ACT[rows, 768 * zz : 768 * zz + 768], reduce_rows(zz))
            for half in range(2):
                live = live_rows(lengths[2 * y + it], half, 128)
                s.TOK[it, half] = jnp.where(live, out[128 * half : 128 * half + 128], 0.0).astype(BF16)
            return carry

        tok_out.wait_send()
        lax.fori_loop(0, 2, one, 0)
        out_copy.start()

    def middle_back():
        def one(it, carry):
            rows = rows_at(256 * it, 256)
            grad = nt(s.GP[rows, :], s.WE[...])
            unit, inverse = normalise(s.MID[rows, :])
            sums[5:6, :] += jnp.sum(grad * unit, axis=0, keepdims=True)
            sums[6:7, :] += jnp.sum(grad, axis=0, keepdims=True)
            incoming = s.INC[it].reshape(256, 768).astype(F32)
            middle_grad = incoming + normalise_back(grad * vector(5), unit, inverse)
            s.MID[rows, :] = middle_grad
            branch = middle_grad.astype(BF16)
            s.XB[rows, :] = branch
            sums[4:5, :] += jnp.sum(branch.astype(F32), axis=0, keepdims=True)
            return carry

        lax.fori_loop(0, 2, one, 0)

    def attended_back():
        def one(it, carry):
            rows = rows_at(256 * it, 256)
            s.XB[rows, :] = nt(s.XB[rows, :], s.WO[...]).astype(BF16)
            return carry

        lax.fori_loop(0, 2, one, 0, unroll=2)

    def attend_back(first, last):
        def one(step, carry):
            it, pair = step // 6, step % 6
            rows = rows_at(256 * it, 256)
            cols = lanes(128 * pair, 128)
            k_cols, v_cols = lanes(768 + 128 * pair, 128), lanes(1536 + 128 * pair, 128)
            q = s.PRJ[rows, cols]
            k = s.PRJ[rows, k_cols]
            v = s.PRJ[rows, v_cols]
            grad = s.XB[rows, cols]
            query_grad = jnp.zeros((128, 256), F32)
            key_grad = jnp.zeros((256, 128), F32)
            value_grad = jnp.zeros((256, 128), F32)
            for head in range(2):
                mask = half_mask(head)
                mine_grad = jnp.where(mask, grad, 0)
                weight_back = nt(v, mine_grad)
                low = s.ATN[2 * step + head]
                attention = low.astype(F32)
                inner = jnp.sum(attention * weight_back, axis=0, keepdims=True)
                scores_grad = (attention * (weight_back - inner)).astype(BF16)
                query_grad = query_grad + tn(jnp.where(mask, k, 0), scores_grad)
                key_grad = key_grad + nn(scores_grad, jnp.where(mask, q, 0))
                value_grad = value_grad + nn(low, mine_grad)
            query_low = (query_grad * SCORE_SCALE).T.astype(BF16)
            value_low = value_grad.astype(BF16)
            s.PRJ[rows, cols] = query_low
            s.PRJ[rows, k_cols] = (key_grad * SCORE_SCALE).astype(BF16)
            s.PRJ[rows, v_cols] = value_low
            sums[2:3, cols] += jnp.sum(query_low.astype(F32), axis=0, keepdims=True)
            sums[3:4, cols] += jnp.sum(value_low.astype(F32), axis=0, keepdims=True)
            return carry

        lax.fori_loop(first, last, one, 0, unroll=6)

    def entry_back(half):
        rows = [rows_at(256 * it + 128 * half, 128) for it in range(2)]

        def both(ref):
            return jnp.concatenate([ref[r, :] for r in rows], axis=0)

        grad = nt(both(s.PRJ), s.WI[...])
        unit, inverse = normalise(both(s.ENT))
        sums[0:1, :] += jnp.sum(grad * unit, axis=0, keepdims=True)
        sums[1:2, :] += jnp.sum(grad, axis=0, keepdims=True)
        return rows, both(s.MID) + normalise_back(grad * vector(0), unit, inverse)

    def entry_back_far():
        _, out = entry_back(1 - y)
        cot_out.wait_send()
        for it in range(2):
            s.INC[it, 1 - y] = out[128 * it : 128 * it + 128].astype(BF16)

    def entry_back_near():
        rows, out = entry_back(y)
        for it in range(2):
            s.ENT[rows[it], :] = out[128 * it : 128 * it + 128]
        for copy in near_copies:
            copy.start()

    def deal_sums():
        group = None
        for number in range(VECTORS):
            dealt = deal(sums[number : number + 1, :], spread_matrix(number % 4), CHUNK, 0)
            group = dealt if number % 4 == 0 else group + dealt
            if number % 4 == 3:
                s.P[VEC][:, :, number // 4, :] = group.reshape(4, 8, 128)
        group = jnp.zeros((32, 128), F32)
        for part in range(4):
            row = s.EBG[:, 768 * part : 768 * part + 768]
            group = group + deal(row, spread_matrix(None), 4 * CHUNK, 8 * part)
        s.P[VEC][:, :, 2, :] = group.reshape(4, 8, 128)
        for row in range(3, 8):
            s.P[VEC][:, :, row, :] = jnp.zeros((4, 8, 128), F32)

    def give_spare(index):
        pl.semaphore_signal(s.SPARE.at[index], inc=1, device_id=here.to_c, device_id_type=MESH)

    def place_grad(number, ref):
        cols = PIECES[number][1]
        half = ref.shape[1] // 2
        if cols is None:
            cols = slice(0, half)
        total = reduce[number].finish()
        ref[:, cols] = total[:24]
        ref[:, half + cols.start : half + cols.stop] = total[24:]

    def take_grad():
        grad_in.wait_recv()
        for it in range(2):
            s.ENT[rows_at(256 * it + 128 * (1 - y), 128), :] = s.TOK[it, 1 - y].astype(F32)
        for copy in far_copies:
            copy.start()

    def free_tokens():
        lay_out.wait_send()
        out_copy.wait()
        lay_in.wait_recv()
        pl.semaphore_signal(s.SPARE.at[4], inc=1, device_id=here.to_y, device_id_type=MESH)

    def send_grad():
        pl.semaphore_wait(s.SPARE.at[4], 1)
        grad_out.start()

    def end():
        for made in (seen_out, grad_out):
            made.wait_send()
        for copy in near_copies + far_copies:
            copy.wait()
        for one in (*gather, *reduce):
            one.drain()

    start()
    gather[W_I].begin_x()
    gather[W_O].begin_x()
    gather[W_E].begin_y()
    gather[W_Q].begin_x()
    gather[W_E].begin_x()
    gather[W_I].begin_y()
    gather[W_I].begin_z()
    gather[W_Q].begin_y()
    gather[W_I].relay(0)
    gather[W_O].begin_y()
    tok_out.start()
    gather[W_I].pass_on(2)
    gather[VEC].begin_z()
    gather[W_I].pass_on(1)
    gather[W_O].begin_z()
    gather[VEC].begin_y()
    gather[W_I].pass_on(3)
    gather[W_I].own_to_core()
    gather[W_E].begin_z()
    gather[VEC].begin_x()
    gather[VEC].pass_on(2)
    seen_out.start()
    gather[W_E].relay(0)
    gather[VEC].pass_on(3)
    gather[W_O].pass_on(1)
    gather[VEC].pass_on(1)
    gather[W_O].pass_on(2)
    gather[W_Q].relay()
    tok_copy.wait()
    tok_in.wait_recv()
    gather[W_I].relay(2)
    gather[VEC].relay(0)
    gather[W_O].pass_on(3)
    gather[VEC].relay(3)
    gather[W_I].relay(3)
    gather[W_I].relay(1)
    gather[VEC].relay(1)
    gather[VEC].own_to_core()
    gather[VEC].relay(2)
    gather[W_I].sides_to_core()
    gather[W_O].relay(0)
    gather[W_E].pass_on(2)
    gather[W_R].begin_z()
    gather[W_E].pass_on(1)
    gather[VEC].sides_to_core()
    gather[W_E].pass_on(3)
    gather[W_O].relay(1)
    gather[W_O].relay(3)
    gather[W_Q].pass_z(1)
    gather[VEC].corner()
    gather[VEC].from_core()
    seen_in.wait_recv()
    gather[W_R].begin_y()
    vectors()
    gather[W_O].relay(2)
    gather[W_I].corner()
    gather[W_O].sides_to_core()
    gather[W_Q].corner()
    gather[W_I].from_core()
    gather[W_Q].pass_z(2)
    gather[W_E].relay(1)
    spread_rows(W_I, s.WI)
    gather[W_O].own_to_core()
    first_norm()
    gather[W_E].own_to_core()
    gather[W_E].relay(2)
    gather[W_R].begin_x()
    gather[W_Q].to_core(1)
    gather[W_R].pass_on(2)
    project()
    gather[W_O].corner()
    gather[W_E].relay(3)
    attend(0, 6)
    cot_out.start()
    gather[W_Q].pass_z(3)
    gather[W_E].sides_to_core()
    gather[W_O].from_core()
    gather[W_Q].own_along_z()
    attend(6, 12)
    gather[W_E].corner()
    gather[W_R].pass_on(3)
    spread_rows(W_O, s.WO)
    second_norm()
    gather[W_Q].to_core(2)
    gather[W_R].relay(0)
    gather[W_Q].to_core(3)
    gather[W_R].pass_on(1)
    gather[W_R].own_to_core()
    gather[W_R].relay(2)
    gather[W_E].from_core()
    spread_rows(W_E, s.WE)
    expand(0, 4)
    gather[W_Q].pass_z(0)
    expand(4, 8)
    gather[W_R].relay(1)
    gather[W_R].relay(3)
    cot_copy.wait()
    cot_in.wait_recv()
    gather[W_Q].to_core(0)
    gather[W_R].sides_to_core()
    take_in()
    reduce_weight_grad(1 - x)
    reduce[D_R].core_send(None, 0, 2)
    gather[W_R].corner()
    reduce_weight_grad(x)
    reduce[D_R].core_add(0)
    reduce[D_R].core_send(None, 2, 4)
    reduce[D_Q].core_send(None, 2, 4)
    gather[W_Q].from_core()
    reduce[D_R].core_add(1)
    reduce[D_Q].core_send(None, 0, 2)
    gather[W_R].from_core()
    expanded_grad(0, 4)
    reduce[D_R].core_add(2)
    expanded_grad(4, 8)
    weight_grad(W_E, s.SECT, s.GP, 0, 2)
    reduce[D_Q].core_add(0)
    reduce[D_R].core_add(3)
    give_spare(0)
    reduce[D_R].relay()
    reduce[D_EA].core_send(s.SPARE.at[0])
    weight_grad(W_E, s.SECT, s.GP, 2, 4)
    reduce[D_EA].core_add(0)
    finish_rows()
    lay_out.start()
    reduce[D_Q].core_add(1)
    reduce[D_EA].core_add(1)
    reduce[D_Q].core_add(2)
    reduce[D_Q].pass_z(0)
    reduce[D_Q].core_add(3)
    give_spare(1)
    reduce[D_EB].core_send(s.SPARE.at[1])
    middle_back()
    reduce[D_EB].core_add(0)
    reduce[D_EB].core_add(1)
    weight_grad(W_O, s.ATTT, s.XB, 0, 1)
    reduce[D_EA].core_add(2)
    attended_back()
    reduce[D_EA].relay()
    reduce[D_O].core_send()
    attend_back(0, 6)
    attend_back(6, 12)
    reduce[D_EB].core_add(2)
    reduce[D_EB].relay()
    weight_grad(W_I, s.NRMT, s.PRJ, 0, 2)
    reduce[D_O].core_add(0)
    weight_grad(W_I, s.NRMT, s.PRJ, 2, 3)
    reduce[D_EA].core_add(3)
    give_spare(2)
    reduce[D_IA].core_send(s.SPARE.at[2])
    reduce[D_Q].pass_z(2)
    reduce[D_O].core_add(1)
    reduce[D_Q].pass_z(1)
    reduce[D_EA].sides()
    free_tokens()
    reduce[D_IA].core_add(0)
    reduce[D_EB].core_add(3)
    give_spare(3)
    reduce[D_R].sides()
    entry_back_far()
    reduce[D_O].core_add(2)
    reduce[D_IA].core_add(1)
    reduce[D_Q].pass_z(3)
    reduce[D_IB].core_send(s.SPARE.at[3])
    reduce[D_IA].core_add(2)
    reduce[D_O].relay()
    entry_back_near()
    reduce[D_IB].core_add(0)
    reduce[D_R].pass_z()
    reduce[D_EB].sides()
    reduce[D_IA].relay()
    deal_sums()
    reduce[D_V].core_send()
    reduce[D_V].core_add(0)
    reduce[D_EB].pass_z()
    reduce[D_V].core_add(1)
    reduce[D_O].core_add(3)
    reduce[D_IB].core_add(1)
    reduce[D_IB].core_add(2)
    reduce[D_IA].core_add(3)
    reduce[D_IB].core_add(3)
    reduce[D_EA].pass_z()
    reduce[D_V].core_add(2)
    reduce[D_Q].relay()
    reduce[D_O].sides()
    reduce[D_IB].relay()
    reduce[D_V].core_add(3)
    reduce[D_IA].sides()
    reduce[D_V].relay()
    send_grad()
    grad_R[0:R_ROWS, :] = reduce[D_R].finish()
    reduce[D_IA].pass_z()
    reduce[D_O].pass_z()
    reduce[D_IB].sides()
    reduce[D_V].sides()
    place_grad(D_IA, grad_I)
    place_grad(D_EA, grad_E)
    reduce[D_V].pass_z()
    reduce[D_Q].sides()
    place_grad(D_O, grad_O)
    reduce[D_IB].pass_z()
    grad_V[...] = reduce[D_V].finish()
    place_grad(D_IB, grad_I)
    take_grad()
    place_grad(D_EB, grad_E)
    grad_R[R_ROWS:96, :] = reduce[D_Q].finish()
    end()


UNITS = ((48, 1152), (48, 384), (48, 1536), (R_ROWS, 768), (Q_ROWS, 768), (8, 128))


PIECES = (
    (W_I, slice(0, 768), 1),
    (W_I, slice(768, 1152), 2),
    (W_O, None, 0),
    (W_E, slice(0, 768), 1),
    (W_E, slice(768, 1536), 2),
    (W_R, None, 1),
    (W_Q, None, 2),
    (VEC, None, 3),
)


def scratch_list():
    dma, vmem = pltpu.SemaphoreType.DMA, pltpu.VMEM
    shapes = dict(
        SWS=dma((5,)),
        SWR=dma((5,)),
        LOC=dma((7,)),
        SPARE=pltpu.SemaphoreType.REGULAR((5,)),
        TOK=vmem((2, 2, 128, 768), BF16),
        INC=vmem((2, 2, 128, 768), BF16),
        SEEN=vmem((2, 2, 8, 128), jnp.int32),
        AWAY=vmem((2, 8, 128), jnp.int32),
        ROWS=vmem((8, 768), F32),
        STAGE=vmem((16, 128), F32),
        EB=vmem((1, 3072), F32),
        PB=vmem((1, 2304), F32),
        SUMS=vmem((8, 768), F32),
        EBG=vmem((1, 3072), F32),
        WI=vmem((768, 2304), BF16),
        WO=vmem((768, 768), BF16),
        WE=vmem((768, 3072), BF16),
        ENT=vmem((512, 768), F32),
        MID=vmem((512, 768), F32),
        XB=vmem((512, 768), BF16),
        NRMT=vmem((768, 512), BF16),
        ATTT=vmem((768, 512), BF16),
        SECT=vmem((768, 512), BF16),
        PRJ=vmem((512, 2304), BF16),
        ATN=vmem((24, 256, 256), BF16),
        ACT=vmem((512, 3072), BF16),
        GP=vmem((512, 3072), BF16),
    )
    many = dict(G=[], GS=[], GQ=[], P=[], RC=[], R1=[], R2=[], RZ=[], RM=[], RS=[], RQ=[])
    for name in TENSORS:
        kind = F32 if name == VEC else BF16
        unit = UNITS[name]
        plane = name == W_Q
        many["G"].append(vmem((4, 8, *unit), kind))
        many["GS"].append(dma((SEMS,)))
        many["GQ"].append(dma((SEMS,)))
        if name in (W_R, W_Q, VEC):
            many["P"].append(vmem((4, 8, *unit), kind))
        if name not in (W_I, W_E):
            room = (max(unit[0], 48), unit[1]) if name == W_R else unit
            many["RC"].append(vmem((4, 4, *room), kind))
        many["R1"].append(vmem(unit if plane else (4, *unit), kind))
        many["R2"].append(vmem((2, *unit) if plane else (4, 2, *unit), kind))
        many["RZ"].append(vmem((3, 4, *unit) if plane else (3, *unit), kind))
        many["RM"].append(vmem((4, *unit) if plane else unit, kind))
    for _ in SUMS:
        many["RS"].append(dma((SEMS,)))
        many["RQ"].append(dma((SEMS,)))
    return shapes, many


class Store:
    def __init__(self, refs):
        shapes, many = scratch_list()
        refs = list(refs)
        for name in shapes:
            setattr(self, name, refs.pop(0))
        for name, listed in many.items():
            setattr(self, name, [refs.pop(0) for _ in listed])
        self.P = self.G[:3] + self.P


def position_table():
    step = np.arange(16, dtype=np.float64)[:, None]
    channel = np.arange(256)
    angle = step * np.power(10000.0, -(channel // 2) / 128.0)
    whole = np.where(channel % 2 == 0, np.sin(angle), np.cos(angle)).astype(np.float32)
    high = whole.astype(jnp.bfloat16)
    rest = whole - high.astype(np.float32)
    middle = rest.astype(jnp.bfloat16)
    low = (rest - middle.astype(np.float32)).astype(jnp.bfloat16)
    return np.concatenate([high, middle, low], axis=0)


def hand_over(*refs):
    given, vectors_in, results, rows = refs[:6], refs[6], refs[7:13], refs[13:22]
    holds, sems = refs[22:28], refs[28]
    steps = []
    for which in (1, 0, 4, 5, 2, 3):
        src, hold, dst = given[which], holds[which], results[which]
        if len(src.shape) == 3:
            places = [(part, slice(first, first + 64)) for part in range(4) for first in (0, 64)]
        else:
            places = [slice(None)]
        for where in places:
            number = len(steps)
            steps.append((
                pltpu.make_async_copy(src.at[where], hold.at[where], sems.at[0, number]),
                pltpu.make_async_copy(hold.at[where], dst.at[where], sems.at[1, number]),
            ))
    for first, _ in steps:
        first.start()
    for number in range(VECTORS):
        slot = number % 4
        rows[number][...] = vectors_in[number // 4 : number // 4 + 1, 32 * slot : 32 * slot + CHUNK]
    row = vectors_in[2:3, :]
    lane = lax.broadcasted_iota(jnp.int32, (1, 128), 1)
    joined = row
    for slot in range(1, 4):
        joined = jnp.where(lane >= CHUNK * slot, pltpu.roll(row, 128 - 8 * slot, 1), joined)
    rows[8][...] = joined[:, : 4 * CHUNK]
    for first, second in steps:
        first.wait()
        second.start()
    for _, second in steps:
        second.wait()


def fused_body(
    tokens, visible, lengths, first_gain, first_shift, input_weight, query_bias, value_bias,
    output_weight, output_bias, second_gain, second_shift, expand_weight, expand_bias,
    reduce_weight, reduce_bias, cotangent,
):
    hbm = pl.BlockSpec(memory_space=pl.ANY)
    vmem = pl.BlockSpec(memory_space=pltpu.VMEM)
    smem = pl.BlockSpec(memory_space=pltpu.SMEM)
    shapes, many = scratch_list()
    results = [
        jax.ShapeDtypeStruct((4, 128, 768), BF16),
        jax.ShapeDtypeStruct((4, 128, 768), F32),
        jax.ShapeDtypeStruct(input_weight.shape, F32),
        jax.ShapeDtypeStruct(output_weight.shape, F32),
        jax.ShapeDtypeStruct(expand_weight.shape, F32),
        jax.ShapeDtypeStruct(reduce_weight.shape, F32),
        jax.ShapeDtypeStruct((8, 128), F32),
    ]
    layer_out, tokens_grad, grad_I, grad_O, grad_E, grad_R, grad_V = pl.pallas_call(
        fused_kernel,
        name="layer",
        out_shape=results,
        in_specs=[smem, hbm, hbm] + [vmem] * 15,
        out_specs=[hbm, hbm, vmem, vmem, vmem, vmem, vmem],
        scratch_shapes=[*shapes.values(), *(shape for listed in many.values() for shape in listed)],
        compiler_params=pltpu.CompilerParams(
            collective_id=0, has_side_effects=True, vmem_limit_bytes=VMEM_BYTES
        ),
    )(
        lengths, tokens[:, 0], cotangent[:, 0], visible, input_weight, output_weight, expand_weight,
        reduce_weight, jnp.asarray(position_table()),
        *(
            vector.reshape(1, -1)
            for vector in (
                first_gain, first_shift, query_bias, value_bias, output_bias, second_gain, second_shift,
                reduce_bias, expand_bias,
            )
        ),
    )
    parts = (layer_out, tokens_grad, grad_I, grad_O, grad_E, grad_R)
    row, long_row = jax.ShapeDtypeStruct((1, CHUNK), F32), jax.ShapeDtypeStruct((1, 4 * CHUNK), F32)
    layer_out, tokens_grad, grad_I, grad_O, grad_E, grad_R, *rows = pl.pallas_call(
        hand_over,
        name="hand_over",
        out_shape=[jax.ShapeDtypeStruct(part.shape, part.dtype) for part in parts] + [row] * VECTORS + [long_row],
        in_specs=[hbm] * 6 + [vmem],
        out_specs=[hbm] * 6 + [vmem] * 9,
        scratch_shapes=[pltpu.VMEM(part.shape, part.dtype) for part in parts] + [pltpu.SemaphoreType.DMA((2, 20))],
    )(*parts, grad_V)
    dealt = [row.reshape(-1) for row in rows]
    return (
        layer_out[:, None], tokens_grad[:, None], dealt[0], dealt[1], grad_I, dealt[2], dealt[3], grad_O,
        dealt[4], dealt[5], dealt[6], grad_E, dealt[8], grad_R, dealt[7],
    )


VMEM_BYTES = 67000000


def solution(mesh):
    in_specs = (
        P("items", "seq", None, None),
        P("items", "seq", None),
        P("items"),
        P(("items", "seq")),
        P(("items", "seq")),
        P(("items", "seq"), None),
        P(("items", "seq")),
        P(("items", "seq")),
        P(("items", "seq"), None),
        P(("items", "seq")),
        P(("items", "seq")),
        P(("items", "seq")),
        P(("items", "seq"), None),
        P(("items", "seq")),
        P(("items", "seq"), None),
        P(("items", "seq")),
        P("items", "seq", None, None),
    )
    out_specs = (
        P("items", "seq", None, None),
        P("items", "seq", None, None),
        P(("items", "seq")),
        P(("items", "seq")),
        P(("items", "seq"), None),
        P(("items", "seq")),
        P(("items", "seq")),
        P(("items", "seq"), None),
        P(("items", "seq")),
        P(("items", "seq")),
        P(("items", "seq")),
        P(("items", "seq"), None),
        P(("items", "seq")),
        P(("items", "seq"), None),
        P(("items", "seq")),
    )
    sizes = (mesh.shape["items"], mesh.shape["seq"])
    chosen = fused_body if sizes == (Z_SIZE * 4, 2) else general_body
    return jax.shard_map(chosen, mesh=mesh, in_specs=in_specs, out_specs=out_specs, check_vma=False)
```
